32 devices in a mesh: dp: 4 (over y, x), mp: 8 (over z, core).
Axes of the slice: x: 2, y: 2, z: 4, core: 2. Of those that a mesh axis runs over, the one named last changes fastest.
Arguments:
- hidden_rows: bfloat16 [256, 16384], P('dp', 'mp'), may hold values from -60 to 60
- head_weight: bfloat16 [16384, 8, 4, 512], P('mp', None, 'dp'), may hold values from -0.046875 to 0.046875
- norm_gain: float32 [8, 4, 512], P('mp', 'dp'), may hold values from 0.1 to 1.9
- vocab_embed: bfloat16 [32768, 8, 4, 512], P('mp', None, 'dp'), may hold values from -6 to 6
- targets: int32 [256], replicated, may hold values from 0 to 32767
Outputs:
- weight_grad: bfloat16 [16384, 8, 4, 512], P('mp', None, 'dp')
- loss: float32 [], replicated
The draws below stay inside these ranges and needn't reach their ends.
All inputs are finite; a program needn't handle non-finite values.
Results may differ from the reference program's by a relative error of at most 0.0046.
Values may be sent and summed in bfloat16 or wider, within the bound.
No kernel may reach another device: no remote copies, remote signals or barrier semaphores. Data moves between devices by JAX's collectives and lax.ppermute only.
A program may use at most 192 MiB of HBM per device.

```python
import math
import jax
import jax.numpy as jnp
from jax import lax

D = 16384
TOKENS = 256
VOCAB = 32768
FB = 512
N_DP = 4
N_MP = 8


def shared_patterns(key):
    base = jax.random.fold_in(key, 101)
    first, second, third, fourth = jax.random.split(base, 4)
    patterns = jax.random.uniform(first, (2, D), jnp.float32, -1.732, 1.732)
    token_rows = jax.random.permutation(second, TOKENS)[:2]
    vocab_rows = jax.random.permutation(third, VOCAB)[:4]
    common = jax.random.uniform(fourth, (D,), jnp.float32, -1.732, 1.732)
    return (patterns, token_rows, vocab_rows, common)


def draw_hidden_rows(key, part):
    patterns, token_rows, vocab_rows, common = shared_patterns(key)
    key = jax.random.fold_in(key, 11)
    first, second, third = jax.random.split(key, 3)
    rising = jnp.exp(math.log(3.0) * jnp.arange(D, dtype=jnp.float32) / (D - 1))
    rough = jnp.exp(jax.random.uniform(second, (D,), jnp.float32, -0.69, 0.69))
    scales = jnp.exp(jax.random.uniform(third, (TOKENS, 1), jnp.float32, -0.69, 0.69))
    position = jnp.arange(TOKENS, dtype=jnp.float32) / (TOKENS - 1)
    base = jnp.clip(jax.random.normal(first, (TOKENS, D), jnp.float32), -4.0, 4.0)
    mixing = 0.9 * position
    rows = base * rising[None, :] * rough[None, :] * scales
    rows = rows * (1.0 - mixing)[:, None] + (2.0 * mixing)[:, None] * common[None, :]
    strength = jnp.array([1.5, 1.0], jnp.float32)[:, None]
    rows = rows.at[token_rows].set(strength * patterns)
    return rows.astype(jnp.bfloat16)


def draw_vocab_embed(key, part):
    patterns, token_rows, vocab_rows, common = shared_patterns(key)
    key = jax.random.fold_in(key, 23)
    first, second, third = jax.random.split(key, 3)
    scales = jnp.exp(jax.random.uniform(second, (VOCAB, 1), jnp.float32, 0.0, math.log(10.0))) * (0.2 / math.sqrt(D))
    base = jnp.clip(jax.random.normal(first, (VOCAB, D), jnp.float32), -4.0, 4.0) * scales
    coefficient = jnp.clip(jax.random.normal(third, (VOCAB, 1), jnp.float32), -3.0, 3.0)
    base = base + coefficient * (1.5 / D) * common[None, :]
    strength = jnp.array([150.0, 152.0, 340.0, 344.0], jnp.float32)[:, None] / D
    chosen = jnp.stack([patterns[0], patterns[0], patterns[1], patterns[1]], axis=0)
    base = base.at[vocab_rows].set(strength * chosen)
    return base.reshape(VOCAB, N_MP, N_DP, D // (N_MP * N_DP)).astype(jnp.bfloat16)


def with_ends(values, own_key, least, high):
    longest = values.shape.index(max(values.shape))
    spots = []
    for shift in (0, 1):
        where = [jax.random.randint(jax.random.fold_in(own_key, axis), (), 0, length) for axis, length in enumerate(values.shape)]
        where[longest] = (where[longest] + shift) % values.shape[longest]
        spots.append(tuple(where))
    return values.at[spots[0]].set(least).at[spots[1]].set(high)


def shard_levels(key, shape, shards, low, high):
    loudness = 1.0
    for dim, blocks in shards:
        heights = jax.random.uniform(jax.random.fold_in(jax.random.fold_in(key, 6), dim), (blocks,), jnp.float32, low / len(shards), high / len(shards))
        loudness = loudness * jnp.repeat(jnp.exp(heights), shape[dim] // blocks).reshape((-1,) + (1,) * (len(shape) - 1 - dim))
    return loudness


def centred(own_key, extent, deviation, reach, cuts=(), kind=jnp.bfloat16):
    loudness = shard_levels(own_key, extent, cuts, -0.22, 0.18) if cuts else 1.0
    values = jax.random.normal(own_key, extent, jnp.float32) * deviation * loudness
    return jnp.minimum(jnp.maximum(values, -reach), reach).astype(kind)


def setup_inputs(seed: int = 0) -> dict:
    key_list = jax.random.split(jax.random.key(seed), 6)
    hidden_rows = draw_hidden_rows(jax.random.fold_in(key_list[5], 71), 0)
    head_weight = centred(key_list[1], (D, N_MP, N_DP, FB), D ** -0.5, 0.046875, ((0, 8), (2, 4)))
    norm_gain = jnp.clip(1.0 + 0.18 * jax.random.normal(key_list[2], (N_MP, N_DP, FB), jnp.float32), 0.1, 1.9)
    vocab_embed = draw_vocab_embed(jax.random.fold_in(key_list[5], 71), 0)
    targets = with_ends(jax.random.randint(key_list[4], (TOKENS,), 0, VOCAB), jax.random.fold_in(key_list[4], 1), 0, VOCAB - 1).astype(jnp.int32)
    return {"hidden_rows": hidden_rows, "head_weight": head_weight, "norm_gain": norm_gain, "vocab_embed": vocab_embed, "targets": targets}


def reference(hidden_rows, head_weight, norm_gain, vocab_embed, targets):
    width = hidden_rows.shape[1]
    weight = head_weight.reshape(width, width)
    gain = norm_gain.reshape(width)
    embed = vocab_embed.reshape(vocab_embed.shape[0], width)
    count = hidden_rows.shape[0]
    pre = jnp.dot(hidden_rows, weight, preferred_element_type=jnp.float32)
    act = hidden_rows.astype(jnp.float32) + jax.nn.silu(pre)
    inv = lax.rsqrt(lax.optimization_barrier(jnp.mean(act * act, axis=1)) + 1e-05)
    normed = (act * inv[:, None] * gain[None, :]).astype(jnp.bfloat16)
    logits = jnp.dot(normed, embed.T, preferred_element_type=jnp.float32)
    top = lax.optimization_barrier(jnp.max(logits, axis=1))
    lse = top + jnp.log(lax.optimization_barrier(jnp.sum(jnp.exp(logits - top[:, None]), axis=1)))
    hit = lax.broadcasted_iota(jnp.int32, logits.shape, 1) == targets[:, None]
    picked = lax.optimization_barrier(jnp.sum(jnp.where(hit, logits, 0.0), axis=1))
    loss = jnp.sum(lse - picked) / count
    dlogits = ((jnp.exp(logits - lse[:, None]) - hit.astype(jnp.float32)) / count).astype(jnp.bfloat16)
    dnormed = jnp.dot(dlogits, embed, preferred_element_type=jnp.float32)
    scaled = gain[None, :] * dnormed
    inner = lax.optimization_barrier(jnp.mean(act * scaled, axis=1))
    dact = inv[:, None] * scaled - act * (inv * inv * inv * inner)[:, None]
    sig = jax.nn.sigmoid(pre)
    dpre = (dact * sig * (1.0 + pre * (1.0 - sig))).astype(jnp.bfloat16)
    grad = jnp.dot(hidden_rows.T, dpre, preferred_element_type=jnp.float32).astype(jnp.bfloat16)
    return (grad.reshape(head_weight.shape), loss)
```

```python
import functools

import jax
import jax.numpy as jnp
from jax import lax
from jax.experimental import pallas as pl
from jax.experimental.pallas import tpu as pltpu
from jax.sharding import PartitionSpec as P

F32 = jnp.float32
BF16 = jnp.bfloat16
LANES = 128


def params(mib):
    return pltpu.CompilerParams(vmem_limit_bytes=mib * 2**20)


def bits_of(n):
    bits = [1 << i for i in range(n.bit_length() - 1)]
    assert 1 << len(bits) == n
    return bits


def swap(value, axis, bit):
    n = lax.axis_size(axis)
    return lax.ppermute(value, axis, [(i, i ^ bit) for i in range(n)])


def gather_xor(value, axis, bits):
    held = {0: value}
    for bit in bits:
        for s in list(held):
            held[s | bit] = swap(held[s], axis, bit)
    return held


def scatter_xor(terms, axis, bits, dtype):
    done = 0
    for bit in bits:
        for s in sorted(terms, reverse=True):
            if s & bit and not s & done:
                total = functools.reduce(jnp.add, terms[s])
                terms[s ^ bit].append(swap(total.astype(dtype), axis, bit))
        done |= bit
    return terms[0]


def whole(shape):
    return pl.BlockSpec(shape, lambda *_: (0,) * len(shape))


def project_kernel(ks, lhs, w, out):
    out[0] = jnp.dot(lhs[...], w[0], preferred_element_type=F32).astype(out.dtype)


def project(lhs, w, ks, dtype):
    _, depth, block = w.shape
    rows = lhs.shape[0]
    count = ks.shape[0]
    return pl.pallas_call(
        project_kernel,
        out_shape=jax.ShapeDtypeStruct((count, rows, block), dtype),
        grid_spec=pltpu.PrefetchScalarGridSpec(
            num_scalar_prefetch=1,
            grid=(count,),
            in_specs=[whole(lhs.shape), pl.BlockSpec((1, depth, block), lambda i, ks: (ks[i], 0, 0))],
            out_specs=pl.BlockSpec((1, rows, block), lambda i, ks: (i, 0, 0)),
        ),
        compiler_params=params(32),
        cost_estimate=pl.CostEstimate(
            flops=2 * count * rows * depth * block, bytes_accessed=2 * count * depth * block, transcendentals=0
        ),
    )(ks, lhs, w)


def act_kernel(n, *refs):
    parts, (h, gain, pre, x, squares) = refs[:n], refs[n:]
    total = parts[0][...]
    for part in parts[1:]:
        total = total + part[...].astype(F32)
    pre[...] = total
    act = h[...].astype(F32) + total / (1.0 + jnp.exp(-total))
    x[...] = (act * gain[...]).astype(BF16)
    squares[...] = jnp.sum(act * act, axis=1, keepdims=True) + jnp.zeros(squares.shape, F32)


def activate(parts, h, gain):
    rows, block = h.shape
    return pl.pallas_call(
        functools.partial(act_kernel, len(parts)),
        out_shape=[
            jax.ShapeDtypeStruct((rows, block), F32),
            jax.ShapeDtypeStruct((rows, block), BF16),
            jax.ShapeDtypeStruct((rows, LANES), F32),
        ],
        compiler_params=params(32),
    )(*parts, h, gain)


def logits_kernel(order, n_out, me, *refs):
    xs, e, outs = refs[: len(order)], refs[len(order)], refs[len(order) + 1 :]
    total = 0.0
    for s, x in zip(order, xs):
        total = total + lax.dot_general(
            x[...], e[me[0] ^ s], (((1,), (1,)), ((), ())), preferred_element_type=F32
        )
    rows = total.shape[0] // n_out
    for i, out in enumerate(outs):
        out[...] = total[i * rows : (i + 1) * rows]


def project_vocab(xs, embed, me, n_out, start, size):
    n, _, block = embed.shape
    order = sorted(xs)
    rows = xs[0].shape[0]
    step = min(512, size)
    return pl.pallas_call(
        functools.partial(logits_kernel, order, n_out),
        out_shape=[jax.ShapeDtypeStruct((rows // n_out, size), F32)] * n_out,
        grid_spec=pltpu.PrefetchScalarGridSpec(
            num_scalar_prefetch=1,
            grid=(size // step,),
            in_specs=[whole((rows, block))] * n
            + [pl.BlockSpec((n, step, block), lambda i, me: (0, start // step + i, 0))],
            out_specs=[pl.BlockSpec((rows // n_out, step), lambda i, me: (0, i))] * n_out,
        ),
        compiler_params=params(40),
        cost_estimate=pl.CostEstimate(
            flops=2 * rows * size * n * block, bytes_accessed=2 * size * n * block, transcendentals=0
        ),
    )(me, *[xs[s] for s in order], embed)


def softmax_kernel(counts, width, *refs):
    parts, refs = refs[: sum(counts)], refs[sum(counts) :]
    squares, targets, refs = refs[0], refs[1], refs[2:]
    qs, stats = refs[:-1], refs[-1]
    inv = lax.rsqrt(squares[:, 0:1] / width + 1e-05)
    target = targets[:, 0:1]
    pieces, hits, at, first = [], [], 0, 0
    for count in counts:
        total = parts[at][...]
        for part in parts[at + 1 : at + count]:
            total = total + part[...]
        at += count
        total = total * inv
        ids = lax.broadcasted_iota(jnp.int32, total.shape, 1) + first
        first += total.shape[1]
        pieces.append(total)
        hits.append(ids == target)
    top = functools.reduce(jnp.maximum, [jnp.max(p, axis=1, keepdims=True) for p in pieces])
    mass, moment, picked = 0.0, 0.0, 0.0
    for piece, hit, q in zip(pieces, hits, qs):
        shifted = piece - top
        e = jnp.exp(shifted)
        mass = mass + jnp.sum(e, axis=1, keepdims=True)
        moment = moment + jnp.sum(e * shifted, axis=1, keepdims=True)
        picked = picked + jnp.sum(jnp.where(hit, piece, 0.0), axis=1, keepdims=True)
        q[...] = e.astype(BF16)
    lane = lax.broadcasted_iota(jnp.int32, stats.shape, 1)
    out = jnp.zeros(stats.shape, F32)
    for i, value in enumerate([top, mass, moment, picked]):
        out = jnp.where(lane == i, value, out)
    stats[...] = out


def softmax(pieces, squares, targets, width):
    counts = [len(p) for p in pieces]
    flat = [part for p in pieces for part in p]
    rows = flat[0].shape[0]
    return pl.pallas_call(
        functools.partial(softmax_kernel, counts, width),
        out_shape=[jax.ShapeDtypeStruct(p[0].shape, BF16) for p in pieces]
        + [jax.ShapeDtypeStruct((rows, LANES), F32)],
        compiler_params=params(32),
    )(*flat, squares, targets)


def tree(op, values):
    while len(values) > 1:
        half = len(values) // 2
        values = [op(a, b) for a, b in zip(values[:half], values[half:])]
    return values[0]


def merge_kernel(n, tokens, width, *refs):
    stats, (squares, targets, out) = refs[:n], refs[n:]
    tops = [st[:, 0:1] for st in stats]
    top = tree(jnp.maximum, tops)
    weights = [jnp.exp(t - top) for t in tops]
    mass = tree(jnp.add, [w * st[:, 1:2] for w, st in zip(weights, stats)])
    moment = tree(
        jnp.add, [w * (st[:, 2:3] + st[:, 1:2] * (t - top)) for w, t, st in zip(weights, tops, stats)]
    )
    picked = tree(jnp.add, [st[:, 3:4] for st in stats])
    lse = top + jnp.log(mass)
    inv = lax.rsqrt(squares[:, 0:1] / width + 1e-05)
    scale = jnp.exp(tops[0] - lse) / tokens
    at_target = (jnp.exp(picked - lse) - 1.0) / tokens
    pull = (moment / mass + (top - picked)) * (inv * inv) / (tokens * width)
    lane = lax.broadcasted_iota(jnp.int32, out.shape, 1)
    packed = jnp.zeros(out.shape, F32)
    values = [scale, at_target, targets[:, 0:1].astype(F32), inv, pull, lse - picked]
    for i, value in enumerate(values):
        packed = jnp.where(lane == i, value, packed)
    out[...] = packed


def merge(stats, squares, targets, tokens, width):
    return pl.pallas_call(
        functools.partial(merge_kernel, len(stats), tokens, width),
        out_shape=jax.ShapeDtypeStruct(stats[0].shape, F32),
        compiler_params=params(32),
    )(*stats, squares, targets)


def dnormed_kernel(n_blocks, n_pieces, ks, *refs):
    qs, refs = refs[: n_blocks * n_pieces], refs[n_blocks * n_pieces :]
    packs, (w, out, dlogits) = refs[:n_blocks], refs[n_blocks:]

    @pl.when(pl.program_id(0) == 0)
    def _():
        for b in range(n_blocks):
            scale, at_target = packs[b][:, 0:1], packs[b][:, 1:2]
            target = packs[b][:, 2:3].astype(jnp.int32)
            rows = scale.shape[0]
            first = 0
            for p in range(n_pieces):
                q = qs[b * n_pieces + p][...].astype(F32) * scale
                ids = lax.broadcasted_iota(jnp.int32, q.shape, 1) + first
                values = jnp.where(ids == target, at_target, q)
                dlogits[b * rows : (b + 1) * rows, first : first + q.shape[1]] = values.astype(BF16)
                first += q.shape[1]

    out[0] = jnp.dot(dlogits[...], w[0], preferred_element_type=F32).astype(out.dtype)


def project_back(qs, packs, w, ks, dtype):
    _, depth, block = w.shape
    n_blocks, n_pieces = len(qs), len(qs[0])
    flat = [q for row in qs for q in row]
    rows = n_blocks * packs[0].shape[0]
    count = ks.shape[0]
    return pl.pallas_call(
        functools.partial(dnormed_kernel, n_blocks, n_pieces),
        out_shape=jax.ShapeDtypeStruct((count, rows, block), dtype),
        grid_spec=pltpu.PrefetchScalarGridSpec(
            num_scalar_prefetch=1,
            grid=(count,),
            in_specs=[whole(q.shape) for q in flat]
            + [whole(p.shape) for p in packs]
            + [pl.BlockSpec((1, depth, block), lambda i, ks: (ks[i], 0, 0))],
            out_specs=pl.BlockSpec((1, rows, block), lambda i, ks: (i, 0, 0)),
            scratch_shapes=[pltpu.VMEM((rows, depth), BF16)],
        ),
        compiler_params=params(40),
        cost_estimate=pl.CostEstimate(
            flops=2 * count * rows * depth * block, bytes_accessed=2 * count * depth * block, transcendentals=0
        ),
    )(ks, *flat, *packs, w)


def dpre_kernel(n, n_blocks, *refs):
    parts, refs = refs[:n], refs[n:]
    packs, (pre, h, gain, out) = refs[:n_blocks], refs[n_blocks:]
    rows = packs[0].shape[0]
    for b in range(n_blocks):
        at = slice(b * rows, (b + 1) * rows)
        dnormed = parts[0][at, :]
        for part in parts[1:]:
            dnormed = dnormed + part[at, :].astype(F32)
        inv, pull = packs[b][:, 3:4], packs[b][:, 4:5]
        v = pre[at, :]
        sigma = 1.0 / (1.0 + jnp.exp(-v))
        act = h[at, :].astype(F32) + v * sigma
        dact = inv * gain[...] * dnormed - act * pull
        out[at, :] = (dact * sigma * (1.0 + v * (1.0 - sigma))).astype(BF16)


def grad_pre(parts, packs, pre, h, gain):
    return pl.pallas_call(
        functools.partial(dpre_kernel, len(parts), len(packs)),
        out_shape=jax.ShapeDtypeStruct(pre.shape, BF16),
        compiler_params=params(32),
    )(*parts, *packs, pre, h, gain)


def grad_kernel(order, me, h, *refs):
    n = len(order)
    ds, out, placed, mixed = refs[:n], refs[n], refs[n + 1], refs[n + 2]

    @pl.when(pl.program_id(0) == 0)
    def _():
        for s, d in zip(order, ds):
            placed[me[0] ^ s] = d[...]

    step = h.shape[1]
    for k in range(n):
        product = lax.dot_general(
            h[...], placed[k], (((0,), (0,)), ((), ())), preferred_element_type=F32
        )
        for j in range(mixed.shape[0]):
            mixed[j, pl.ds(k, step, stride=n), :] = product[:, j * LANES : (j + 1) * LANES]
    for j in range(mixed.shape[0]):
        out[:, j * LANES : (j + 1) * LANES] = mixed[j].astype(BF16)


def weight_grad(h, ds, me):
    rows, width = h.shape
    n = len(ds)
    block = ds[0].shape[1]
    order = sorted(ds)
    step = min(128, width)
    return pl.pallas_call(
        functools.partial(grad_kernel, order),
        out_shape=jax.ShapeDtypeStruct((width * n, block), BF16),
        grid_spec=pltpu.PrefetchScalarGridSpec(
            num_scalar_prefetch=1,
            grid=(width // step,),
            in_specs=[pl.BlockSpec((rows, step), lambda i, me: (0, i))] + [whole((rows, block))] * n,
            out_specs=pl.BlockSpec((step * n, block), lambda i, me: (i, 0)),
            scratch_shapes=[pltpu.VMEM((n, rows, block), BF16), pltpu.VMEM((block // LANES, step * n, LANES), F32)],
        ),
        compiler_params=params(40),
        cost_estimate=pl.CostEstimate(
            flops=2 * rows * width * n * block, bytes_accessed=2 * width * n * block, transcendentals=0
        ),
    )(me, h, *[ds[s] for s in order])


def column(values):
    return jnp.broadcast_to(values[:, None], (values.shape[0], LANES))


def on_device(hidden_rows, head_weight, norm_gain, vocab_embed, targets):
    n_dp, n_mp = lax.axis_size("dp"), lax.axis_size("mp")
    tok_dp, width_mp = hidden_rows.shape
    block = head_weight.shape[3]
    width = width_mp * n_mp
    tokens = tok_dp * n_dp
    vocab_mp = vocab_embed.shape[0]
    dp_bits, mp_bits = bits_of(n_dp), bits_of(n_mp)
    dp_index = lax.axis_index("dp")
    mp_index = lax.axis_index("mp")
    me = mp_index.astype(jnp.int32).reshape(1)
    odd = [s for s in range(n_mp - 1, -1, -1) if s & 1]
    even = [s - 1 for s in odd]
    ks_odd = mp_index.astype(jnp.int32) ^ jnp.array(odd, jnp.int32)
    ks_even = mp_index.astype(jnp.int32) ^ jnp.array(even, jnp.int32)
    orders = [dp_bits, dp_bits[::-1]]

    weight = head_weight.reshape(width_mp, n_mp, block).transpose(1, 0, 2)
    embed = vocab_embed.reshape(vocab_mp, n_mp, block).transpose(1, 0, 2)
    gain = norm_gain.reshape(1, block)

    half = width_mp // 2
    left, right = (
        gather_xor(hidden_rows[:, i * half : (i + 1) * half], "dp", orders[i]) for i in range(2)
    )
    h = jnp.concatenate(
        [jnp.concatenate([left[s], right[s]], axis=1) for s in range(n_dp)], axis=0
    )
    own_h = lax.dynamic_slice_in_dim(h, dp_index * block, block, 1)

    def reduce_blocks(sent, kept):
        arrived = swap(sent, "mp", 1)
        terms = {s: [kept[i], arrived[i]] for i, s in enumerate(even)}
        return scatter_xor(terms, "mp", mp_bits[1:], BF16)

    parts = reduce_blocks(project(h, weight, ks_odd, BF16), project(h, weight, ks_even, F32))
    pre, x, squares = activate(parts, own_h, gain)

    squares = squares[:, 0].reshape(n_dp, tok_dp)
    for bit in mp_bits:
        squares = squares + swap(squares, "mp", bit)
    for bit in dp_bits:
        arrived = swap(squares, "dp", bit)
        squares = squares + jnp.stack([arrived[s ^ bit] for s in range(n_dp)])
    squares = column(squares[0])

    xs = gather_xor(x, "mp", mp_bits[::-1])
    half = vocab_mp // 2
    pieces = []
    for i in range(2):
        partial = project_vocab(xs, embed, me, n_dp, i * half, half)
        pieces.append(scatter_xor({s: [p] for s, p in enumerate(partial)}, "dp", orders[i], F32))
    local = lax.dynamic_slice_in_dim(targets, dp_index * tok_dp, tok_dp, 0) - mp_index * vocab_mp
    local = column(local)
    *own_q, stats = softmax(pieces, squares, local, width)
    q = [gather_xor(own_q[i], "dp", orders[i]) for i in range(2)]
    all_stats = gather_xor(stats, "mp", mp_bits)
    packed = merge([all_stats[s] for s in range(n_mp)], squares, local, tokens, width)
    packs = gather_xor(packed, "dp", dp_bits)
    packs = [packs[s] for s in range(n_dp)]
    loss = tree(jnp.add, [jnp.sum(p[:, 5]) for p in packs]) / tokens

    rows = [[q[0][s], q[1][s]] for s in range(n_dp)]
    parts = reduce_blocks(
        project_back(rows, packs, embed, ks_odd, BF16), project_back(rows, packs, embed, ks_even, F32)
    )
    dpre = grad_pre(parts, packs, pre, own_h, gain)
    grad = weight_grad(h, gather_xor(dpre, "mp", mp_bits[::-1]), me)
    return (grad.reshape(head_weight.shape), loss)


def solution(mesh):
    return jax.shard_map(
        on_device,
        mesh=mesh,
        in_specs=(
            P("dp", "mp"),
            P("mp", None, "dp", None),
            P("mp", "dp", None),
            P("mp", None, "dp", None),
            P(),
        ),
        out_specs=(P("mp", None, "dp", None), P()),
        check_vma=False,
    )
```

```python
import functools

import jax
import jax.numpy as jnp
from jax import lax
from jax.experimental import pallas as pl
from jax.experimental.pallas import tpu as pltpu
from jax.sharding import PartitionSpec as P

F32 = jnp.float32
BF16 = jnp.bfloat16
LANES = 128


def params(mib):
    return pltpu.CompilerParams(vmem_limit_bytes=mib * 2**20)


def bits_of(n):
    bits = [1 << i for i in range(n.bit_length() - 1)]
    assert 1 << len(bits) == n
    return bits


def swap(value, axis, bit):
    n = lax.axis_size(axis)
    return lax.ppermute(value, axis, [(i, i ^ bit) for i in range(n)])


def gather_xor(value, axis, bits):
    held = {0: value}
    for bit in bits:
        for s in list(held):
            held[s | bit] = swap(held[s], axis, bit)
    return held


def gather_direct(value, axis):
    return [value] + [swap(value, axis, s) for s in range(1, lax.axis_size(axis))]


def scatter_xor(terms, axis, bits):
    done = 0
    for bit in bits:
        for s in sorted(terms, reverse=True):
            if s & bit and not s & done:
                total = functools.reduce(jnp.add, terms[s])
                terms[s ^ bit].append(swap(total, axis, bit))
        done |= bit
    return terms[0]


def whole(shape):
    return pl.BlockSpec(shape, lambda *_: (0,) * len(shape))


def after(deps):
    return [pl.BlockSpec(memory_space=pl.ANY)] * len(deps)


def relayout_kernel(n, n_skip, x, *refs):
    out, mixed = refs[n_skip:]
    rows = out.shape[1]
    for j in range(mixed.shape[0]):
        mixed[j] = x[:, j * LANES : (j + 1) * LANES].astype(F32)
    for k in range(n):
        for j in range(mixed.shape[0]):
            out[k, :, j * LANES : (j + 1) * LANES] = mixed[j, pl.ds(k, rows, stride=n), :].astype(BF16)


def relayout(flat, n, start, rows, into, deps):
    total, block = flat.shape[0] // n, flat.shape[1]
    step = min(128, rows)
    skipped = list(deps) if into is None else [into, *deps]
    return pl.pallas_call(
        functools.partial(relayout_kernel, n, len(skipped)),
        out_shape=jax.ShapeDtypeStruct((n, total, block), BF16),
        grid=(rows // step,),
        in_specs=[pl.BlockSpec((step * n, block), lambda i: (start // step + i, 0))] + after(skipped),
        out_specs=pl.BlockSpec((n, step, block), lambda i: (0, start // step + i, 0)),
        scratch_shapes=[pltpu.VMEM((block // LANES, step * n, LANES), F32)],
        input_output_aliases={} if into is None else {1: 0},
        compiler_params=params(40),
        cost_estimate=pl.CostEstimate(flops=0, bytes_accessed=4 * rows * n * block, transcendentals=0),
    )(flat, *skipped)


def project_kernel(n_skip, ks, lhs, w, *refs):
    odd, even, total = refs[n_skip:]
    i, c = pl.program_id(0), pl.program_id(1)
    depth = w.shape[1]
    part = jnp.dot(lhs[:, pl.ds(pl.multiple_of(c * depth, depth), depth)], w[0], preferred_element_type=F32)

    @pl.when(c == 0)
    def _():
        total[...] = part

    @pl.when(c > 0)
    def _():
        total[...] += part

    last = c == pl.num_programs(1) - 1

    @pl.when(jnp.logical_and(last, i % 2 == 0))
    def _():
        odd[0] = total[...].astype(odd.dtype)

    @pl.when(jnp.logical_and(last, i % 2 == 1))
    def _():
        even[0] = total[...]


def project(lhs, w, me, pairs, deps=()):
    _, depth, block = w.shape
    rows = lhs.shape[0]
    count = len(pairs)
    step = min(2048, depth)
    ks = me ^ jnp.array([s for pair in pairs for s in (pair + 1, pair)], jnp.int32)
    return pl.pallas_call(
        functools.partial(project_kernel, len(deps)),
        out_shape=[
            jax.ShapeDtypeStruct((count, rows, block), BF16),
            jax.ShapeDtypeStruct((count, rows, block), F32),
        ],
        grid_spec=pltpu.PrefetchScalarGridSpec(
            num_scalar_prefetch=1,
            grid=(2 * count, depth // step),
            in_specs=[whole(lhs.shape), pl.BlockSpec((1, step, block), lambda i, c, ks: (ks[i], c, 0))]
            + after(deps),
            out_specs=[pl.BlockSpec((1, rows, block), lambda i, c, ks: (i // 2, 0, 0))] * 2,
            scratch_shapes=[pltpu.VMEM((rows, block), F32)],
        ),
        compiler_params=params(40),
        cost_estimate=pl.CostEstimate(
            flops=4 * count * rows * depth * block, bytes_accessed=4 * count * depth * block, transcendentals=0
        ),
    )(ks, lhs, w, *deps)


def pick(term, rows, block):
    array, place = term
    return pl.BlockSpec((1, rows, block), lambda *_: (place, 0, 0))


def add_kernel(n, *refs):
    out = refs[-1]
    total = refs[0][0].astype(F32)
    for ref in refs[1:n]:
        total = total + ref[0].astype(F32)
    out[0] = total.astype(out.dtype)


def add_round(terms, deps=()):
    _, rows, block = terms[0][0].shape
    return pl.pallas_call(
        functools.partial(add_kernel, len(terms)),
        out_shape=jax.ShapeDtypeStruct((1, rows, block), BF16),
        grid=(1,),
        in_specs=[pick(t, rows, block) for t in terms] + after(deps),
        out_specs=whole((1, rows, block)),
        compiler_params=params(40),
    )(*[t[0] for t in terms], *deps)


def act_kernel(n, *refs):
    parts, (h, gain, pre, x, squares) = refs[:n], refs[-5:]
    total = parts[0][0]
    for part in parts[1:]:
        total = total + part[0].astype(F32)
    pre[...] = total
    act = h[...].astype(F32) + total / (1.0 + jnp.exp(-total))
    x[...] = (act * gain[...]).astype(BF16)
    sums = jnp.broadcast_to(jnp.sum(act * act, axis=1, keepdims=True), (act.shape[0], LANES))
    squares[...] = jnp.transpose(sums)[: squares.shape[0]]


def activate(parts, h, gain, deps=()):
    rows, block = h.shape
    return pl.pallas_call(
        functools.partial(act_kernel, len(parts)),
        out_shape=[
            jax.ShapeDtypeStruct((rows, block), F32),
            jax.ShapeDtypeStruct((rows, block), BF16),
            jax.ShapeDtypeStruct((8, rows), F32),
        ],
        grid=(1,),
        in_specs=[pick(t, rows, block) for t in parts] + after(deps) + [whole(h.shape), whole(gain.shape)],
        out_specs=[whole((rows, block)), whole((rows, block)), whole((8, rows))],
        compiler_params=params(40),
    )(*[t[0] for t in parts], *deps, h, gain)


def logits_kernel(n, n_out, me, *refs):
    xs, es, before, outs = refs[:n], refs[n : 2 * n], refs[2 * n : -n_out], refs[-n_out:]
    total = before[0][...] if before else 0.0
    for x, e in zip(xs, es):
        total = total + lax.dot_general(
            x[...], e[0], (((1,), (1,)), ((), ())), preferred_element_type=F32
        )
    rows = total.shape[0] // n_out
    for i, out in enumerate(outs):
        out[...] = total[i * rows : (i + 1) * rows]


def project_vocab(xs, embed, me, before, n_out, start, size):
    block = embed.shape[2]
    order = sorted(xs)
    n = len(order)
    rows = xs[order[0]].shape[0]
    step = min(512, size)
    first = start // step
    sources = [] if before is None else [before]

    def place(s):
        return pl.BlockSpec((1, step, block), lambda i, me: (me[0] ^ s, first + i, 0))

    return pl.pallas_call(
        functools.partial(logits_kernel, n, n_out),
        out_shape=[jax.ShapeDtypeStruct((rows // n_out, size), F32)] * n_out,
        grid_spec=pltpu.PrefetchScalarGridSpec(
            num_scalar_prefetch=1,
            grid=(size // step,),
            in_specs=[whole((rows, block))] * n
            + [place(s) for s in order]
            + [pl.BlockSpec((rows, step), lambda i, me: (0, first + i))] * len(sources),
            out_specs=[pl.BlockSpec((rows // n_out, step), lambda i, me: (0, i))] * n_out,
        ),
        compiler_params=params(40),
        cost_estimate=pl.CostEstimate(
            flops=2 * rows * size * n * block,
            bytes_accessed=2 * size * n * block + 8 * rows * size,
            transcendentals=0,
        ),
    )(me, *[xs[s] for s in order], *[embed] * n, *sources)


def softmax_kernel(counts, width, *refs):
    parts, refs = refs[: sum(counts)], refs[sum(counts) :]
    squares, targets, refs = refs[0], refs[1], refs[2:]
    qs, stats = refs[:-1], refs[-1]
    inv = lax.rsqrt(squares[:, 0:1] / width + 1e-05)
    target = targets[:, 0:1]
    pieces, hits, at, first = [], [], 0, 0
    for count in counts:
        total = parts[at][...]
        for part in parts[at + 1 : at + count]:
            total = total + part[...]
        at += count
        total = total * inv
        ids = lax.broadcasted_iota(jnp.int32, total.shape, 1) + first
        first += total.shape[1]
        pieces.append(total)
        hits.append(ids == target)
    top = functools.reduce(jnp.maximum, [jnp.max(p, axis=1, keepdims=True) for p in pieces])
    mass, moment, picked = 0.0, 0.0, 0.0
    for piece, hit, q in zip(pieces, hits, qs):
        shifted = piece - top
        e = jnp.exp(shifted)
        mass = mass + jnp.sum(e, axis=1, keepdims=True)
        moment = moment + jnp.sum(e * shifted, axis=1, keepdims=True)
        picked = picked + jnp.sum(jnp.where(hit, piece, 0.0), axis=1, keepdims=True)
        q[...] = e.astype(BF16)
    lane = lax.broadcasted_iota(jnp.int32, stats.shape, 1)
    out = jnp.zeros(stats.shape, F32)
    for i, value in enumerate([top, mass, moment, picked]):
        out = jnp.where(lane == i, value, out)
    stats[...] = out


def softmax(pieces, squares, targets, width):
    counts = [len(p) for p in pieces]
    flat = [part for p in pieces for part in p]
    rows = flat[0].shape[0]
    return pl.pallas_call(
        functools.partial(softmax_kernel, counts, width),
        out_shape=[jax.ShapeDtypeStruct(p[0].shape, BF16) for p in pieces]
        + [jax.ShapeDtypeStruct((rows, LANES), F32)],
        compiler_params=params(32),
    )(*flat, squares, targets)


def tree(op, values):
    while len(values) > 1:
        half = len(values) // 2
        values = [op(a, b) for a, b in zip(values[:half], values[half:])]
    return values[0]


def hold_kernel(value, *refs):
    refs[-1][...] = value[...]


def hold(value, deps):
    return pl.pallas_call(
        hold_kernel,
        out_shape=jax.ShapeDtypeStruct(value.shape, value.dtype),
        in_specs=[pl.BlockSpec(memory_space=pltpu.VMEM)] + after(deps),
        compiler_params=params(40),
    )(value, *deps)


def merge_kernel(n, tokens, width, *refs):
    stats, (squares, targets, out) = refs[:n], refs[n:]
    tops = [st[:, 0:1] for st in stats]
    top = tree(jnp.maximum, tops)
    weights = [jnp.exp(t - top) for t in tops]
    mass = tree(jnp.add, [w * st[:, 1:2] for w, st in zip(weights, stats)])
    moment = tree(
        jnp.add, [w * (st[:, 2:3] + st[:, 1:2] * (t - top)) for w, t, st in zip(weights, tops, stats)]
    )
    picked = tree(jnp.add, [st[:, 3:4] for st in stats])
    lse = top + jnp.log(mass)
    inv = lax.rsqrt(squares[:, 0:1] / width + 1e-05)
    scale = jnp.exp(tops[0] - lse) / tokens
    at_target = (jnp.exp(picked - lse) - 1.0) / tokens
    pull = (moment / mass + (top - picked)) * (inv * inv) / (tokens * width)
    lane = lax.broadcasted_iota(jnp.int32, out.shape, 1)
    packed = jnp.zeros(out.shape, F32)
    values = [scale, at_target, targets[:, 0:1].astype(F32), inv, pull, lse - picked]
    for i, value in enumerate(values):
        packed = jnp.where(lane == i, value, packed)
    out[...] = packed


def merge(stats, squares, targets, tokens, width):
    return pl.pallas_call(
        functools.partial(merge_kernel, len(stats), tokens, width),
        out_shape=jax.ShapeDtypeStruct(stats[0].shape, F32),
        compiler_params=params(40),
    )(*stats, squares, targets)


def dlogits_kernel(n_blocks, n_pieces, *refs):
    qs, (packs, dlogits) = refs[: n_blocks * n_pieces], refs[-2:]
    rows = qs[0].shape[0]
    for b in range(n_blocks):
        at = slice(b * rows, (b + 1) * rows)
        scale, at_target, target = packs[at, 0:1], packs[at, 1:2], packs[at, 2:3].astype(jnp.int32)
        first = 0
        for p in range(n_pieces):
            q = qs[b * n_pieces + p][...].astype(F32) * scale
            ids = lax.broadcasted_iota(jnp.int32, q.shape, 1) + first
            dlogits[at, first : first + q.shape[1]] = jnp.where(ids == target, at_target, q).astype(BF16)
            first += q.shape[1]


def scale_rows(qs, packs):
    flat = [q for row in qs for q in row]
    shape = (packs.shape[0], sum(q.shape[1] for q in qs[0]))
    return pl.pallas_call(
        functools.partial(dlogits_kernel, len(qs), len(qs[0])),
        out_shape=jax.ShapeDtypeStruct(shape, BF16),
        compiler_params=params(40),
    )(*flat, packs)


def dpre_kernel(n, *refs):
    parts, (packs, pre, h, gain, out) = refs[:n], refs[n:]
    dnormed = parts[0][0]
    for part in parts[1:]:
        dnormed = dnormed + part[0].astype(F32)
    inv, pull = packs[:, 3:4], packs[:, 4:5]
    v = pre[...]
    sigma = 1.0 / (1.0 + jnp.exp(-v))
    act = h[...].astype(F32) + v * sigma
    dact = inv * gain[...] * dnormed - act * pull
    out[...] = (dact * sigma * (1.0 + v * (1.0 - sigma))).astype(BF16)


def grad_pre(parts, packs, pre, h, gain):
    rows, block = pre.shape
    rest = [packs, pre, h, gain]
    return pl.pallas_call(
        functools.partial(dpre_kernel, len(parts)),
        out_shape=jax.ShapeDtypeStruct(pre.shape, BF16),
        grid=(1,),
        in_specs=[pick(t, rows, block) for t in parts] + [whole(r.shape) for r in rest],
        out_specs=whole(pre.shape),
        compiler_params=params(40),
    )(*[t[0] for t in parts], *rest)


def grad_kernel(order, me, h, *refs):
    n = len(order)
    ds, out, placed, mixed = refs[:n], refs[n], refs[n + 1], refs[n + 2]

    @pl.when(pl.program_id(0) == 0)
    def _():
        for s, d in zip(order, ds):
            placed[me[0] ^ s] = d[...]

    step = h.shape[0]
    for k in range(n):
        product = jnp.dot(h[...], placed[k], preferred_element_type=F32)
        for j in range(mixed.shape[0]):
            mixed[j, pl.ds(k, step, stride=n), :] = product[:, j * LANES : (j + 1) * LANES]
    for j in range(mixed.shape[0]):
        out[:, j * LANES : (j + 1) * LANES] = mixed[j].astype(BF16)


def weight_grad(h, ds, me):
    width, rows = h.shape
    n = len(ds)
    block = ds[0].shape[1]
    order = sorted(ds)
    step = min(256, width)
    return pl.pallas_call(
        functools.partial(grad_kernel, order),
        out_shape=jax.ShapeDtypeStruct((width * n, block), BF16),
        grid_spec=pltpu.PrefetchScalarGridSpec(
            num_scalar_prefetch=1,
            grid=(width // step,),
            in_specs=[pl.BlockSpec((step, rows), lambda i, me: (i, 0))] + [whole((rows, block))] * n,
            out_specs=pl.BlockSpec((step * n, block), lambda i, me: (i, 0)),
            scratch_shapes=[pltpu.VMEM((n, rows, block), BF16), pltpu.VMEM((block // LANES, step * n, LANES), F32)],
        ),
        compiler_params=params(40),
        cost_estimate=pl.CostEstimate(
            flops=2 * rows * width * n * block, bytes_accessed=2 * width * n * block, transcendentals=0
        ),
    )(me, h, *[ds[s] for s in order])


def column(values):
    return jnp.broadcast_to(values[:, None], (values.shape[0], LANES))


def on_device(hidden_rows, head_weight, norm_gain, vocab_embed, targets):
    n_dp, n_mp = lax.axis_size("dp"), lax.axis_size("mp")
    tok_dp, width_mp = hidden_rows.shape
    block = head_weight.shape[3]
    width = width_mp * n_mp
    tokens = tok_dp * n_dp
    vocab_mp = vocab_embed.shape[0]
    dp_bits, mp_bits = bits_of(n_dp), bits_of(n_mp)
    dp_index = lax.axis_index("dp")
    mp_index = lax.axis_index("mp")
    me = mp_index.astype(jnp.int32).reshape(1)
    pairs = list(range(n_mp - 2, -1, -2))
    orders = [dp_bits, dp_bits[::-1]]

    weight_rows = head_weight.reshape(width_mp * n_mp, block)
    embed_rows = vocab_embed.reshape(vocab_mp * n_mp, block)
    gain = norm_gain.reshape(1, block)
    quarter = vocab_mp // 4

    h = jnp.concatenate(gather_direct(hidden_rows, "dp"), axis=0)
    weight = relayout(weight_rows, n_mp, 0, width_mp, None, [])
    own_h = lax.dynamic_slice_in_dim(h, dp_index * block, block, 1)

    def reduce_blocks(products, fillers):
        terms = {}
        for group, (odd, even) in products:
            arrived = swap(odd, "mp", 1)
            for i, s in enumerate(group):
                terms[s] = [(even, i), (arrived, i)]
        done, filled = 1, []
        for bit in mp_bits[1:]:
            senders = [s for s in sorted(terms, reverse=True) if s & bit and not s & done]
            totals = [add_round(terms[s], filled) for s in senders]
            for s, total in zip(senders, totals):
                terms[s ^ bit].append((swap(total, "mp", bit), 0))
            if fillers:
                filled = [fillers.pop(0)(totals)]
            done |= bit
        return terms[0], filled

    cut = n_mp // 4
    early = project(h, weight, me, pairs[:cut])
    late = project(h, weight, me, pairs[cut:], [early[1]])
    made = []

    def fill(first, count):
        def run(deps):
            into = made[-1] if made else None
            made.append(relayout(embed_rows, n_mp, first * quarter, count * quarter, into, deps))
            return made[-1]

        return run

    parts, filled = reduce_blocks([(pairs[:cut], early), (pairs[cut:], late)], [fill(0, 1), fill(1, 2)])
    pre, x, squares = activate(parts, own_h, gain, filled)

    xs = gather_xor(x, "mp", mp_bits[::-1])
    for bit in mp_bits:
        squares = squares + swap(squares, "mp", bit)
    embed = fill(3, 1)([x])

    partial = None
    for blocks in ([0, 1], list(range(2, n_mp - 2))):
        [partial] = project_vocab({s: xs[s] for s in blocks}, embed, me, partial, 1, 0, vocab_mp)
    half = vocab_mp // 2
    pieces = []
    for i in range(2):
        last = project_vocab(
            {s: xs[s] for s in (n_mp - 2, n_mp - 1)}, embed, me, partial, n_dp, i * half, half
        )
        pieces.append(scatter_xor({s: [p] for s, p in enumerate(last)}, "dp", orders[i]))

    squares = squares[0].reshape(n_dp, tok_dp)
    for bit in dp_bits:
        arrived = swap(squares, "dp", bit)
        squares = squares + jnp.stack([arrived[s ^ bit] for s in range(n_dp)])
    squares = column(squares[0])
    local = lax.dynamic_slice_in_dim(targets, dp_index * tok_dp, tok_dp, 0) - mp_index * vocab_mp
    local = column(local)
    *own_q, stats = softmax(pieces, squares, local, width)
    q = [gather_xor(own_q[i], "dp", orders[i]) for i in range(2)]
    stats = hold(stats, [q[0][orders[0][0]]])
    packed = merge(gather_direct(stats, "mp"), squares, local, tokens, width)
    packs = jnp.concatenate(gather_direct(packed, "dp"), axis=0)
    sums = [jnp.sum(packs[s * tok_dp : (s + 1) * tok_dp, 5]) for s in range(n_dp)]
    loss = tree(jnp.add, sums) / tokens

    dlogits = scale_rows([[q[0][s], q[1][s]] for s in range(n_dp)], packs)
    products, deps = [], []
    for pair in pairs:
        product = project(dlogits, embed, me, [pair], deps)
        deps = [product[1]]
        products.append(([pair], product))
    parts, _ = reduce_blocks(products, [])
    dpre = grad_pre(parts, packs, pre, own_h, gain)
    grad = weight_grad(h.T, gather_xor(dpre, "mp", mp_bits[::-1]), me)
    return (grad.reshape(head_weight.shape), loss)


def solution(mesh):
    return jax.shard_map(
        on_device,
        mesh=mesh,
        in_specs=(
            P("dp", "mp"),
            P("mp", None, "dp", None),
            P("mp", "dp", None),
            P("mp", None, "dp", None),
            P(),
        ),
        out_specs=(P("mp", None, "dp", None), P()),
        check_vma=False,
    )
```

```python
import functools

import jax
import jax.numpy as jnp
from jax import lax
from jax.experimental import pallas as pl
from jax.experimental.pallas import tpu as pltpu
from jax.sharding import PartitionSpec as P

F32 = jnp.float32
BF16 = jnp.bfloat16
LANES = 128


def params(mib):
    return pltpu.CompilerParams(vmem_limit_bytes=mib * 2**20)


def bits_of(n):
    bits = [1 << i for i in range(n.bit_length() - 1)]
    assert 1 << len(bits) == n
    return bits


def swap(value, axis, bit):
    n = lax.axis_size(axis)
    return lax.ppermute(value, axis, [(i, i ^ bit) for i in range(n)])


def gather_xor(value, axis, bits):
    held = {0: value}
    for bit in bits:
        for s in list(held):
            held[s | bit] = swap(held[s], axis, bit)
    return held


def gather_rows(value, axis, bits):
    first, places = None, [0]
    for bit in bits:
        arrived = swap(value, axis, bit)
        first = arrived if first is None else first
        value = jnp.concatenate([value, arrived], axis=0)
        places = places + [s ^ bit for s in places]
    return (value, places), first


def gather_direct(value, axis):
    return [value] + [swap(value, axis, s) for s in range(1, lax.axis_size(axis))]


def scatter_xor(terms, axis, bits):
    done = 0
    for bit in bits:
        for s in sorted(terms, reverse=True):
            if s & bit and not s & done:
                total = functools.reduce(jnp.add, terms[s])
                terms[s ^ bit].append(swap(total, axis, bit))
        done |= bit
    return terms[0]


def whole(shape):
    return pl.BlockSpec(shape, lambda *_: (0,) * len(shape))


def after(deps):
    return [pl.BlockSpec(memory_space=pl.ANY)] * len(deps)


def each_tile(n, rows, run):
    group = max(1, 16 // n)

    def body(i, carry):
        run(i * group, group)
        return carry

    lax.fori_loop(0, rows // group, body, 0, unroll=8)


def relayout_kernel(n, n_skip, x, *refs):
    out, mixed = refs[n_skip:]
    rows = out.shape[1]
    lanes = range(0, x.shape[1], LANES)

    def spread(first, group):
        at = pl.multiple_of(first * n, 16)
        values = x[pl.ds(at, group * n), :].astype(F32)
        for g in range(group):
            for p in range(0, n, 8):
                part = values[g * n + p : g * n + p + 8]
                for j, lane in enumerate(lanes):
                    mixed[j, pl.ds((first + g) * (n + 1) + p, 8), :] = part[:, lane : lane + LANES]

    each_tile(n, rows, spread)
    for k in range(n):
        for j, lane in enumerate(lanes):
            out[k, :, lane : lane + LANES] = mixed[j, pl.ds(k, rows, stride=n + 1), :].astype(BF16)


def relayout(flat, n, start, rows, into, deps):
    total, block = flat.shape[0] // n, flat.shape[1]
    step = min(128, rows)
    skipped = list(deps) if into is None else [into, *deps]
    return pl.pallas_call(
        functools.partial(relayout_kernel, n, len(skipped)),
        out_shape=jax.ShapeDtypeStruct((n, total, block), BF16),
        grid=(rows // step,),
        in_specs=[pl.BlockSpec((step * n, block), lambda i: (start // step + i, 0))] + after(skipped),
        out_specs=pl.BlockSpec((n, step, block), lambda i: (0, start // step + i, 0)),
        scratch_shapes=[pltpu.VMEM((block // LANES, step * (n + 1), LANES), F32)],
        input_output_aliases={} if into is None else {1: 0},
        compiler_params=params(48),
        cost_estimate=pl.CostEstimate(flops=0, bytes_accessed=4 * rows * n * block, transcendentals=0),
    )(flat, *skipped)


def project_kernel(n, n_skip, ks, lhs, *refs):
    ws, (odd, even) = refs[:n], refs[n + n_skip :]
    total, first = 0.0, 0
    for w in ws:
        depth = w.shape[1]
        total = total + jnp.dot(lhs[:, first : first + depth], w[0], preferred_element_type=F32)
        first += depth
    is_odd = pl.program_id(0) % 2 == 0

    @pl.when(is_odd)
    def _():
        odd[0] = total.astype(odd.dtype)

    @pl.when(jnp.logical_not(is_odd))
    def _():
        even[0] = total


def project(lhs, ws, me, pairs, deps=()):
    block = ws[0].shape[2]
    rows, depth = lhs.shape
    count = len(pairs)
    ks = me ^ jnp.array([s for pair in pairs for s in (pair + 1, pair)], jnp.int32)
    return pl.pallas_call(
        functools.partial(project_kernel, len(ws), len(deps)),
        out_shape=[
            jax.ShapeDtypeStruct((count, rows, block), BF16),
            jax.ShapeDtypeStruct((count, rows, block), F32),
        ],
        grid_spec=pltpu.PrefetchScalarGridSpec(
            num_scalar_prefetch=1,
            grid=(2 * count,),
            in_specs=[whole(lhs.shape)]
            + [pl.BlockSpec((1, w.shape[1], block), lambda i, ks: (ks[i], 0, 0)) for w in ws]
            + after(deps),
            out_specs=[pl.BlockSpec((1, rows, block), lambda i, ks: (i // 2, 0, 0))] * 2,
        ),
        compiler_params=params(48),
        cost_estimate=pl.CostEstimate(
            flops=4 * count * rows * depth * block, bytes_accessed=4 * count * depth * block, transcendentals=0
        ),
    )(ks, lhs, *ws, *deps)


def pick(term, rows, block):
    array, place = term
    return pl.BlockSpec((1, rows, block), lambda *_: (place, 0, 0))


def add_kernel(n, *refs):
    out = refs[-1]
    total = refs[0][0].astype(F32)
    for ref in refs[1:n]:
        total = total + ref[0].astype(F32)
    out[0] = total.astype(out.dtype)


def add_round(terms, deps=()):
    _, rows, block = terms[0][0].shape
    return pl.pallas_call(
        functools.partial(add_kernel, len(terms)),
        out_shape=jax.ShapeDtypeStruct((1, rows, block), BF16),
        grid=(1,),
        in_specs=[pick(t, rows, block) for t in terms] + after(deps),
        out_specs=whole((1, rows, block)),
        compiler_params=params(48),
    )(*[t[0] for t in terms], *deps)


def act_kernel(n, *refs):
    parts, (h, gain, pre, x, squares) = refs[:n], refs[-5:]
    total = parts[0][0]
    for part in parts[1:]:
        total = total + part[0].astype(F32)
    pre[...] = total
    act = h[...].astype(F32) + total / (1.0 + jnp.exp(-total))
    x[...] = (act * gain[...]).astype(BF16)
    sums = jnp.broadcast_to(jnp.sum(act * act, axis=1, keepdims=True), (act.shape[0], LANES))
    squares[...] = jnp.transpose(sums)[: squares.shape[0]]


def activate(parts, h, gain, deps=()):
    rows, block = h.shape
    return pl.pallas_call(
        functools.partial(act_kernel, len(parts)),
        out_shape=[
            jax.ShapeDtypeStruct((rows, block), F32),
            jax.ShapeDtypeStruct((rows, block), BF16),
            jax.ShapeDtypeStruct((8, rows), F32),
        ],
        grid=(1,),
        in_specs=[pick(t, rows, block) for t in parts] + after(deps) + [whole(h.shape), whole(gain.shape)],
        out_specs=[whole((rows, block)), whole((rows, block)), whole((8, rows))],
        compiler_params=params(48),
    )(*[t[0] for t in parts], *deps, h, gain)


def logits_kernel(order, n_out, me, *refs):
    xs, e, outs = refs[: len(order)], refs[len(order)], refs[len(order) + 1 :]
    total = 0.0
    for s, x in zip(order, xs):
        total = total + lax.dot_general(
            x[...], e[me[0] ^ s], (((1,), (1,)), ((), ())), preferred_element_type=F32
        )
    rows = total.shape[0] // n_out
    for i, out in enumerate(outs):
        out[...] = total[i * rows : (i + 1) * rows]


def project_vocab(xs, embed, me, n_out, start, size):
    n, _, block = embed.shape
    order = sorted(xs)
    rows = xs[0].shape[0]
    step = min(512, size)
    return pl.pallas_call(
        functools.partial(logits_kernel, order, n_out),
        out_shape=[jax.ShapeDtypeStruct((rows // n_out, size), F32)] * n_out,
        grid_spec=pltpu.PrefetchScalarGridSpec(
            num_scalar_prefetch=1,
            grid=(size // step,),
            in_specs=[whole((rows, block))] * n
            + [pl.BlockSpec((n, step, block), lambda i, me: (0, start // step + i, 0))],
            out_specs=[pl.BlockSpec((rows // n_out, step), lambda i, me: (0, i))] * n_out,
        ),
        compiler_params=params(48),
        cost_estimate=pl.CostEstimate(
            flops=2 * rows * size * n * block, bytes_accessed=2 * size * n * block, transcendentals=0
        ),
    )(me, *[xs[s] for s in order], embed)


def softmax_kernel(counts, width, *refs):
    parts, refs = refs[: sum(counts)], refs[sum(counts) :]
    squares, targets, refs = refs[0], refs[1], refs[2:]
    qs, stats = refs[:-1], refs[-1]
    inv = lax.rsqrt(squares[:, 0:1] / width + 1e-05)
    target = targets[:, 0:1]
    pieces, hits, at, first = [], [], 0, 0
    for count in counts:
        total = parts[at][...]
        for part in parts[at + 1 : at + count]:
            total = total + part[...]
        at += count
        total = total * inv
        ids = lax.broadcasted_iota(jnp.int32, total.shape, 1) + first
        first += total.shape[1]
        pieces.append(total)
        hits.append(ids == target)
    top = functools.reduce(jnp.maximum, [jnp.max(p, axis=1, keepdims=True) for p in pieces])
    mass, moment, picked = 0.0, 0.0, 0.0
    for i, (piece, hit) in enumerate(zip(pieces, hits)):
        shifted = piece - top
        e = jnp.exp(shifted)
        mass = mass + jnp.sum(e, axis=1, keepdims=True)
        moment = moment + jnp.sum(e * shifted, axis=1, keepdims=True)
        picked = picked + jnp.sum(jnp.where(hit, piece, 0.0), axis=1, keepdims=True)
        size = piece.shape[1]
        first = i // len(qs) * size
        qs[i % len(qs)][:, first : first + size] = e.astype(BF16)
    lane = lax.broadcasted_iota(jnp.int32, stats.shape, 1)
    out = jnp.zeros(stats.shape, F32)
    for i, value in enumerate([top, mass, moment, picked]):
        out = jnp.where(lane == i, value, out)
    stats[...] = out


def softmax(pieces, squares, targets, width):
    counts = [len(p) for p in pieces]
    flat = [part for p in pieces for part in p]
    rows = flat[0].shape[0]
    return pl.pallas_call(
        functools.partial(softmax_kernel, counts, width),
        out_shape=[jax.ShapeDtypeStruct((rows, len(pieces) // 2 * flat[0].shape[1]), BF16)] * 2
        + [jax.ShapeDtypeStruct((rows, LANES), F32)],
        compiler_params=params(48),
    )(*flat, squares, targets)


def tree(op, values):
    while len(values) > 1:
        half = len(values) // 2
        values = [op(a, b) for a, b in zip(values[:half], values[half:])]
    return values[0]


def merge_kernel(n, tokens, width, *refs):
    stats, (squares, targets), out = refs[:n], refs[n : n + 2], refs[-1]
    tops = [st[:, 0:1] for st in stats]
    top = tree(jnp.maximum, tops)
    weights = [jnp.exp(t - top) for t in tops]
    mass = tree(jnp.add, [w * st[:, 1:2] for w, st in zip(weights, stats)])
    moment = tree(
        jnp.add, [w * (st[:, 2:3] + st[:, 1:2] * (t - top)) for w, t, st in zip(weights, tops, stats)]
    )
    picked = tree(jnp.add, [st[:, 3:4] for st in stats])
    lse = top + jnp.log(mass)
    inv = lax.rsqrt(squares[:, 0:1] / width + 1e-05)
    scale = jnp.exp(tops[0] - lse) / tokens
    at_target = (jnp.exp(picked - lse) - 1.0) / tokens
    pull = (moment / mass + (top - picked)) * (inv * inv) / (tokens * width)
    lane = lax.broadcasted_iota(jnp.int32, out.shape, 1)
    packed = jnp.zeros(out.shape, F32)
    values = [scale, at_target, targets[:, 0:1].astype(F32), inv, pull, lse - picked]
    for i, value in enumerate(values):
        packed = jnp.where(lane == i, value, packed)
    out[...] = packed


def merge(stats, squares, targets, tokens, width, deps):
    n = len(stats)
    return pl.pallas_call(
        functools.partial(merge_kernel, n, tokens, width),
        out_shape=jax.ShapeDtypeStruct(stats[0].shape, F32),
        in_specs=[pl.BlockSpec(memory_space=pltpu.VMEM)] * (n + 2) + after(deps),
        compiler_params=params(48),
    )(*stats, squares, targets, *deps)


def dlogits_kernel(places, quarter, *refs):
    qs, (packs, dlogits) = refs[:-2], refs[-2:]
    n = len(places[0])
    rows = packs.shape[0] // n
    for s in range(n):
        at = slice(s * rows, (s + 1) * rows)
        scale, at_target, target = packs[at, 0:1], packs[at, 1:2], packs[at, 2:3].astype(jnp.int32)
        for i, q in enumerate(qs):
            here = places[i].index(s) * rows
            for j in range(q.shape[1] // quarter):
                first = (j * len(qs) + i) * quarter
                values = q[here : here + rows, j * quarter : (j + 1) * quarter].astype(F32) * scale
                ids = lax.broadcasted_iota(jnp.int32, values.shape, 1) + first
                dlogits[at, first : first + quarter] = jnp.where(ids == target, at_target, values).astype(BF16)


def scale_rows(q, packs, quarter):
    values, places = zip(*q)
    shape = (packs.shape[0], sum(v.shape[1] for v in values))
    return pl.pallas_call(
        functools.partial(dlogits_kernel, places, quarter),
        out_shape=jax.ShapeDtypeStruct(shape, BF16),
        compiler_params=params(48),
    )(*values, packs)


def dpre_kernel(n, *refs):
    parts, (packs, pre, h, gain, out) = refs[:n], refs[n:]
    dnormed = parts[0][0]
    for part in parts[1:]:
        dnormed = dnormed + part[0].astype(F32)
    inv, pull = packs[:, 3:4], packs[:, 4:5]
    v = pre[...]
    sigma = 1.0 / (1.0 + jnp.exp(-v))
    act = h[...].astype(F32) + v * sigma
    dact = inv * gain[...] * dnormed - act * pull
    out[...] = (dact * sigma * (1.0 + v * (1.0 - sigma))).astype(BF16)


def grad_pre(parts, packs, pre, h, gain):
    rows, block = pre.shape
    rest = [packs, pre, h, gain]
    return pl.pallas_call(
        functools.partial(dpre_kernel, len(parts)),
        out_shape=jax.ShapeDtypeStruct(pre.shape, BF16),
        grid=(1,),
        in_specs=[pick(t, rows, block) for t in parts] + [whole(r.shape) for r in rest],
        out_specs=whole(pre.shape),
        compiler_params=params(48),
    )(*[t[0] for t in parts], *rest)


def grad_kernel(order, me, h, *refs):
    n = len(order)
    ds, out, placed, mixed = refs[:n], refs[n], refs[n + 1], refs[n + 2]

    @pl.when(pl.program_id(0) == 0)
    def _():
        for s, d in zip(order, ds):
            placed[me[0] ^ s] = d[...]

    step = h.shape[0]
    lanes = range(0, out.shape[1], LANES)
    for k in range(n):
        product = jnp.dot(h[...], placed[k], preferred_element_type=F32)
        for j, lane in enumerate(lanes):
            mixed[j, pl.ds(k, step, stride=n + 1), :] = product[:, lane : lane + LANES]

    def collect(first, group):
        at = pl.multiple_of(first * n, 16)
        for j, lane in enumerate(lanes):
            parts = [
                mixed[j, pl.ds((first + g) * (n + 1) + p, 8), :] for g in range(group) for p in range(0, n, 8)
            ]
            out[pl.ds(at, group * n), lane : lane + LANES] = jnp.concatenate(parts, axis=0).astype(BF16)

    each_tile(n, step, collect)


def weight_grad(h, ds, me):
    width, rows = h.shape
    n = len(ds)
    block = ds[0].shape[1]
    order = sorted(ds)
    step = min(256, width)
    return pl.pallas_call(
        functools.partial(grad_kernel, order),
        out_shape=jax.ShapeDtypeStruct((width * n, block), BF16),
        grid_spec=pltpu.PrefetchScalarGridSpec(
            num_scalar_prefetch=1,
            grid=(width // step,),
            in_specs=[pl.BlockSpec((step, rows), lambda i, me: (i, 0))] + [whole((rows, block))] * n,
            out_specs=pl.BlockSpec((step * n, block), lambda i, me: (i, 0)),
            scratch_shapes=[pltpu.VMEM((n, rows, block), BF16), pltpu.VMEM((block // LANES, step * (n + 1), LANES), F32)],
        ),
        compiler_params=params(48),
        cost_estimate=pl.CostEstimate(
            flops=2 * rows * width * n * block, bytes_accessed=2 * width * n * block, transcendentals=0
        ),
    )(me, h, *[ds[s] for s in order])


def column(values):
    return jnp.broadcast_to(values[:, None], (values.shape[0], LANES))


def on_device(hidden_rows, head_weight, norm_gain, vocab_embed, targets):
    n_dp, n_mp = lax.axis_size("dp"), lax.axis_size("mp")
    tok_dp, width_mp = hidden_rows.shape
    block = head_weight.shape[3]
    width = width_mp * n_mp
    tokens = tok_dp * n_dp
    vocab_mp = vocab_embed.shape[0]
    dp_bits, mp_bits = bits_of(n_dp), bits_of(n_mp)
    dp_index = lax.axis_index("dp")
    mp_index = lax.axis_index("mp")
    me = mp_index.astype(jnp.int32).reshape(1)
    pairs = list(range(n_mp - 2, -1, -2))
    orders = [dp_bits, dp_bits[::-1]]

    embed_rows = vocab_embed.reshape(vocab_mp * n_mp, block)
    gain = norm_gain.reshape(1, block)
    quarter = vocab_mp // 4

    h = jnp.concatenate(gather_direct(hidden_rows, "dp"), axis=0)
    weight = relayout(head_weight.reshape(width_mp * n_mp, block), n_mp, 0, width_mp, None, [])
    own_h = lax.dynamic_slice_in_dim(h, dp_index * block, block, 1)

    def reduce_blocks(products, fillers):
        terms = {}
        for group, (odd, even) in products:
            arrived = swap(odd, "mp", 1)
            for i, s in enumerate(group):
                terms[s] = [(even, i), (arrived, i)]
        done, made = 1, None
        for bit in mp_bits[1:]:
            senders = [s for s in sorted(terms, reverse=True) if s & bit and not s & done]
            totals = [add_round(terms[s], [] if made is None else [made]) for s in senders]
            for s, total in zip(senders, totals):
                terms[s ^ bit].append((swap(total, "mp", bit), 0))
            if fillers:
                made = fillers.pop(0)(made, totals)
            done |= bit
        return terms[0], made

    def fill(first, count):
        def run(into, deps):
            return relayout(embed_rows, n_mp, first * quarter, count * quarter, into, deps)

        return run

    cut = n_mp // 4
    early = project(h, [weight], me, pairs[:cut])
    late = project(h, [weight], me, pairs[cut:], [early[1]])
    parts, embed = reduce_blocks([(pairs[:cut], early), (pairs[cut:], late)], [fill(0, 1), fill(1, 2)])
    pre, x, squares = activate(parts, own_h, gain, [embed])

    xs = gather_xor(x, "mp", mp_bits[::-1])
    for bit in mp_bits:
        squares = squares + swap(squares, "mp", bit)
    embed = fill(3, 1)(embed, [x])
    pieces = []
    for i in range(4):
        partial = project_vocab(xs, embed, me, n_dp, i * quarter, quarter)
        pieces.append(scatter_xor({s: [p] for s, p in enumerate(partial)}, "dp", orders[i % 2]))

    squares = squares[0].reshape(n_dp, tok_dp)
    for bit in dp_bits:
        arrived = swap(squares, "dp", bit)
        squares = squares + jnp.stack([arrived[s ^ bit] for s in range(n_dp)])
    squares = column(squares[0])
    local = lax.dynamic_slice_in_dim(targets, dp_index * tok_dp, tok_dp, 0) - mp_index * vocab_mp
    local = column(local)
    *own_q, stats = softmax(pieces, squares, local, width)
    q, first_hops = zip(*[gather_rows(own_q[i], "dp", orders[i]) for i in range(2)])
    packed = merge(gather_direct(stats, "mp"), squares, local, tokens, width, first_hops)
    packs = jnp.concatenate(gather_direct(packed, "dp"), axis=0)
    sums = [jnp.sum(packs[s * tok_dp : (s + 1) * tok_dp, 5]) for s in range(n_dp)]
    loss = tree(jnp.add, sums) / tokens

    dlogits = scale_rows(q, packs, quarter)
    early = project(dlogits, [embed], me, pairs[:cut])
    late = project(dlogits, [embed], me, pairs[cut:], [early[1]])
    parts, _ = reduce_blocks([(pairs[:cut], early), (pairs[cut:], late)], [])
    dpre = grad_pre(parts, packs, pre, own_h, gain)
    grad = weight_grad(h.T, gather_xor(dpre, "mp", mp_bits[::-1]), me)
    return (grad.reshape(head_weight.shape), loss)


def solution(mesh):
    return jax.shard_map(
        on_device,
        mesh=mesh,
        in_specs=(
            P("dp", "mp"),
            P("mp", None, "dp", None),
            P("mp", "dp", None),
            P("mp", None, "dp", None),
            P(),
        ),
        out_specs=(P("mp", None, "dp", None), P()),
        check_vma=False,
    )
```

```python
import functools

import jax
import jax.numpy as jnp
from jax import lax
from jax.experimental import pallas as pl
from jax.experimental.pallas import tpu as pltpu
from jax.sharding import PartitionSpec as P

F32 = jnp.float32
BF16 = jnp.bfloat16
LANES = 128
SHORT = pl.CostEstimate(flops=1, bytes_accessed=1, transcendentals=0)


def params(mib):
    return pltpu.CompilerParams(vmem_limit_bytes=mib * 2**20)


def bits_of(n):
    bits = [1 << i for i in range(n.bit_length() - 1)]
    assert 1 << len(bits) == n
    return bits


def swap(value, axis, bit):
    n = lax.axis_size(axis)
    return lax.ppermute(value, axis, [(i, i ^ bit) for i in range(n)])


def gather_xor(value, axis, bits, deps=()):
    held = {0: value}
    for bit in bits:
        for s in list(held):
            held[s | bit] = swap(held[s], axis, bit)
        if deps and len(held) == 2:
            held[bit] = hold(held[bit], deps)
    return held


def gather_rows(value, axis, bits):
    first, places = None, [0]
    for bit in bits:
        arrived = swap(value, axis, bit)
        first = arrived if first is None else first
        value = jnp.concatenate([value, arrived], axis=0)
        places = places + [s ^ bit for s in places]
    return (value, places), first


def gather_direct(value, axis):
    return [value] + [swap(value, axis, s) for s in range(1, lax.axis_size(axis))]


def whole(shape):
    return pl.BlockSpec(shape, lambda *_: (0,) * len(shape))


def after(deps):
    return [pl.BlockSpec(memory_space=pl.ANY)] * len(deps)


def each_tile(n, rows, run):
    group = max(1, 16 // n)

    def body(i, carry):
        run(i * group, group)
        return carry

    lax.fori_loop(0, rows // group, body, 0, unroll=8)


def relayout_kernel(n, n_skip, x, *refs):
    out, order = refs[n_skip:]
    size = order.shape[0]
    rows = size // n

    @pl.when(pl.program_id(0) == 0)
    def _():
        to = lax.broadcasted_iota(jnp.int32, order.shape, 0)
        source = lax.broadcasted_iota(jnp.int32, order.shape, 1)
        order[...] = jnp.where(source == to % rows * n + to // rows, 1.0, 0.0).astype(BF16)

    for part in range(out.shape[1] // rows):
        mixed = jnp.dot(order[...], x[part * size : (part + 1) * size, :], preferred_element_type=F32)
        mixed = mixed.astype(BF16)
        for k in range(n):
            out[k, part * rows : (part + 1) * rows, :] = mixed[k * rows : (k + 1) * rows]


def relayout(flat, n, start, rows, into, deps):
    total, block = flat.shape[0] // n, flat.shape[1]
    step = min(128, rows)
    skipped = list(deps) if into is None else [into, *deps]
    return pl.pallas_call(
        functools.partial(relayout_kernel, n, len(skipped)),
        out_shape=jax.ShapeDtypeStruct((n, total, block), BF16),
        grid=(rows // step,),
        in_specs=[pl.BlockSpec((step * n, block), lambda i: (start // step + i, 0))] + after(skipped),
        out_specs=pl.BlockSpec((n, step, block), lambda i: (0, start // step + i, 0)),
        scratch_shapes=[pltpu.VMEM((256, 256), BF16)],
        input_output_aliases={} if into is None else {1: 0},
        compiler_params=params(48),
        cost_estimate=SHORT,
    )(flat, *skipped)


def hold_kernel(value, *refs):
    refs[-1][...] = value[...]


def hold(value, deps):
    return pl.pallas_call(
        hold_kernel,
        out_shape=jax.ShapeDtypeStruct(value.shape, value.dtype),
        grid=(1,),
        in_specs=[whole(value.shape)] + after(deps),
        out_specs=whole(value.shape),
        compiler_params=params(48),
    )(value, *deps)


def project_kernel(n, n_skip, ks, lhs, *refs):
    ws, (odd, even) = refs[:n], refs[n + n_skip :]
    total, first = 0.0, 0
    for w in ws:
        depth = w.shape[1]
        total = total + jnp.dot(lhs[:, first : first + depth], w[0], preferred_element_type=F32)
        first += depth
    is_odd = pl.program_id(0) % 2 == 0

    @pl.when(is_odd)
    def _():
        odd[0] = total.astype(odd.dtype)

    @pl.when(jnp.logical_not(is_odd))
    def _():
        even[0] = total


def project(lhs, ws, me, pairs, deps=()):
    block = ws[0].shape[2]
    rows, depth = lhs.shape
    count = len(pairs)
    ks = me ^ jnp.array([s for pair in pairs for s in (pair + 1, pair)], jnp.int32)
    return pl.pallas_call(
        functools.partial(project_kernel, len(ws), len(deps)),
        out_shape=[
            jax.ShapeDtypeStruct((count, rows, block), BF16),
            jax.ShapeDtypeStruct((count, rows, block), F32),
        ],
        grid_spec=pltpu.PrefetchScalarGridSpec(
            num_scalar_prefetch=1,
            grid=(2 * count,),
            in_specs=[whole(lhs.shape)]
            + [pl.BlockSpec((1, w.shape[1], block), lambda i, ks: (ks[i], 0, 0)) for w in ws]
            + after(deps),
            out_specs=[pl.BlockSpec((1, rows, block), lambda i, ks: (i // 2, 0, 0))] * 2,
        ),
        compiler_params=params(48),
        cost_estimate=SHORT,
    )(ks, lhs, *ws, *deps)


def pick(term, rows, block):
    array, place = term
    return pl.BlockSpec((1, rows, block), lambda *_: (place, 0, 0))


def add_kernel(n, *refs):
    out = refs[-1]
    total = refs[0][0].astype(F32)
    for ref in refs[1:n]:
        total = total + ref[0].astype(F32)
    out[0] = total.astype(out.dtype)


def add_round(terms, deps=()):
    _, rows, block = terms[0][0].shape
    return pl.pallas_call(
        functools.partial(add_kernel, len(terms)),
        out_shape=jax.ShapeDtypeStruct((1, rows, block), BF16),
        grid=(1,),
        in_specs=[pick(t, rows, block) for t in terms] + after(deps),
        out_specs=whole((1, rows, block)),
        compiler_params=params(48),
    )(*[t[0] for t in terms], *deps)


def act_kernel(n, *refs):
    parts, (h, gain, pre, x) = refs[:n], refs[-4:]
    total = parts[0][0]
    for part in parts[1:]:
        total = total + part[0].astype(F32)
    pre[...] = total
    act = h[...].astype(F32) + total / (1.0 + jnp.exp(-total))
    x[...] = (act * gain[...]).astype(BF16)


def activate(parts, h, gain, deps=()):
    rows, block = h.shape
    return pl.pallas_call(
        functools.partial(act_kernel, len(parts)),
        out_shape=[
            jax.ShapeDtypeStruct((rows, block), F32),
            jax.ShapeDtypeStruct((rows, block), BF16),
        ],
        grid=(1,),
        in_specs=[pick(t, rows, block) for t in parts] + after(deps) + [whole(h.shape), whole(gain.shape)],
        out_specs=[whole((rows, block))] * 2,
        compiler_params=params(48),
    )(*[t[0] for t in parts], *deps, h, gain)


def hop_order(bits):
    places = [0]
    for bit in bits[::-1]:
        places = places + [s | bit for s in places]
    return places


def logits_kernel(order, places, n_gains, me, *refs):
    n = len(order)
    xs, gains, e, (sent, kept) = refs[:n], refs[n : n + n_gains], refs[n + n_gains], refs[-2:]
    total = 0.0
    for s, x in zip(order, xs):
        total = total + lax.dot_general(
            x[...], e[me[0] ^ s], (((1,), (1,)), ((), ())), preferred_element_type=F32
        )
    rows, step = total.shape[0] // len(places), total.shape[1]

    def store(values, at):
        for i, s in enumerate(places):
            out, j = (kept, i) if i < len(places) // 2 else (sent, i - len(places) // 2)
            out[j * rows : (j + 1) * rows, at] = values[s * rows : (s + 1) * rows]

    store(total, pl.ds(pl.multiple_of(pl.program_id(0) * step, step), step))
    if n_gains:

        @pl.when(pl.program_id(0) == 0)
        def _():
            squares = 0.0
            for x, gain in zip(xs, gains):
                act = x[...].astype(F32) / gain[...]
                squares = squares + jnp.sum(act * act, axis=1, keepdims=True)
            size = kept.shape[1] - LANES
            store(jnp.broadcast_to(squares, (squares.shape[0], LANES)), slice(size, size + LANES))


def project_vocab(xs, gains, embed, me, bits, start, size, deps):
    n, _, block = embed.shape
    order = sorted(xs)
    rows = xs[0].shape[0]
    step = min(256, size)
    shape = (rows // 2, size + (LANES if gains else 0))
    return pl.pallas_call(
        functools.partial(logits_kernel, order, hop_order(bits), len(gains)),
        out_shape=[jax.ShapeDtypeStruct(shape, F32)] * 2,
        grid_spec=pltpu.PrefetchScalarGridSpec(
            num_scalar_prefetch=1,
            grid=(size // step,),
            in_specs=[whole((rows, block))] * n
            + [whole(g.shape) for g in gains]
            + [pl.BlockSpec((n, step, block), lambda i, me: (0, start // step + i, 0))]
            + after(deps),
            out_specs=[whole(shape)] * 2,
        ),
        compiler_params=params(48),
        cost_estimate=SHORT,
    )(me, *[xs[s] for s in order], *gains, embed, *deps)


def hop_kernel(n, *refs):
    total = refs[0][...]
    for ref in refs[1:n]:
        total = total + ref[...]
    refs[-1][...] = total


def hop_sum(terms, rows, deps):
    size = terms[0].shape[1]
    return pl.pallas_call(
        functools.partial(hop_kernel, len(terms)),
        out_shape=jax.ShapeDtypeStruct((rows, size), F32),
        grid=(1,),
        in_specs=[pl.BlockSpec((rows, size), lambda i: (1, 0))] * len(terms) + after(deps),
        out_specs=whole((rows, size)),
        compiler_params=params(48),
    )(*terms, *deps)


def sum_hops(pieces, axis, orders):
    terms = [[kept, swap(sent, axis, orders[i][0])] for i, (sent, kept) in enumerate(pieces)]
    rows, before = pieces[0][1].shape[0], []
    for hop in range(1, len(orders[0])):
        rows //= 2
        for i, held in enumerate(terms):
            before = [hop_sum(held, rows, before)]
            held.append(swap(before[0], axis, orders[i][hop]))
    return terms


def softmax_kernel(counts, size, width, *refs):
    parts, (targets, *refs) = refs[: sum(counts)], refs[sum(counts) :]
    qs, stats = refs[:-1], refs[-1]
    target = targets[:, 0:1]
    pieces, hits, at = [], [], 0
    for i, count in enumerate(counts):
        total = parts[at][...]
        for part in parts[at + 1 : at + count]:
            total = total + part[...]
        at += count
        if i == 0:
            inv = lax.rsqrt(total[:, size : size + 1] / width + 1e-05)
            total = total[:, :size]
        ids = lax.broadcasted_iota(jnp.int32, total.shape, 1) + i * size
        pieces.append(total * inv)
        hits.append(ids == target)
    top = functools.reduce(jnp.maximum, [jnp.max(p, axis=1, keepdims=True) for p in pieces])
    mass, moment, picked = 0.0, 0.0, 0.0
    for i, (piece, hit) in enumerate(zip(pieces, hits)):
        shifted = piece - top
        e = jnp.exp(shifted)
        mass = mass + jnp.sum(e, axis=1, keepdims=True)
        moment = moment + jnp.sum(e * shifted, axis=1, keepdims=True)
        picked = picked + jnp.sum(jnp.where(hit, piece, 0.0), axis=1, keepdims=True)
        first = i // len(qs) * size
        qs[i % len(qs)][:, first : first + size] = e.astype(BF16)
    lane = lax.broadcasted_iota(jnp.int32, stats.shape, 1)
    out = jnp.zeros(stats.shape, F32)
    for i, value in enumerate([top, mass, moment, picked, inv]):
        out = jnp.where(lane == i, value, out)
    stats[...] = out


def softmax(pieces, targets, size, width):
    counts = [len(p) for p in pieces]
    flat = [part for p in pieces for part in p]
    rows = targets.shape[0]
    return pl.pallas_call(
        functools.partial(softmax_kernel, counts, size, width),
        out_shape=[jax.ShapeDtypeStruct((rows, len(pieces) // 2 * size), BF16)] * 2
        + [jax.ShapeDtypeStruct((rows, LANES), F32)],
        grid=(1,),
        in_specs=[whole((rows, part.shape[1])) for part in flat] + [whole(targets.shape)],
        out_specs=[whole((rows, len(pieces) // 2 * size))] * 2 + [whole((rows, LANES))],
        compiler_params=params(48),
    )(*flat, targets)


def tree(op, values):
    while len(values) > 1:
        half = len(values) // 2
        values = [op(a, b) for a, b in zip(values[:half], values[half:])]
    return values[0]


def merge_kernel(n, tokens, width, *refs):
    stats, targets, out = refs[:n], refs[n], refs[-1]
    tops = [st[:, 0:1] for st in stats]
    top = tree(jnp.maximum, tops)
    weights = [jnp.exp(t - top) for t in tops]
    mass = tree(jnp.add, [w * st[:, 1:2] for w, st in zip(weights, stats)])
    moment = tree(
        jnp.add, [w * (st[:, 2:3] + st[:, 1:2] * (t - top)) for w, t, st in zip(weights, tops, stats)]
    )
    picked = tree(jnp.add, [st[:, 3:4] for st in stats])
    lse = top + jnp.log(mass)
    inv = stats[0][:, 4:5]
    scale = jnp.exp(tops[0] - lse) / tokens
    at_target = (jnp.exp(picked - lse) - 1.0) / tokens
    pull = (moment / mass + (top - picked)) * (inv * inv) / (tokens * width)
    lane = lax.broadcasted_iota(jnp.int32, out.shape, 1)
    packed = jnp.zeros(out.shape, F32)
    values = [scale, at_target, targets[:, 0:1].astype(F32), inv, pull, lse - picked]
    for i, value in enumerate(values):
        packed = jnp.where(lane == i, value, packed)
    out[...] = packed


def merge(stats, targets, tokens, width, deps):
    n = len(stats)
    return pl.pallas_call(
        functools.partial(merge_kernel, n, tokens, width),
        out_shape=jax.ShapeDtypeStruct(stats[0].shape, F32),
        in_specs=[pl.BlockSpec(memory_space=pltpu.VMEM)] * (n + 1) + after(deps),
        compiler_params=params(48),
    )(*stats, targets, *deps)


def dlogits_kernel(places, quarter, *refs):
    qs, (packs, dlogits) = refs[:-2], refs[-2:]
    n = len(places[0])
    rows = packs.shape[0] // n
    for s in range(n):
        at = slice(s * rows, (s + 1) * rows)
        scale, at_target, target = packs[at, 0:1], packs[at, 1:2], packs[at, 2:3].astype(jnp.int32)
        for i, q in enumerate(qs):
            here = places[i].index(s) * rows
            for j in range(q.shape[1] // quarter):
                first = (j * len(qs) + i) * quarter
                values = q[here : here + rows, j * quarter : (j + 1) * quarter].astype(F32) * scale
                ids = lax.broadcasted_iota(jnp.int32, values.shape, 1) + first
                dlogits[at, first : first + quarter] = jnp.where(ids == target, at_target, values).astype(BF16)


def scale_rows(q, packs, quarter):
    values, places = zip(*q)
    shape = (packs.shape[0], sum(v.shape[1] for v in values))
    return pl.pallas_call(
        functools.partial(dlogits_kernel, places, quarter),
        out_shape=jax.ShapeDtypeStruct(shape, BF16),
        compiler_params=params(48),
    )(*values, packs)


def dpre_kernel(n, *refs):
    parts, (packs, pre, h, gain, out) = refs[:n], refs[n:]
    dnormed = parts[0][0]
    for part in parts[1:]:
        dnormed = dnormed + part[0].astype(F32)
    inv, pull = packs[:, 3:4], packs[:, 4:5]
    v = pre[...]
    sigma = 1.0 / (1.0 + jnp.exp(-v))
    act = h[...].astype(F32) + v * sigma
    dact = inv * gain[...] * dnormed - act * pull
    out[...] = (dact * sigma * (1.0 + v * (1.0 - sigma))).astype(BF16)


def grad_pre(parts, packs, pre, h, gain):
    rows, block = pre.shape
    rest = [packs, pre, h, gain]
    return pl.pallas_call(
        functools.partial(dpre_kernel, len(parts)),
        out_shape=jax.ShapeDtypeStruct(pre.shape, BF16),
        grid=(1,),
        in_specs=[pick(t, rows, block) for t in parts] + [whole(r.shape) for r in rest],
        out_specs=whole(pre.shape),
        compiler_params=params(48),
    )(*[t[0] for t in parts], *rest)


def grad_kernel(order, me, h, *refs):
    n = len(order)
    ds, out, placed, mixed = refs[:n], refs[n], refs[n + 1], refs[n + 2]

    @pl.when(pl.program_id(0) == 0)
    def _():
        for s, d in zip(order, ds):
            placed[me[0] ^ s] = d[...]

    step = h.shape[0]
    lanes = range(0, out.shape[1], LANES)
    for k in range(n):
        product = jnp.dot(h[...], placed[k], preferred_element_type=F32)
        for j, lane in enumerate(lanes):
            mixed[j, pl.ds(k, step, stride=n + 1), :] = product[:, lane : lane + LANES]

    def collect(first, group):
        at = pl.multiple_of(first * n, 16)
        for j, lane in enumerate(lanes):
            parts = [
                mixed[j, pl.ds((first + g) * (n + 1) + p, 8), :] for g in range(group) for p in range(0, n, 8)
            ]
            out[pl.ds(at, group * n), lane : lane + LANES] = jnp.concatenate(parts, axis=0).astype(BF16)

    each_tile(n, step, collect)


def weight_grad(h, ds, me):
    width, rows = h.shape
    n = len(ds)
    block = ds[0].shape[1]
    order = sorted(ds)
    step = min(256, width)
    return pl.pallas_call(
        functools.partial(grad_kernel, order),
        out_shape=jax.ShapeDtypeStruct((width * n, block), BF16),
        grid_spec=pltpu.PrefetchScalarGridSpec(
            num_scalar_prefetch=1,
            grid=(width // step,),
            in_specs=[pl.BlockSpec((step, rows), lambda i, me: (i, 0))] + [whole((rows, block))] * n,
            out_specs=pl.BlockSpec((step * n, block), lambda i, me: (i, 0)),
            scratch_shapes=[pltpu.VMEM((n, rows, block), BF16), pltpu.VMEM((block // LANES, step * (n + 1), LANES), F32)],
        ),
        compiler_params=params(48),
        cost_estimate=SHORT,
    )(me, h, *[ds[s] for s in order])


def column(values):
    return jnp.broadcast_to(values[:, None], (values.shape[0], LANES))


def on_device(hidden_rows, head_weight, norm_gain, vocab_embed, targets):
    n_dp, n_mp = lax.axis_size("dp"), lax.axis_size("mp")
    tok_dp, width_mp = hidden_rows.shape
    block = head_weight.shape[3]
    width = width_mp * n_mp
    tokens = tok_dp * n_dp
    vocab_mp = vocab_embed.shape[0]
    dp_bits, mp_bits = bits_of(n_dp), bits_of(n_mp)
    dp_index = lax.axis_index("dp")
    mp_index = lax.axis_index("mp")
    me = mp_index.astype(jnp.int32).reshape(1)
    pairs = list(range(n_mp - 2, -1, -2))

    embed_rows = vocab_embed.reshape(vocab_mp * n_mp, block)
    gain = norm_gain.reshape(1, block)
    quarter = vocab_mp // 4

    h = jnp.concatenate(gather_direct(hidden_rows, "dp"), axis=0)
    weight = relayout(head_weight.reshape(width_mp * n_mp, block), n_mp, 0, width_mp, None, [])
    own_h = lax.dynamic_slice_in_dim(h, dp_index * block, block, 1)

    def reduce_product(lhs, w, deps, fillers):
        terms = {}

        def run(group, deps):
            odd, even = project(lhs, [w], me, group, deps)
            arrived = swap(odd, "mp", 1)
            for i, s in enumerate(group):
                terms[s] = [(even, i), (arrived, i)]
            return even

        even = run(pairs[:1], deps)
        even = run(pairs[1:2], [even])
        leaving = {pairs[0]: add_round(terms[pairs[0]])}
        before = [even, leaving[pairs[0]]]
        for pair in pairs[2:]:
            before = [run([pair], before)]
        done, made = 1, None
        for bit in mp_bits[1:]:
            senders = [s for s in sorted(terms, reverse=True) if s & bit and not s & done]
            totals = [leaving.get(s) for s in senders]
            for i, s in enumerate(senders):
                if totals[i] is None:
                    totals[i] = add_round(terms[s], [] if made is None else [made])
                terms[s ^ bit].append((swap(totals[i], "mp", bit), 0))
            if fillers:
                made = fillers.pop(0)(made, totals)
            done |= bit
        return terms[0], made

    def fill(first, count):
        def run(into, deps):
            return relayout(embed_rows, n_mp, first * quarter, count * quarter, into, deps)

        return run

    gains = gather_direct(gain, "mp")
    parts, embed = reduce_product(h, weight, gains[1:], [fill(0, 1), fill(1, 2)])
    pre, x = activate(parts, own_h, gain, [embed])

    embed = fill(3, 1)(embed, [x])
    xs = gather_xor(x, "mp", mp_bits[::-1], [embed])
    orders = [dp_bits, dp_bits[::-1]] * 2
    pieces, before = [], []
    for i, order in enumerate(orders):
        pieces.append(project_vocab(xs, [] if i else gains, embed, me, order, i * quarter, quarter, before))
        before = pieces[-1][1:]
    pieces = sum_hops(pieces, "dp", orders)

    local = lax.dynamic_slice_in_dim(targets, dp_index * tok_dp, tok_dp, 0) - mp_index * vocab_mp
    local = column(local)
    *own_q, stats = softmax(pieces, local, quarter, width)
    q, first_hops = zip(*[gather_rows(own_q[i], "dp", orders[i]) for i in range(2)])
    packed = merge(gather_direct(stats, "mp"), local, tokens, width, first_hops)
    packs = jnp.concatenate(gather_direct(packed, "dp"), axis=0)
    sums = [jnp.sum(packs[s * tok_dp : (s + 1) * tok_dp, 5]) for s in range(n_dp)]
    loss = tree(jnp.add, sums) / tokens

    dlogits = scale_rows(q, packs, quarter)
    parts, _ = reduce_product(dlogits, embed, [], [])
    dpre = grad_pre(parts, packs, pre, own_h, gain)
    grad = weight_grad(h.T, gather_xor(dpre, "mp", mp_bits[::-1]), me)
    return (grad.reshape(head_weight.shape), loss)


def solution(mesh):
    return jax.shard_map(
        on_device,
        mesh=mesh,
        in_specs=(
            P("dp", "mp"),
            P("mp", None, "dp", None),
            P("mp", "dp", None),
            P("mp", None, "dp", None),
            P(),
        ),
        out_specs=(P("mp", None, "dp", None), P()),
        check_vma=False,
    )
```

```python
import collections
import functools
import itertools

import jax
import jax.numpy as jnp
from jax import lax
from jax.experimental import pallas as pl
from jax.experimental.pallas import tpu as pltpu
from jax.sharding import PartitionSpec as P

F32 = jnp.float32
BF16 = jnp.bfloat16
LANES = 128
SHORT = pl.CostEstimate(flops=1, bytes_accessed=1, transcendentals=0)


def params(mib):
    return pltpu.CompilerParams(vmem_limit_bytes=mib * 2**20)


def bits_of(n):
    bits = [1 << i for i in range(n.bit_length() - 1)]
    assert 1 << len(bits) == n
    return bits


def swap(value, axis, bit):
    n = lax.axis_size(axis)
    return lax.ppermute(value, axis, [(i, i ^ bit) for i in range(n)])


def gather_xor(value, axis, bits, deps=()):
    held = {0: value}
    if deps:
        first, second = bits[:2]
        held[second] = swap(value, axis, second)
        held[first] = hold(swap(value, axis, first), [*deps, held[second]])
    for bit in bits:
        for s in list(held):
            if s % (2 * bit) == 0 and s | bit not in held:
                held[s | bit] = swap(held[s], axis, bit)
    return held


def join_kernel(a, b, *refs):
    out = refs[-1]
    out[: a.shape[0]] = a[...]
    out[a.shape[0] :] = b[...]


def join(a, b, deps):
    shape = (2 * a.shape[0], a.shape[1])
    return pl.pallas_call(
        join_kernel,
        out_shape=jax.ShapeDtypeStruct(shape, a.dtype),
        grid=(1,),
        in_specs=[whole(a.shape)] * 2 + after(deps),
        out_specs=whole(shape),
        compiler_params=params(48),
    )(a, b, *deps)


def gather_rows(value, axis, bits, deps):
    places, hops = [0], []
    for bit in bits:
        value = join(value, swap(value, axis, bit), [] if hops else deps)
        hops.append(value)
        places = places + [s ^ bit for s in places]
    return (value, places), hops[0]


def gather_direct(value, axis):
    return [value] + [swap(value, axis, s) for s in range(1, lax.axis_size(axis))]


def whole(shape):
    return pl.BlockSpec(shape, lambda *_: (0,) * len(shape))


def stream(sources, buffer, sems, use):
    slots = buffer.shape[0]

    def copy(i):
        return pltpu.make_async_copy(sources[i], buffer.at[i % slots], sems.at[i % slots])

    for i in range(min(slots, len(sources))):
        copy(i).start()
    for i in range(len(sources)):
        copy(i).wait()
        use(i, i % slots)
        if i + slots < len(sources):
            copy(i + slots).start()


def after(deps):
    return [pl.BlockSpec(memory_space=pl.ANY)] * len(deps)


def each_tile(n, rows, run):
    group = max(1, 16 // n)

    def body(i, carry):
        run(i * group, group)
        return carry

    lax.fori_loop(0, rows // group, body, 0, unroll=8)


def relayout_kernel(n, start, rows, step, x, *refs):
    out, order, inputs, outputs, arrived, left = refs[-6:]
    size = order.shape[0]
    group = size // n

    to = lax.broadcasted_iota(jnp.int32, order.shape, 0)
    source = lax.broadcasted_iota(jnp.int32, order.shape, 1)
    order[...] = jnp.where(source == to % group * n + to // group, 1.0, 0.0).astype(BF16)
    slots = outputs.shape[0]

    def leave(i):
        target = out.at[:, pl.ds(start + i * step, step), :]
        return pltpu.make_async_copy(outputs.at[i % slots], target, left.at[i % slots])

    def use(i, slot):
        if i >= slots:
            leave(i - slots).wait()
        for part in range(step // group):
            taken = inputs[slot, part * size : (part + 1) * size, :]
            mixed = jnp.dot(order[...], taken, preferred_element_type=F32).astype(BF16)
            for k in range(n):
                at = slice(part * group, (part + 1) * group)
                outputs[i % slots, k, at, :] = mixed[k * group : (k + 1) * group]
        leave(i).start()

    steps = rows // step
    sources = [x.at[pl.ds((start + i * step) * n, step * n), :] for i in range(steps)]
    stream(sources, inputs, arrived, use)
    for i in range(max(0, steps - slots), steps):
        leave(i).wait()


def relayout(flat, n, start, rows, into, deps):
    total, block = flat.shape[0] // n, flat.shape[1]
    step = min(128, rows)
    slots = 4
    skipped = list(deps) if into is None else [into, *deps]
    return pl.pallas_call(
        functools.partial(relayout_kernel, n, start, rows, step),
        out_shape=jax.ShapeDtypeStruct((n, total, block), BF16),
        in_specs=after([flat, *skipped]),
        out_specs=pl.BlockSpec(memory_space=pl.ANY),
        scratch_shapes=[
            pltpu.VMEM((256, 256), BF16),
            pltpu.VMEM((slots, step * n, block), BF16),
            pltpu.VMEM((slots, n, step, block), BF16),
            pltpu.SemaphoreType.DMA((slots,)),
            pltpu.SemaphoreType.DMA((slots,)),
        ],
        input_output_aliases={} if into is None else {1: 0},
        compiler_params=params(48),
        cost_estimate=SHORT,
    )(flat, *skipped)


def hold_kernel(value, *refs):
    refs[-1][...] = value[...]


def hold(value, deps):
    return pl.pallas_call(
        hold_kernel,
        out_shape=jax.ShapeDtypeStruct(value.shape, value.dtype),
        grid=(1,),
        in_specs=[whole(value.shape)] + after(deps),
        out_specs=whole(value.shape),
        compiler_params=params(48),
    )(value, *deps)


def project_kernel(pair, step, me, lhs, w, *refs):
    odd, even, total, buffer, sems = refs[-5:]
    steps = w.shape[1] // step
    blocks = [me[0] ^ (pair + 1), me[0] ^ pair]
    sources = [w.at[k, pl.ds(c * step, step), :] for k in blocks for c in range(steps)]

    def use(i, slot):
        c = i % steps
        part = jnp.dot(lhs[:, c * step : (c + 1) * step], buffer[slot], preferred_element_type=F32)
        if c > 0:
            part = part + total[...]
        if c < steps - 1:
            total[...] = part
        elif i < steps:
            odd[0] = part.astype(odd.dtype)
        else:
            even[0] = part

    stream(sources, buffer, sems, use)


def project(lhs, w, me, pair, deps):
    _, depth, block = w.shape
    rows = lhs.shape[0]
    step = min(1024, depth)
    slots = 4
    return pl.pallas_call(
        functools.partial(project_kernel, pair, step),
        out_shape=[
            jax.ShapeDtypeStruct((1, rows, block), BF16),
            jax.ShapeDtypeStruct((1, rows, block), F32),
        ],
        grid_spec=pltpu.PrefetchScalarGridSpec(
            num_scalar_prefetch=1,
            grid=(1,),
            in_specs=[whole(lhs.shape)] + after([w, *deps]),
            out_specs=[whole((1, rows, block))] * 2,
            scratch_shapes=[
                pltpu.VMEM((rows, block), F32),
                pltpu.VMEM((slots, step, block), BF16),
                pltpu.SemaphoreType.DMA((slots,)),
            ],
        ),
        compiler_params=params(48),
        cost_estimate=SHORT,
    )(me, lhs, w, *deps)


def pick(term, rows, block):
    array, place = term
    return pl.BlockSpec((1, rows, block), lambda *_: (place, 0, 0))


def add_kernel(n, *refs):
    out = refs[-1]
    total = refs[0][0].astype(F32)
    for ref in refs[1:n]:
        total = total + ref[0].astype(F32)
    out[0] = total.astype(out.dtype)


def add_round(terms, deps=()):
    _, rows, block = terms[0][0].shape
    return pl.pallas_call(
        functools.partial(add_kernel, len(terms)),
        out_shape=jax.ShapeDtypeStruct((1, rows, block), BF16),
        grid=(1,),
        in_specs=[pick(t, rows, block) for t in terms] + after(deps),
        out_specs=whole((1, rows, block)),
        compiler_params=params(48),
    )(*[t[0] for t in terms], *deps)


def square_rows(tokens, block):
    return max(1, tokens // block)


def act_kernel(n, *refs):
    parts, (h, gain, pre, x) = refs[:n], refs[-4:]
    total = parts[0][0].astype(F32)
    for part in parts[1:]:
        total = total + part[0].astype(F32)
    pre[...] = total
    act = h[...].astype(F32) + total / (1.0 + jnp.exp(-total))
    tokens, block = act.shape
    x[:tokens] = (act * gain[...]).astype(BF16)

    sums = jnp.broadcast_to(jnp.sum(act * act, axis=1, keepdims=True), (tokens, LANES))
    rest = jnp.transpose(sums)[0:1]
    count = square_rows(tokens, block)
    span = tokens // count
    row = lax.broadcasted_iota(jnp.int32, (16, span), 0)
    extra = jnp.zeros((16, span), F32)
    for term in range(3):
        high = rest.astype(BF16).astype(F32)
        rest = rest - high
        for i in range(count):
            extra = jnp.where(row == term * count + i, high[:, i * span : (i + 1) * span], extra)
    x[tokens:] = jnp.zeros((16, block), BF16)
    x[tokens:, :span] = extra.astype(BF16)


def activate(parts, h, gain, deps=()):
    rows, block = h.shape
    return pl.pallas_call(
        functools.partial(act_kernel, len(parts)),
        out_shape=[
            jax.ShapeDtypeStruct((rows, block), F32),
            jax.ShapeDtypeStruct((rows + 16, block), BF16),
        ],
        grid=(1,),
        in_specs=[pick(t, rows, block) for t in parts] + after(deps) + [whole(h.shape), whole(gain.shape)],
        out_specs=[whole((rows, block)), whole((rows + 16, block))],
        compiler_params=params(48),
    )(*[t[0] for t in parts], *deps, h, gain)


def hop_order(bits):
    places = [0]
    for bit in bits[::-1]:
        places = places + [s | bit for s in places]
    return places


def logits_kernel(order, places, squares, start, me, *refs):
    n = len(order)
    xs, e, (sent, kept, buffer, sems) = refs[:n], refs[n], refs[-4:]
    tokens, block = xs[0].shape[0] - 16, xs[0].shape[1]
    rows, step = tokens // len(places), buffer.shape[2]
    size = kept.shape[1] - (LANES if squares else 0)

    def store(values, at):
        for i, s in enumerate(places):
            out, j = (kept, i) if i < len(places) // 2 else (sent, i - len(places) // 2)
            out[j * rows : (j + 1) * rows, at] = values[s * rows : (s + 1) * rows]

    def use(i, slot):
        total = 0.0
        for s, x in zip(order, xs):
            total = total + lax.dot_general(
                x[:tokens], buffer[slot, me[0] ^ s], (((1,), (1,)), ((), ())), preferred_element_type=F32
            )
        store(total, slice(i * step, (i + 1) * step))

    sources = [e.at[:, pl.ds(start + i * step, step), :] for i in range(size // step)]
    stream(sources, buffer, sems, use)
    if squares:
        extra = functools.reduce(jnp.add, [x[tokens:].astype(F32) for x in xs])
        count = square_rows(tokens, block)
        span = tokens // count
        for i in range(count):
            terms = [extra[t * count + i : t * count + i + 1, :span] for t in range(3)]
            line = jnp.broadcast_to(functools.reduce(jnp.add, terms), (LANES, span))
            if i == 0:
                columns = jnp.transpose(line)
            else:
                columns = jnp.concatenate([columns, jnp.transpose(line)], axis=0)
        store(columns, slice(size, size + LANES))


def project_vocab(xs, squares, embed, me, bits, start, size, deps):
    n, _, block = embed.shape
    order = sorted(xs)
    rows = xs[0].shape[0] - 16
    step = min(256, size)
    slots = 4
    shape = (rows // 2, size + (LANES if squares else 0))
    return pl.pallas_call(
        functools.partial(logits_kernel, order, hop_order(bits), squares, start),
        out_shape=[jax.ShapeDtypeStruct(shape, F32)] * 2,
        grid_spec=pltpu.PrefetchScalarGridSpec(
            num_scalar_prefetch=1,
            grid=(1,),
            in_specs=[whole((rows + 16, block))] * n + after([embed, *deps]),
            out_specs=[whole(shape)] * 2,
            scratch_shapes=[pltpu.VMEM((slots, n, step, block), BF16), pltpu.SemaphoreType.DMA((slots,))],
        ),
        compiler_params=params(48),
        cost_estimate=SHORT,
    )(me, *[xs[s] for s in order], embed, *deps)


def hop_kernel(n, *refs):
    total = refs[0][...]
    for ref in refs[1:n]:
        total = total + ref[...]
    refs[-1][...] = total


def hop_sum(terms, rows, deps):
    size = terms[0].shape[1]
    return pl.pallas_call(
        functools.partial(hop_kernel, len(terms)),
        out_shape=jax.ShapeDtypeStruct((rows, size), F32),
        grid=(1,),
        in_specs=[pl.BlockSpec((rows, size), lambda i: (1, 0))] * len(terms) + after(deps),
        out_specs=whole((rows, size)),
        compiler_params=params(48),
    )(*terms, *deps)


def sum_hops(pieces, axis, orders):
    terms = [[kept, swap(sent, axis, orders[i][0])] for i, (sent, kept) in enumerate(pieces)]
    rows, before = pieces[0][1].shape[0], []
    for hop in range(1, len(orders[0])):
        rows //= 2
        for i, held in enumerate(terms):
            before = [hop_sum(held, rows, before)]
            held.append(swap(before[0], axis, orders[i][hop]))
    return terms


def softmax_kernel(counts, size, width, *refs):
    parts, (targets, *refs) = refs[: sum(counts)], refs[sum(counts) :]
    qs, stats = refs[:-1], refs[-1]
    target = targets[:, 0:1]
    pieces, hits, at = [], [], 0
    for i, count in enumerate(counts):
        total = parts[at][...]
        for part in parts[at + 1 : at + count]:
            total = total + part[...]
        at += count
        if i == 0:
            inv = lax.rsqrt(total[:, size : size + 1] / width + 1e-05)
            total = total[:, :size]
        ids = lax.broadcasted_iota(jnp.int32, total.shape, 1) + i * size
        pieces.append(total * inv)
        hits.append(ids == target)
    top = functools.reduce(jnp.maximum, [jnp.max(p, axis=1, keepdims=True) for p in pieces])
    mass, moment, picked = 0.0, 0.0, 0.0
    for i, (piece, hit) in enumerate(zip(pieces, hits)):
        shifted = piece - top
        e = jnp.exp(shifted)
        mass = mass + jnp.sum(e, axis=1, keepdims=True)
        moment = moment + jnp.sum(e * shifted, axis=1, keepdims=True)
        picked = picked + jnp.sum(jnp.where(hit, piece, 0.0), axis=1, keepdims=True)
        first = i // len(qs) * size
        qs[i % len(qs)][:, first : first + size] = e.astype(BF16)
    stats[...] = lanes_of([top, mass, moment, picked, inv], stats.shape)


def softmax(pieces, targets, size, width):
    counts = [len(p) for p in pieces]
    flat = [part for p in pieces for part in p]
    rows = targets.shape[0]
    return pl.pallas_call(
        functools.partial(softmax_kernel, counts, size, width),
        out_shape=[jax.ShapeDtypeStruct((rows, len(pieces) // 2 * size), BF16)] * 2
        + [jax.ShapeDtypeStruct((rows, LANES), F32)],
        grid=(1,),
        in_specs=[whole((rows, part.shape[1])) for part in flat] + [whole(targets.shape)],
        out_specs=[whole((rows, len(pieces) // 2 * size))] * 2 + [whole((rows, LANES))],
        compiler_params=params(48),
    )(*flat, targets)


def tree(op, values):
    while len(values) > 1:
        half = len(values) // 2
        values = [op(a, b) for a, b in zip(values[:half], values[half:])]
    return values[0]


def lanes_of(values, shape):
    lane = lax.broadcasted_iota(jnp.int32, shape, 1)
    out = jnp.zeros(shape, F32)
    for i, value in enumerate(values):
        out = jnp.where(lane == i, value, out)
    return out


def merge_two(a, b):
    top = jnp.maximum(a[:, 0:1], b[:, 0:1])
    mass, moment = 0.0, 0.0
    for part in (a, b):
        shift = part[:, 0:1] - top
        weight = jnp.exp(shift)
        mass = mass + weight * part[:, 1:2]
        moment = moment + weight * (part[:, 2:3] + part[:, 1:2] * shift)
    return top, mass, moment, a[:, 3:4] + b[:, 3:4]


def merge_kernel(a, b, *refs):
    refs[-1][...] = lanes_of(merge_two(a[...], b[...]), refs[-1].shape)


def finish_kernel(tokens, width, a, b, own, targets, *refs):
    top, mass, moment, picked = merge_two(a[...], b[...])
    lse = top + jnp.log(mass)
    inv = own[:, 4:5]
    scale = jnp.exp(own[:, 0:1] - lse) / tokens
    at_target = (jnp.exp(picked - lse) - 1.0) / tokens
    pull = (moment / mass + (top - picked)) * (inv * inv) / (tokens * width)
    values = [scale, at_target, targets[:, 0:1].astype(F32), inv, pull, lse - picked]
    refs[-1][...] = lanes_of(values, refs[-1].shape)


def merge(body, values, deps):
    shape = values[0].shape
    return pl.pallas_call(
        body,
        out_shape=jax.ShapeDtypeStruct(shape, F32),
        grid=(1,),
        in_specs=[whole(shape)] * len(values) + after(deps),
        out_specs=whole(shape),
        compiler_params=params(48),
    )(*values, *deps)


def dlogits_kernel(places, quarter, *refs):
    qs, (packs, dlogits, loss) = refs[:-3], refs[-3:]
    n = len(places[0])
    rows = packs.shape[0] // n
    sums = [jnp.sum(packs[s * rows : (s + 1) * rows, 5:6], axis=0, keepdims=True) for s in range(n)]
    loss[...] = jnp.broadcast_to(tree(jnp.add, sums) / packs.shape[0], loss.shape)
    for s in range(n):
        at = slice(s * rows, (s + 1) * rows)
        scale, at_target, target = packs[at, 0:1], packs[at, 1:2], packs[at, 2:3].astype(jnp.int32)
        for i, q in enumerate(qs):
            here = places[i].index(s) * rows
            for j in range(q.shape[1] // quarter):
                first = (j * len(qs) + i) * quarter
                values = q[here : here + rows, j * quarter : (j + 1) * quarter].astype(F32) * scale
                ids = lax.broadcasted_iota(jnp.int32, values.shape, 1) + first
                dlogits[at, first : first + quarter] = jnp.where(ids == target, at_target, values).astype(BF16)


def scale_rows(q, packs, quarter):
    values, places = zip(*q)
    shape = (packs.shape[0], sum(v.shape[1] for v in values))
    return pl.pallas_call(
        functools.partial(dlogits_kernel, places, quarter),
        out_shape=[jax.ShapeDtypeStruct(shape, BF16), jax.ShapeDtypeStruct((8, LANES), F32)],
        compiler_params=params(48),
    )(*values, packs)


def dpre_kernel(n, *refs):
    parts, (packs, pre, h, gain, out) = refs[:n], refs[n:]
    dnormed = parts[0][0]
    for part in parts[1:]:
        dnormed = dnormed + part[0].astype(F32)
    inv, pull = packs[:, 3:4], packs[:, 4:5]
    v = pre[...]
    sigma = 1.0 / (1.0 + jnp.exp(-v))
    act = h[...].astype(F32) + v * sigma
    dact = inv * gain[...] * dnormed - act * pull
    out[...] = (dact * sigma * (1.0 + v * (1.0 - sigma))).astype(BF16)


def grad_pre(parts, packs, pre, h, gain):
    rows, block = pre.shape
    rest = [packs, pre, h, gain]
    return pl.pallas_call(
        functools.partial(dpre_kernel, len(parts)),
        out_shape=jax.ShapeDtypeStruct(pre.shape, BF16),
        grid=(1,),
        in_specs=[pick(t, rows, block) for t in parts] + [whole(r.shape) for r in rest],
        out_specs=whole(pre.shape),
        compiler_params=params(48),
    )(*[t[0] for t in parts], *rest)


def grad_kernel(order, step, me, h, *refs):
    n = len(order)
    ds, (out, placed, mixed, outputs, left) = refs[:n], refs[n:]
    slots = outputs.shape[0]
    lanes = range(0, out.shape[1], LANES)
    for s, d in zip(order, ds):
        placed[me[0] ^ s] = d[...]

    def leave(i):
        target = out.at[pl.ds(i * step * n, step * n), :]
        return pltpu.make_async_copy(outputs.at[i % slots], target, left.at[i % slots])

    steps = h.shape[0] // step
    for i in range(steps):
        if i >= slots:
            leave(i - slots).wait()
        for k in range(n):
            product = jnp.dot(h[i * step : (i + 1) * step, :], placed[k], preferred_element_type=F32)
            for j, lane in enumerate(lanes):
                mixed[j, pl.ds(k, step, stride=n + 1), :] = product[:, lane : lane + LANES]

        def collect(first, group):
            at = pl.multiple_of(first * n, 16)
            for j, lane in enumerate(lanes):
                parts = [
                    mixed[j, pl.ds((first + g) * (n + 1) + p, 8), :]
                    for g in range(group)
                    for p in range(0, n, 8)
                ]
                values = jnp.concatenate(parts, axis=0).astype(BF16)
                outputs[i % slots, pl.ds(at, group * n), lane : lane + LANES] = values

        each_tile(n, step, collect)
        leave(i).start()
    for i in range(max(0, steps - slots), steps):
        leave(i).wait()


def weight_grad(h, ds, me):
    width, rows = h.shape
    n = len(ds)
    block = ds[0].shape[1]
    order = sorted(ds)
    step = min(256, width)
    slots = 3
    return pl.pallas_call(
        functools.partial(grad_kernel, order, step),
        out_shape=jax.ShapeDtypeStruct((width * n, block), BF16),
        grid_spec=pltpu.PrefetchScalarGridSpec(
            num_scalar_prefetch=1,
            grid=(1,),
            in_specs=[whole(h.shape)] + [whole((rows, block))] * n,
            out_specs=pl.BlockSpec(memory_space=pl.ANY),
            scratch_shapes=[
                pltpu.VMEM((n, rows, block), BF16),
                pltpu.VMEM((block // LANES, step * (n + 1), LANES), F32),
                pltpu.VMEM((slots, step * n, block), BF16),
                pltpu.SemaphoreType.DMA((slots,)),
            ],
        ),
        compiler_params=params(48),
        cost_estimate=SHORT,
    )(me, h, *[ds[s] for s in order])


def column(values):
    return jnp.broadcast_to(values[:, None], (values.shape[0], LANES))


def on_device(hidden_rows, head_weight, norm_gain, vocab_embed, targets):
    n_dp, n_mp = lax.axis_size("dp"), lax.axis_size("mp")
    tok_dp, width_mp = hidden_rows.shape
    block = head_weight.shape[3]
    width = width_mp * n_mp
    tokens = tok_dp * n_dp
    vocab_mp = vocab_embed.shape[0]
    dp_bits, mp_bits = bits_of(n_dp), bits_of(n_mp)
    dp_index = lax.axis_index("dp")
    mp_index = lax.axis_index("mp")
    me = mp_index.astype(jnp.int32).reshape(1)
    pairs = list(range(n_mp - 2, -1, -2))

    embed_rows = vocab_embed.reshape(vocab_mp * n_mp, block)
    gain = norm_gain.reshape(1, block)
    quarter = vocab_mp // 4

    h = jnp.concatenate(gather_direct(hidden_rows, "dp"), axis=0)
    weight = relayout(head_weight.reshape(width_mp * n_mp, block), n_mp, 0, width_mp, None, [])
    own_h = lax.dynamic_slice_in_dim(h, dp_index * block, block, 1)

    def reduce_product(lhs, w, fillers):
        terms, totals, made = collections.defaultdict(list), {}, None

        def run(pair, deps):
            odd, even = project(lhs, w, me, pair, deps)
            terms[pair][:0] = [(even, 0), (swap(odd, "mp", 1), 0)]
            return [even]

        def leave(s, bit, deps=()):
            totals[s] = add_round(terms[s], deps)
            terms[s ^ bit].append((swap(totals[s], "mp", bit), 0))

        first, second = pairs[:2]
        before = run(second, run(first, []))
        leave(first, mp_bits[1])
        before = [*run(pairs[2], [*before, totals[first]]), totals[first]]
        leave(second, mp_bits[2])
        if pairs[3:] == [0] and not any(fillers):
            leave(pairs[2], mp_bits[1])
            before.append(terms[0][-1][0])
        else:
            before.append(totals[second])
        for pair in pairs[3:]:
            before = run(pair, before)
        done = 1
        for bit, filler in itertools.zip_longest(mp_bits[1:], fillers):
            for s in sorted(terms, reverse=True):
                if s & bit and not s & done and s not in totals:
                    leave(s, bit, [] if made is None else [made])
            done |= bit
            if filler:
                made = filler(None, list(totals.values()))
        return terms[0], made

    def fill(first, count):
        def run(into, deps):
            return relayout(embed_rows, n_mp, first * quarter, count * quarter, into, deps)

        return run

    parts, embed = reduce_product(h, weight, [None, fill(0, 2)])
    pre, x = activate(parts, own_h, gain, [embed])

    embed = fill(2, 2)(embed, [x])
    xs = gather_xor(x, "mp", mp_bits[::-1], [embed])
    orders = [dp_bits, dp_bits[::-1]] * 2
    pieces, before = [], []
    for i, order in enumerate(orders):
        pieces.append(project_vocab(xs, i == 0, embed, me, order, i * quarter, quarter, before))
        before = pieces[-1][1:]
    pieces = sum_hops(pieces, "dp", orders)

    local = lax.dynamic_slice_in_dim(targets, dp_index * tok_dp, tok_dp, 0) - mp_index * vocab_mp
    local = column(local)
    *own_q, stats = softmax(pieces, local, quarter, width)
    total = merge(merge_kernel, [stats, swap(stats, "mp", mp_bits[0])], [])
    q, hops = zip(*[gather_rows(own_q[i], "dp", orders[i], [total]) for i in range(2)])
    for bit in mp_bits[1:-1]:
        total = merge(merge_kernel, [total, swap(total, "mp", bit)], hops)
    finish = functools.partial(finish_kernel, tokens, width)
    packed = merge(finish, [total, swap(total, "mp", mp_bits[-1]), stats, local], [])
    packs = jnp.concatenate(gather_direct(packed, "dp"), axis=0)
    dlogits, loss = scale_rows(q, packs, quarter)
    parts, _ = reduce_product(dlogits, embed, [None, None])
    dpre = grad_pre(parts, packs, pre, own_h, gain)
    grad = weight_grad(h.T, gather_xor(dpre, "mp", mp_bits[::-1]), me)
    return (grad.reshape(head_weight.shape), loss[0, 0])


def solution(mesh):
    return jax.shard_map(
        on_device,
        mesh=mesh,
        in_specs=(
            P("dp", "mp"),
            P("mp", None, "dp", None),
            P("mp", "dp", None),
            P("mp", None, "dp", None),
            P(),
        ),
        out_specs=(P("mp", None, "dp", None), P()),
        check_vma=False,
    )
```

```python
import collections
import functools
import itertools

import jax
import jax.numpy as jnp
from jax import lax
from jax.experimental import pallas as pl
from jax.experimental.pallas import tpu as pltpu
from jax.sharding import PartitionSpec as P

F32 = jnp.float32
BF16 = jnp.bfloat16
LANES = 128
SHORT = pl.CostEstimate(flops=1, bytes_accessed=1, transcendentals=0)


def params(mib):
    return pltpu.CompilerParams(vmem_limit_bytes=mib * 2**20)


def bits_of(n):
    bits = [1 << i for i in range(n.bit_length() - 1)]
    assert 1 << len(bits) == n
    return bits


def swap(value, axis, bit):
    n = lax.axis_size(axis)
    return lax.ppermute(value, axis, [(i, i ^ bit) for i in range(n)])


def gather_xor(value, axis, bits, deps=()):
    held = {0: value}
    if deps:
        first, second = bits[:2]
        held[second] = swap(value, axis, second)
        held[first] = hold(swap(value, axis, first), [*deps, held[second]])
    for bit in bits:
        for s in list(held):
            if s % (2 * bit) == 0 and s | bit not in held:
                held[s | bit] = swap(held[s], axis, bit)
    return held


def join_kernel(a, b, *refs):
    out = refs[-1]
    out[: a.shape[0]] = a[...]
    out[a.shape[0] :] = b[...]


def join(a, b, deps):
    shape = (2 * a.shape[0], a.shape[1])
    return pl.pallas_call(
        join_kernel,
        out_shape=jax.ShapeDtypeStruct(shape, a.dtype),
        grid=(1,),
        in_specs=[whole(a.shape)] * 2 + after(deps),
        out_specs=whole(shape),
        compiler_params=params(48),
    )(a, b, *deps)


def gather_rows(value, axis, bits, deps):
    places, hops = [0], []
    for bit in bits[:-1]:
        value = join(value, swap(value, axis, bit), [] if hops else deps)
        hops.append(value)
        places = places + [s ^ bit for s in places]
    arrived = swap(value, axis, bits[-1])
    return [(value, places), (arrived, [s ^ bits[-1] for s in places])], hops[0]


def lay_kernel(places, *refs):
    out = refs[-1]
    width = refs[0].shape[1]
    for i, order in enumerate(places):
        rows = refs[i].shape[0] // len(order)
        first = i // 2 * width
        for j, s in enumerate(order):
            out[s * rows : (s + 1) * rows, first : first + width] = refs[i][j * rows : (j + 1) * rows]


def lay(gathered):
    values, places = zip(*[part for half in gathered for part in half])
    shape = (2 * values[0].shape[0], 2 * values[0].shape[1])
    return pl.pallas_call(
        functools.partial(lay_kernel, places),
        out_shape=jax.ShapeDtypeStruct(shape, values[0].dtype),
        grid=(1,),
        in_specs=[whole(v.shape) for v in values],
        out_specs=whole(shape),
        compiler_params=params(48),
    )(*values)


def gather_direct(value, axis):
    return [value] + [swap(value, axis, s) for s in range(1, lax.axis_size(axis))]


def whole(shape):
    return pl.BlockSpec(shape, lambda *_: (0,) * len(shape))


def stream(sources, buffer, sems, use):
    slots = buffer.shape[0]

    def copy(i):
        return pltpu.make_async_copy(sources[i], buffer.at[i % slots], sems.at[i % slots])

    for i in range(min(slots, len(sources))):
        copy(i).start()
    for i in range(len(sources)):
        copy(i).wait()
        use(i, i % slots)
        if i + slots < len(sources):
            copy(i + slots).start()


def after(deps):
    return [pl.BlockSpec(memory_space=pl.ANY)] * len(deps)


def each_tile(n, rows, run):
    group = max(1, 16 // n)

    def body(i, carry):
        run(i * group, group)
        return carry

    lax.fori_loop(0, rows // group, body, 0, unroll=8)


def relayout_kernel(n, start, rows, step, x, *refs):
    out, order, inputs, outputs, arrived, left = refs[-6:]
    size = order.shape[0]
    group = size // n

    to = lax.broadcasted_iota(jnp.int32, order.shape, 0)
    source = lax.broadcasted_iota(jnp.int32, order.shape, 1)
    order[...] = jnp.where(source == to % group * n + to // group, 1.0, 0.0).astype(BF16)
    slots = outputs.shape[0]

    def leave(i):
        target = out.at[:, pl.ds(start + i * step, step), :]
        return pltpu.make_async_copy(outputs.at[i % slots], target, left.at[i % slots])

    def use(i, slot):
        if i >= slots:
            leave(i - slots).wait()
        for part in range(step // group):
            taken = inputs[slot, part * size : (part + 1) * size, :]
            mixed = jnp.dot(order[...], taken, preferred_element_type=F32).astype(BF16)
            for k in range(n):
                at = slice(part * group, (part + 1) * group)
                outputs[i % slots, k, at, :] = mixed[k * group : (k + 1) * group]
        leave(i).start()

    steps = rows // step
    sources = [x.at[pl.ds((start + i * step) * n, step * n), :] for i in range(steps)]
    stream(sources, inputs, arrived, use)
    for i in range(max(0, steps - slots), steps):
        leave(i).wait()


def relayout(flat, n, start, rows, into, deps):
    total, block = flat.shape[0] // n, flat.shape[1]
    step = min(128, rows)
    slots = 4
    skipped = list(deps) if into is None else [into, *deps]
    return pl.pallas_call(
        functools.partial(relayout_kernel, n, start, rows, step),
        out_shape=jax.ShapeDtypeStruct((n, total, block), BF16),
        in_specs=after([flat, *skipped]),
        out_specs=pl.BlockSpec(memory_space=pl.ANY),
        scratch_shapes=[
            pltpu.VMEM((256, 256), BF16),
            pltpu.VMEM((slots, step * n, block), BF16),
            pltpu.VMEM((slots, n, step, block), BF16),
            pltpu.SemaphoreType.DMA((slots,)),
            pltpu.SemaphoreType.DMA((slots,)),
        ],
        input_output_aliases={} if into is None else {1: 0},
        compiler_params=params(48),
        cost_estimate=SHORT,
    )(flat, *skipped)


def hold_kernel(value, *refs):
    refs[-1][...] = value[...]


def hold(value, deps):
    return pl.pallas_call(
        hold_kernel,
        out_shape=jax.ShapeDtypeStruct(value.shape, value.dtype),
        grid=(1,),
        in_specs=[whole(value.shape)] + after(deps),
        out_specs=whole(value.shape),
        compiler_params=params(48),
    )(value, *deps)


def project_kernel(pairs, step, me, lhs, w, *refs):
    total, buffer, sems = refs[-3:]
    outs = refs[-3 - 2 * len(pairs) : -3]
    steps = w.shape[1] // step
    blocks = [me[0] ^ s for pair in pairs for s in (pair + 1, pair)]
    sources = [w.at[k, pl.ds(c * step, step), :] for k in blocks for c in range(steps)]

    def use(i, slot):
        c = i % steps
        part = jnp.dot(lhs[:, c * step : (c + 1) * step], buffer[slot], preferred_element_type=F32)
        if c > 0:
            part = part + total[...]
        if c < steps - 1:
            total[...] = part
        else:
            out = outs[i // steps]
            out[0] = part.astype(out.dtype)

    stream(sources, buffer, sems, use)


def project(lhs, w, me, pairs, deps):
    _, depth, block = w.shape
    rows = lhs.shape[0]
    step = min(1024, depth)
    slots = 4
    out = whole((1, rows, block))
    return pl.pallas_call(
        functools.partial(project_kernel, pairs, step),
        out_shape=[jax.ShapeDtypeStruct((1, rows, block), kind) for _ in pairs for kind in (BF16, F32)],
        grid_spec=pltpu.PrefetchScalarGridSpec(
            num_scalar_prefetch=1,
            grid=(1,),
            in_specs=[whole(lhs.shape)] + after([w, *deps]),
            out_specs=[out] * (2 * len(pairs)),
            scratch_shapes=[
                pltpu.VMEM((rows, block), F32),
                pltpu.VMEM((slots, step, block), BF16),
                pltpu.SemaphoreType.DMA((slots,)),
            ],
        ),
        compiler_params=params(48),
        cost_estimate=SHORT,
    )(me, lhs, w, *deps)


def pick(term, rows, block):
    array, place = term
    return pl.BlockSpec((1, rows, block), lambda *_: (place, 0, 0))


def add_kernel(n, *refs):
    out = refs[-1]
    total = refs[0][0].astype(F32)
    for ref in refs[1:n]:
        total = total + ref[0].astype(F32)
    out[0] = total.astype(out.dtype)


def add_round(terms, deps=()):
    _, rows, block = terms[0][0].shape
    return pl.pallas_call(
        functools.partial(add_kernel, len(terms)),
        out_shape=jax.ShapeDtypeStruct((1, rows, block), BF16),
        grid=(1,),
        in_specs=[pick(t, rows, block) for t in terms] + after(deps),
        out_specs=whole((1, rows, block)),
        compiler_params=params(48),
    )(*[t[0] for t in terms], *deps)


def square_rows(tokens, block):
    return max(1, tokens // block)


def act_kernel(n, *refs):
    parts, (h, gain, pre, x) = refs[:n], refs[-4:]
    total = parts[0][0].astype(F32)
    for part in parts[1:]:
        total = total + part[0].astype(F32)
    pre[...] = total
    act = h[...].astype(F32) + total / (1.0 + jnp.exp(-total))
    tokens, block = act.shape
    x[:tokens] = (act * gain[...]).astype(BF16)

    sums = jnp.broadcast_to(jnp.sum(act * act, axis=1, keepdims=True), (tokens, LANES))
    rest = jnp.transpose(sums)[0:1]
    count = square_rows(tokens, block)
    span = tokens // count
    row = lax.broadcasted_iota(jnp.int32, (16, span), 0)
    extra = jnp.zeros((16, span), F32)
    for term in range(3):
        high = rest.astype(BF16).astype(F32)
        rest = rest - high
        for i in range(count):
            extra = jnp.where(row == term * count + i, high[:, i * span : (i + 1) * span], extra)
    x[tokens:] = jnp.zeros((16, block), BF16)
    x[tokens:, :span] = extra.astype(BF16)


def activate(parts, h, gain, deps=()):
    rows, block = h.shape
    return pl.pallas_call(
        functools.partial(act_kernel, len(parts)),
        out_shape=[
            jax.ShapeDtypeStruct((rows, block), F32),
            jax.ShapeDtypeStruct((rows + 16, block), BF16),
        ],
        grid=(1,),
        in_specs=[pick(t, rows, block) for t in parts] + after(deps) + [whole(h.shape), whole(gain.shape)],
        out_specs=[whole((rows, block)), whole((rows + 16, block))],
        compiler_params=params(48),
    )(*[t[0] for t in parts], *deps, h, gain)


def hop_order(bits):
    places = [0]
    for bit in bits[::-1]:
        places = places + [s | bit for s in places]
    return places


def logits_kernel(order, places, squares, start, me, *refs):
    n = len(order)
    xs, e, (sent, kept, total, buffer, sems) = refs[:n], refs[n], refs[-5:]
    tokens, block = xs[0].shape[0] - 16, xs[0].shape[1]
    rows = tokens // len(places)
    size = kept.shape[1] - (LANES if squares else 0)

    def store(values, at):
        for i, s in enumerate(places):
            out, j = (kept, i) if i < len(places) // 2 else (sent, i - len(places) // 2)
            out[j * rows : (j + 1) * rows, at] = values[s * rows : (s + 1) * rows]

    def use(i, slot):
        part = lax.dot_general(
            xs[i][:tokens], buffer[slot], (((1,), (1,)), ((), ())), preferred_element_type=F32
        )
        if i > 0:
            part = part + total[...]
        if i < n - 1:
            total[...] = part
        else:
            store(part, slice(0, size))

    stream([e.at[me[0] ^ s, pl.ds(start, size), :] for s in order], buffer, sems, use)
    if squares:
        extra = functools.reduce(jnp.add, [x[tokens:].astype(F32) for x in xs])
        count = square_rows(tokens, block)
        span = tokens // count
        for i in range(count):
            terms = [extra[t * count + i : t * count + i + 1, :span] for t in range(3)]
            line = jnp.broadcast_to(functools.reduce(jnp.add, terms), (LANES, span))
            if i == 0:
                columns = jnp.transpose(line)
            else:
                columns = jnp.concatenate([columns, jnp.transpose(line)], axis=0)
        store(columns, slice(size, size + LANES))


def project_vocab(xs, squares, embed, me, bits, start, size, deps):
    n, _, block = embed.shape
    order = sorted(xs)
    rows = xs[0].shape[0] - 16
    slots = 4
    shape = (rows // 2, size + (LANES if squares else 0))
    return pl.pallas_call(
        functools.partial(logits_kernel, order, hop_order(bits), squares, start),
        out_shape=[jax.ShapeDtypeStruct(shape, F32)] * 2,
        grid_spec=pltpu.PrefetchScalarGridSpec(
            num_scalar_prefetch=1,
            grid=(1,),
            in_specs=[whole((rows + 16, block))] * n + after([embed, *deps]),
            out_specs=[whole(shape)] * 2,
            scratch_shapes=[
                pltpu.VMEM((rows, size), F32),
                pltpu.VMEM((slots, size, block), BF16),
                pltpu.SemaphoreType.DMA((slots,)),
            ],
        ),
        compiler_params=params(48),
        cost_estimate=SHORT,
    )(me, *[xs[s] for s in order], embed, *deps)


def hop_kernel(n, *refs):
    total = refs[0][...]
    for ref in refs[1:n]:
        total = total + ref[...]
    refs[-1][...] = total


def hop_sum(terms, rows, deps):
    size = terms[0].shape[1]
    return pl.pallas_call(
        functools.partial(hop_kernel, len(terms)),
        out_shape=jax.ShapeDtypeStruct((rows, size), F32),
        grid=(1,),
        in_specs=[pl.BlockSpec((rows, size), lambda i: (1, 0))] * len(terms) + after(deps),
        out_specs=whole((rows, size)),
        compiler_params=params(48),
    )(*terms, *deps)


def sum_hops(pieces, axis, orders):
    terms = [[kept, swap(sent, axis, orders[i][0])] for i, (sent, kept) in enumerate(pieces)]
    rows, before = pieces[0][1].shape[0], []
    for hop in range(1, len(orders[0])):
        rows //= 2
        for i, held in enumerate(terms):
            before = [hop_sum(held, rows, before)]
            held.append(swap(before[0], axis, orders[i][hop]))
    return terms


def softmax_kernel(counts, size, width, *refs):
    parts, (targets, *refs) = refs[: sum(counts)], refs[sum(counts) :]
    qs, stats = refs[:-1], refs[-1]
    target = targets[:, 0:1]
    pieces, hits, at = [], [], 0
    for i, count in enumerate(counts):
        total = parts[at][...]
        for part in parts[at + 1 : at + count]:
            total = total + part[...]
        at += count
        if i == 0:
            inv = lax.rsqrt(total[:, size : size + 1] / width + 1e-05)
            total = total[:, :size]
        ids = lax.broadcasted_iota(jnp.int32, total.shape, 1) + i * size
        pieces.append(total * inv)
        hits.append(ids == target)
    top = functools.reduce(jnp.maximum, [jnp.max(p, axis=1, keepdims=True) for p in pieces])
    mass, moment, picked = 0.0, 0.0, 0.0
    for i, (piece, hit) in enumerate(zip(pieces, hits)):
        shifted = piece - top
        e = jnp.exp(shifted)
        mass = mass + jnp.sum(e, axis=1, keepdims=True)
        moment = moment + jnp.sum(e * shifted, axis=1, keepdims=True)
        picked = picked + jnp.sum(jnp.where(hit, piece, 0.0), axis=1, keepdims=True)
        first = i // len(qs) * size
        qs[i % len(qs)][:, first : first + size] = e.astype(BF16)
    stats[...] = lanes_of([top, mass, moment, picked, inv], stats.shape)


def softmax(pieces, targets, size, width):
    counts = [len(p) for p in pieces]
    flat = [part for p in pieces for part in p]
    rows = targets.shape[0]
    return pl.pallas_call(
        functools.partial(softmax_kernel, counts, size, width),
        out_shape=[jax.ShapeDtypeStruct((rows, len(pieces) // 2 * size), BF16)] * 2
        + [jax.ShapeDtypeStruct((rows, LANES), F32)],
        grid=(1,),
        in_specs=[whole((rows, part.shape[1])) for part in flat] + [whole(targets.shape)],
        out_specs=[whole((rows, len(pieces) // 2 * size))] * 2 + [whole((rows, LANES))],
        compiler_params=params(48),
    )(*flat, targets)


def tree(op, values):
    while len(values) > 1:
        half = len(values) // 2
        values = [op(a, b) for a, b in zip(values[:half], values[half:])]
    return values[0]


def lanes_of(values, shape):
    lane = lax.broadcasted_iota(jnp.int32, shape, 1)
    out = jnp.zeros(shape, F32)
    for i, value in enumerate(values):
        out = jnp.where(lane == i, value, out)
    return out


def merge_two(a, b):
    top = jnp.maximum(a[:, 0:1], b[:, 0:1])
    mass, moment = 0.0, 0.0
    for part in (a, b):
        shift = part[:, 0:1] - top
        weight = jnp.exp(shift)
        mass = mass + weight * part[:, 1:2]
        moment = moment + weight * (part[:, 2:3] + part[:, 1:2] * shift)
    return top, mass, moment, a[:, 3:4] + b[:, 3:4]


def merge_kernel(a, b, *refs):
    refs[-1][...] = lanes_of(merge_two(a[...], b[...]), refs[-1].shape)


def finish_kernel(tokens, width, a, b, own, targets, *refs):
    top, mass, moment, picked = merge_two(a[...], b[...])
    lse = top + jnp.log(mass)
    inv = own[:, 4:5]
    scale = jnp.exp(own[:, 0:1] - lse) / tokens
    at_target = (jnp.exp(picked - lse) - 1.0) / tokens
    pull = (moment / mass + (top - picked)) * (inv * inv) / (tokens * width)
    values = [scale, at_target, targets[:, 0:1].astype(F32), inv, pull, lse - picked]
    refs[-1][...] = lanes_of(values, refs[-1].shape)


def merge(body, values, deps):
    shape = values[0].shape
    return pl.pallas_call(
        body,
        out_shape=jax.ShapeDtypeStruct(shape, F32),
        grid=(1,),
        in_specs=[whole(shape)] * len(values) + after(deps),
        out_specs=whole(shape),
        compiler_params=params(48),
    )(*values, *deps)


def dlogits_kernel(places, quarter, *refs):
    qs, (packs, dlogits, loss) = refs[:-3], refs[-3:]
    n = 2 * len(places[0])
    rows = packs.shape[0] // n
    sums = [jnp.sum(packs[s * rows : (s + 1) * rows, 5:6], axis=0, keepdims=True) for s in range(n)]
    loss[...] = jnp.broadcast_to(tree(jnp.add, sums) / packs.shape[0], loss.shape)
    for i, (q, order) in enumerate(zip(qs, places)):
        for here, s in enumerate(order):
            at = slice(s * rows, (s + 1) * rows)
            scale, at_target, target = packs[at, 0:1], packs[at, 1:2], packs[at, 2:3].astype(jnp.int32)
            for j in range(q.shape[1] // quarter):
                first = (j * len(qs) // 2 + i // 2) * quarter
                values = q[here * rows : (here + 1) * rows, j * quarter : (j + 1) * quarter].astype(F32) * scale
                ids = lax.broadcasted_iota(jnp.int32, values.shape, 1) + first
                dlogits[at, first : first + quarter] = jnp.where(ids == target, at_target, values).astype(BF16)


def scale_rows(q, packs, quarter):
    values, places = zip(*[part for half in q for part in half])
    shape = (packs.shape[0], 2 * values[0].shape[1])
    return pl.pallas_call(
        functools.partial(dlogits_kernel, places, quarter),
        out_shape=[jax.ShapeDtypeStruct(shape, BF16), jax.ShapeDtypeStruct((8, LANES), F32)],
        compiler_params=params(48),
    )(*values, packs)


def dpre_kernel(n, *refs):
    parts, (packs, pre, h, gain, out) = refs[:n], refs[n:]
    dnormed = parts[0][0]
    for part in parts[1:]:
        dnormed = dnormed + part[0].astype(F32)
    inv, pull = packs[:, 3:4], packs[:, 4:5]
    v = pre[...]
    sigma = 1.0 / (1.0 + jnp.exp(-v))
    act = h[...].astype(F32) + v * sigma
    dact = inv * gain[...] * dnormed - act * pull
    out[...] = (dact * sigma * (1.0 + v * (1.0 - sigma))).astype(BF16)


def grad_pre(parts, packs, pre, h, gain):
    rows, block = pre.shape
    rest = [packs, pre, h, gain]
    return pl.pallas_call(
        functools.partial(dpre_kernel, len(parts)),
        out_shape=jax.ShapeDtypeStruct(pre.shape, BF16),
        grid=(1,),
        in_specs=[pick(t, rows, block) for t in parts] + [whole(r.shape) for r in rest],
        out_specs=whole(pre.shape),
        compiler_params=params(48),
    )(*[t[0] for t in parts], *rest)


def grad_kernel(order, step, me, h, *refs):
    n = len(order)
    ds, (out, placed, mixed, outputs, left) = refs[:n], refs[n:]
    slots = outputs.shape[0]
    lanes = range(0, out.shape[1], LANES)
    for s, d in zip(order, ds):
        placed[me[0] ^ s] = d[...]

    def leave(i):
        target = out.at[pl.ds(i * step * n, step * n), :]
        return pltpu.make_async_copy(outputs.at[i % slots], target, left.at[i % slots])

    steps = h.shape[0] // step
    for i in range(steps):
        if i >= slots:
            leave(i - slots).wait()
        for k in range(n):
            product = jnp.dot(h[i * step : (i + 1) * step, :], placed[k], preferred_element_type=F32)
            for j, lane in enumerate(lanes):
                mixed[j, pl.ds(k, step, stride=n + 1), :] = product[:, lane : lane + LANES]

        def collect(first, group):
            at = pl.multiple_of(first * n, 16)
            for j, lane in enumerate(lanes):
                parts = [
                    mixed[j, pl.ds((first + g) * (n + 1) + p, 8), :]
                    for g in range(group)
                    for p in range(0, n, 8)
                ]
                values = jnp.concatenate(parts, axis=0).astype(BF16)
                outputs[i % slots, pl.ds(at, group * n), lane : lane + LANES] = values

        each_tile(n, step, collect)
        leave(i).start()
    for i in range(max(0, steps - slots), steps):
        leave(i).wait()


def weight_grad(h, ds, me):
    width, rows = h.shape
    n = len(ds)
    block = ds[0].shape[1]
    order = sorted(ds)
    step = min(256, width)
    slots = 3
    return pl.pallas_call(
        functools.partial(grad_kernel, order, step),
        out_shape=jax.ShapeDtypeStruct((width * n, block), BF16),
        grid_spec=pltpu.PrefetchScalarGridSpec(
            num_scalar_prefetch=1,
            grid=(1,),
            in_specs=[whole(h.shape)] + [whole((rows, block))] * n,
            out_specs=pl.BlockSpec(memory_space=pl.ANY),
            scratch_shapes=[
                pltpu.VMEM((n, rows, block), BF16),
                pltpu.VMEM((block // LANES, step * (n + 1), LANES), F32),
                pltpu.VMEM((slots, step * n, block), BF16),
                pltpu.SemaphoreType.DMA((slots,)),
            ],
        ),
        compiler_params=params(48),
        cost_estimate=SHORT,
    )(me, h, *[ds[s] for s in order])


def column(values):
    return jnp.broadcast_to(values[:, None], (values.shape[0], LANES))


def on_device(hidden_rows, head_weight, norm_gain, vocab_embed, targets):
    n_dp, n_mp = lax.axis_size("dp"), lax.axis_size("mp")
    tok_dp, width_mp = hidden_rows.shape
    block = head_weight.shape[3]
    width = width_mp * n_mp
    tokens = tok_dp * n_dp
    vocab_mp = vocab_embed.shape[0]
    dp_bits, mp_bits = bits_of(n_dp), bits_of(n_mp)
    dp_index = lax.axis_index("dp")
    mp_index = lax.axis_index("mp")
    me = mp_index.astype(jnp.int32).reshape(1)
    pairs = list(range(n_mp - 2, -1, -2))

    embed_rows = vocab_embed.reshape(vocab_mp * n_mp, block)
    gain = norm_gain.reshape(1, block)
    quarter = vocab_mp // 4

    orders = [dp_bits, dp_bits[::-1]] * 2
    half = width_mp // 2
    weight_rows = head_weight.reshape(width_mp * n_mp, block)
    weight = relayout(weight_rows, n_mp, 0, half, None, [])
    gathered, hops = zip(
        *[gather_rows(hidden_rows[:, i * half : (i + 1) * half], "dp", orders[i], [weight]) for i in range(2)]
    )
    weight = relayout(weight_rows, n_mp, half, half, weight, hops)
    h = lay(gathered)
    own_h = lax.dynamic_slice_in_dim(h, dp_index * block, block, 1)

    def reduce_product(lhs, w, fillers):
        terms, totals, made = collections.defaultdict(list), {}, None

        def run(group, deps):
            outs = project(lhs, w, me, group, deps)
            for pair, odd, even in zip(group, outs[::2], outs[1::2]):
                terms[pair][:0] = [(even, 0), (swap(odd, "mp", 1), 0)]
            return [outs[1]]

        def leave(s, bit, deps=()):
            totals[s] = add_round(terms[s], deps)
            terms[s ^ bit].append((swap(totals[s], "mp", bit), 0))

        first = pairs[0]
        before = run(pairs[1:2], run([first], []))
        leave(first, mp_bits[1])
        run(pairs[2:], [*before, totals[first]])
        done = 1
        for bit, filler in itertools.zip_longest(mp_bits[1:], fillers):
            for s in sorted(terms, reverse=True):
                if s & bit and not s & done and s not in totals:
                    leave(s, bit, [] if made is None else [made])
            done |= bit
            if filler:
                made = filler(None, list(totals.values()))
        return terms[0], made

    def fill(first, count):
        def run(into, deps):
            return relayout(embed_rows, n_mp, first * quarter, count * quarter, into, deps)

        return run

    parts, embed = reduce_product(h, weight, [None, fill(0, 2)])
    pre, x = activate(parts, own_h, gain, [embed])

    embed = fill(2, 2)(embed, [x])
    xs = gather_xor(x, "mp", mp_bits[::-1], [embed])
    pieces, before = [], []
    for i, order in enumerate(orders):
        pieces.append(project_vocab(xs, i == 0, embed, me, order, i * quarter, quarter, before))
        before = pieces[-1][1:]
    pieces = sum_hops(pieces, "dp", orders)

    local = lax.dynamic_slice_in_dim(targets, dp_index * tok_dp, tok_dp, 0) - mp_index * vocab_mp
    local = column(local)
    *own_q, stats = softmax(pieces, local, quarter, width)
    total = stats
    for bit in mp_bits[:-1]:
        total = merge(merge_kernel, [total, swap(total, "mp", bit)], [])
    q, hops = zip(*[gather_rows(own_q[i], "dp", orders[i], [total]) for i in range(2)])
    finish = functools.partial(finish_kernel, tokens, width)
    packed = merge(finish, [total, swap(total, "mp", mp_bits[-1]), stats, local], hops)
    packs = jnp.concatenate(gather_direct(packed, "dp"), axis=0)
    dlogits, loss = scale_rows(q, packs, quarter)
    parts, _ = reduce_product(dlogits, embed, [None, None])
    dpre = grad_pre(parts, packs, pre, own_h, gain)
    grad = weight_grad(h.T, gather_xor(dpre, "mp", mp_bits[::-1]), me)
    return (grad.reshape(head_weight.shape), loss[0, 0])


def solution(mesh):
    return jax.shard_map(
        on_device,
        mesh=mesh,
        in_specs=(
            P("dp", "mp"),
            P("mp", None, "dp", None),
            P("mp", "dp", None),
            P("mp", None, "dp", None),
            P(),
        ),
        out_specs=(P("mp", None, "dp", None), P()),
        check_vma=False,
    )
```

```python
import collections
import functools
import itertools
import math

import jax
import jax.numpy as jnp
from jax import lax
from jax.experimental import pallas as pl
from jax.experimental.pallas import tpu as pltpu
from jax.sharding import PartitionSpec as P

F32 = jnp.float32
BF16 = jnp.bfloat16
LANES = 128
SHORT = pl.CostEstimate(flops=1, bytes_accessed=1, transcendentals=0)


def params(mib):
    return pltpu.CompilerParams(vmem_limit_bytes=mib * 2**20)


def bits_of(n):
    bits = [1 << i for i in range(n.bit_length() - 1)]
    assert 1 << len(bits) == n
    return bits


def swap(value, axis, bit):
    n = lax.axis_size(axis)
    return lax.ppermute(value, axis, [(i, i ^ bit) for i in range(n)])


def gather_xor(value, axis, bits, deps=()):
    held = {0: value}
    if deps:
        first, second = bits[:2]
        held[second] = swap(value, axis, second)
        held[first] = hold(swap(value, axis, first), [*deps, held[second]])
    for bit in bits:
        for s in list(held):
            if s % (2 * bit) == 0 and s | bit not in held:
                held[s | bit] = swap(held[s], axis, bit)
    return held


def join_kernel(a, b, *refs):
    out = refs[-1]
    out[: a.shape[0]] = a[...]
    out[a.shape[0] :] = b[...]


def join(a, b, deps):
    shape = (2 * a.shape[0], a.shape[1])
    return pl.pallas_call(
        join_kernel,
        out_shape=jax.ShapeDtypeStruct(shape, a.dtype),
        grid=(1,),
        in_specs=[whole(a.shape)] * 2 + after(deps),
        out_specs=whole(shape),
        compiler_params=params(48),
    )(a, b, *deps)


def gather_rows(value, axis, bits, deps):
    places, hops = [0], []
    for bit in bits[:-1]:
        value = join(value, swap(value, axis, bit), [] if hops else deps)
        hops.append(value)
        places = places + [s ^ bit for s in places]
    arrived = swap(value, axis, bits[-1])
    return [(value, places), (arrived, [s ^ bits[-1] for s in places])], hops[0]


def lay_kernel(places, *refs):
    out = refs[-1]
    width = refs[0].shape[1]
    for i, order in enumerate(places):
        rows = refs[i].shape[0] // len(order)
        first = i // 2 * width
        for j, s in enumerate(order):
            out[s * rows : (s + 1) * rows, first : first + width] = refs[i][j * rows : (j + 1) * rows]


def lay(gathered):
    values, places = zip(*[part for half in gathered for part in half])
    shape = (2 * values[0].shape[0], 2 * values[0].shape[1])
    return pl.pallas_call(
        functools.partial(lay_kernel, places),
        out_shape=jax.ShapeDtypeStruct(shape, values[0].dtype),
        grid=(1,),
        in_specs=[whole(v.shape) for v in values],
        out_specs=whole(shape),
        compiler_params=params(48),
    )(*values)


def gather_direct(value, axis):
    return [value] + [swap(value, axis, s) for s in range(1, lax.axis_size(axis))]


def whole(shape):
    return pl.BlockSpec(shape, lambda *_: (0,) * len(shape))


def stream(sources, buffer, sems, use):
    slots = buffer.shape[0]

    def copy(i):
        return pltpu.make_async_copy(sources[i], buffer.at[i % slots], sems.at[i % slots])

    for i in range(min(slots, len(sources))):
        copy(i).start()
    for i in range(len(sources)):
        copy(i).wait()
        use(i, i % slots)
        if i + slots < len(sources):
            copy(i + slots).start()


def after(deps):
    return [pl.BlockSpec(memory_space=pl.ANY)] * len(deps)


def each_tile(n, rows, run):
    group = max(1, 16 // n)

    def body(i, carry):
        run(i * group, group)
        return carry

    lax.fori_loop(0, rows // group, body, 0, unroll=8)


def relayout_kernel(n, start, rows, step, x, *refs):
    out, order, inputs, outputs, arrived, left = refs[-6:]
    size = order.shape[0]
    group = size // n

    to = lax.broadcasted_iota(jnp.int32, order.shape, 0)
    source = lax.broadcasted_iota(jnp.int32, order.shape, 1)
    order[...] = jnp.where(source == to % group * n + to // group, 1.0, 0.0).astype(BF16)
    slots = outputs.shape[0]

    def leave(i):
        target = out.at[:, pl.ds(start + i * step, step), :]
        return pltpu.make_async_copy(outputs.at[i % slots], target, left.at[i % slots])

    def use(i, slot):
        if i >= slots:
            leave(i - slots).wait()
        for part in range(step // group):
            taken = inputs[slot, part * size : (part + 1) * size, :]
            mixed = jnp.dot(order[...], taken, preferred_element_type=F32).astype(BF16)
            for k in range(n):
                at = slice(part * group, (part + 1) * group)
                outputs[i % slots, k, at, :] = mixed[k * group : (k + 1) * group]
        leave(i).start()

    steps = rows // step
    sources = [x.at[pl.ds((start + i * step) * n, step * n), :] for i in range(steps)]
    stream(sources, inputs, arrived, use)
    for i in range(max(0, steps - slots), steps):
        leave(i).wait()


def relayout(flat, n, start, rows, into, deps):
    total, block = flat.shape[0] // n, flat.shape[1]
    step = min(128, rows)
    slots = 4
    skipped = list(deps) if into is None else [into, *deps]
    return pl.pallas_call(
        functools.partial(relayout_kernel, n, start, rows, step),
        out_shape=jax.ShapeDtypeStruct((n, total, block), BF16),
        in_specs=after([flat, *skipped]),
        out_specs=pl.BlockSpec(memory_space=pl.ANY),
        scratch_shapes=[
            pltpu.VMEM((256, 256), BF16),
            pltpu.VMEM((slots, step * n, block), BF16),
            pltpu.VMEM((slots, n, step, block), BF16),
            pltpu.SemaphoreType.DMA((slots,)),
            pltpu.SemaphoreType.DMA((slots,)),
        ],
        input_output_aliases={} if into is None else {1: 0},
        compiler_params=params(48),
        cost_estimate=SHORT,
    )(flat, *skipped)


def hold_kernel(value, *refs):
    refs[-1][...] = value[...]


def hold(value, deps):
    return pl.pallas_call(
        hold_kernel,
        out_shape=jax.ShapeDtypeStruct(value.shape, value.dtype),
        grid=(1,),
        in_specs=[whole(value.shape)] + after(deps),
        out_specs=whole(value.shape),
        compiler_params=params(48),
    )(value, *deps)


def project_kernel(pairs, step, me, lhs, w, *refs):
    total, buffer, sems = refs[-3:]
    outs = refs[-3 - 2 * len(pairs) : -3]
    steps = w.shape[1] // step
    blocks = [me[0] ^ s for pair in pairs for s in (pair + 1, pair)]
    sources = [w.at[k, pl.ds(c * step, step), :] for k in blocks for c in range(steps)]

    def use(i, slot):
        c = i % steps
        part = jnp.dot(lhs[:, c * step : (c + 1) * step], buffer[slot], preferred_element_type=F32)
        if c > 0:
            part = part + total[...]
        if c < steps - 1:
            total[...] = part
        else:
            out = outs[i // steps]
            out[0] = part.astype(out.dtype)

    stream(sources, buffer, sems, use)


def project(lhs, w, me, pairs, deps):
    _, depth, block = w.shape
    rows = lhs.shape[0]
    step = min(1024, depth)
    slots = 4
    out = whole((1, rows, block))
    return pl.pallas_call(
        functools.partial(project_kernel, pairs, step),
        out_shape=[jax.ShapeDtypeStruct((1, rows, block), kind) for _ in pairs for kind in (BF16, F32)],
        grid_spec=pltpu.PrefetchScalarGridSpec(
            num_scalar_prefetch=1,
            grid=(1,),
            in_specs=[whole(lhs.shape)] + after([w, *deps]),
            out_specs=[out] * (2 * len(pairs)),
            scratch_shapes=[
                pltpu.VMEM((rows, block), F32),
                pltpu.VMEM((slots, step, block), BF16),
                pltpu.SemaphoreType.DMA((slots,)),
            ],
        ),
        compiler_params=params(48),
        cost_estimate=SHORT,
    )(me, lhs, w, *deps)


def pick(term, rows, block):
    array, place = term
    return pl.BlockSpec((1, rows, block), lambda *_: (place, 0, 0))


def add_kernel(n, *refs):
    out = refs[-1]
    total = refs[0][0].astype(F32)
    for ref in refs[1:n]:
        total = total + ref[0].astype(F32)
    out[0] = total.astype(out.dtype)


def add_round(terms, deps=()):
    _, rows, block = terms[0][0].shape
    return pl.pallas_call(
        functools.partial(add_kernel, len(terms)),
        out_shape=jax.ShapeDtypeStruct((1, rows, block), BF16),
        grid=(1,),
        in_specs=[pick(t, rows, block) for t in terms] + after(deps),
        out_specs=whole((1, rows, block)),
        compiler_params=params(48),
    )(*[t[0] for t in terms], *deps)


def square_rows(tokens, block):
    return max(1, tokens // block)


def act_kernel(n, *refs):
    parts, (h, gain, pre, x) = refs[:n], refs[-4:]
    total = parts[0][0].astype(F32)
    for part in parts[1:]:
        total = total + part[0].astype(F32)
    pre[...] = total
    act = h[...].astype(F32) + total / (1.0 + jnp.exp(-total))
    tokens, block = act.shape
    x[:tokens] = (act * gain[...]).astype(BF16)

    sums = jnp.broadcast_to(jnp.sum(act * act, axis=1, keepdims=True), (tokens, LANES))
    rest = jnp.transpose(sums)[0:1]
    count = square_rows(tokens, block)
    span = tokens // count
    row = lax.broadcasted_iota(jnp.int32, (16, span), 0)
    extra = jnp.zeros((16, span), F32)
    for term in range(3):
        high = rest.astype(BF16).astype(F32)
        rest = rest - high
        for i in range(count):
            extra = jnp.where(row == term * count + i, high[:, i * span : (i + 1) * span], extra)
    x[tokens:] = jnp.zeros((16, block), BF16)
    x[tokens:, :span] = extra.astype(BF16)


def activate(parts, h, gain, deps=()):
    rows, block = h.shape
    return pl.pallas_call(
        functools.partial(act_kernel, len(parts)),
        out_shape=[
            jax.ShapeDtypeStruct((rows, block), F32),
            jax.ShapeDtypeStruct((rows + 16, block), BF16),
        ],
        grid=(1,),
        in_specs=[pick(t, rows, block) for t in parts] + after(deps) + [whole(h.shape), whole(gain.shape)],
        out_specs=[whole((rows, block)), whole((rows + 16, block))],
        compiler_params=params(48),
    )(*[t[0] for t in parts], *deps, h, gain)


def hop_order(bits):
    places = [0]
    for bit in bits[::-1]:
        places = places + [s | bit for s in places]
    return places


def power(exponent):
    return jnp.exp(exponent * math.log(2.0))


def exponent_of(values):
    return jnp.ceil(jnp.log(jnp.maximum(values, 1e-30)) * (1.0 / math.log(2.0)))


def integers(values):
    values = jnp.clip(jnp.floor(values), -32768.0, 32767.0)
    return values.astype(jnp.int32).astype(jnp.int16)


def encode(values, squares):
    exponent = exponent_of(jnp.max(jnp.abs(values), axis=1, keepdims=True))
    own = exponent_of(squares)
    scaled = squares * power(15.0 - own)
    high = jnp.minimum(jnp.floor(scaled), 32767.0)
    extra = [exponent, own, high, (scaled - high) * 32768.0]
    return integers(values * power(15.0 - exponent) + 0.5), integers(
        lanes_of(extra, (values.shape[0], LANES))
    )


def decode(ref, rows, size):
    values = ref[rows, :size].astype(jnp.int32).astype(F32)
    extra = ref[rows, size:].astype(jnp.int32).astype(F32)
    squares = (extra[:, 2:3] + extra[:, 3:4] / 32768.0) * power(extra[:, 1:2] - 15.0)
    return values * power(extra[:, 0:1] - 15.0), squares


def piece_sum(refs, rows, size):
    values, squares = refs[0][rows, :size], refs[0][rows, size : size + 1]
    for ref in refs[1:]:
        more = decode(ref, rows, size)
        values, squares = values + more[0], squares + more[1]
    return values, squares


def logits_kernel(order, places, start, me, *refs):
    n = len(order)
    xs, e, (sent, kept, total, buffer, sems) = refs[:n], refs[n], refs[-5:]
    tokens, block = xs[0].shape[0] - 16, xs[0].shape[1]
    rows = tokens // len(places)
    size = kept.shape[1] - LANES

    extra = functools.reduce(jnp.add, [x[tokens:].astype(F32) for x in xs])
    count = square_rows(tokens, block)
    span = tokens // count
    columns = []
    for i in range(count):
        terms = [extra[t * count + i : t * count + i + 1, :span] for t in range(3)]
        columns.append(jnp.transpose(jnp.broadcast_to(functools.reduce(jnp.add, terms), (LANES, span))))
    squares = jnp.concatenate(columns, axis=0) if count > 1 else columns[0]

    def use(i, slot):
        part = lax.dot_general(
            xs[i][:tokens], buffer[slot], (((1,), (1,)), ((), ())), preferred_element_type=F32
        )
        if i > 0:
            part = part + total[...]
        if i < n - 1:
            total[...] = part
            return
        for j, s in enumerate(places):
            here = slice(s * rows, (s + 1) * rows)
            first = j % (len(places) // 2) * rows
            to = slice(first, first + rows)
            if j < len(places) // 2:
                kept[to, :size], kept[to, size:] = part[here], squares[here]
            else:
                sent[to, :size], sent[to, size:] = encode(part[here], squares[here, 0:1])

    stream([e.at[me[0] ^ s, pl.ds(start, size), :] for s in order], buffer, sems, use)


def project_vocab(xs, embed, me, bits, start, size, deps):
    n, _, block = embed.shape
    order = sorted(xs)
    rows = xs[0].shape[0] - 16
    slots = 4
    shape = (rows // 2, size + LANES)
    return pl.pallas_call(
        functools.partial(logits_kernel, order, hop_order(bits), start),
        out_shape=[jax.ShapeDtypeStruct(shape, kind) for kind in (jnp.int16, F32)],
        grid_spec=pltpu.PrefetchScalarGridSpec(
            num_scalar_prefetch=1,
            grid=(1,),
            in_specs=[whole((rows + 16, block))] * n + after([embed, *deps]),
            out_specs=[whole(shape)] * 2,
            scratch_shapes=[
                pltpu.VMEM((rows, size), F32),
                pltpu.VMEM((slots, size, block), BF16),
                pltpu.SemaphoreType.DMA((slots,)),
            ],
        ),
        compiler_params=params(48),
        cost_estimate=SHORT,
    )(me, *[xs[s] for s in order], embed, *deps)


def hop_kernel(n, *refs):
    out = refs[-1]
    size = out.shape[1] - LANES
    out[:, :size], out[:, size:] = encode(*piece_sum(refs[:n], slice(None), size))


def hop_sum(terms, rows, deps):
    size = terms[0].shape[1]
    return pl.pallas_call(
        functools.partial(hop_kernel, len(terms)),
        out_shape=jax.ShapeDtypeStruct((rows, size), jnp.int16),
        grid=(1,),
        in_specs=[pl.BlockSpec((rows, size), lambda i: (1, 0))] * len(terms) + after(deps),
        out_specs=whole((rows, size)),
        compiler_params=params(48),
    )(*terms, *deps)


def sum_hops(terms, axis, orders):
    rows, before = terms[0][0].shape[0], []
    for hop in range(1, len(orders[0])):
        rows //= 2
        for i, held in enumerate(terms):
            if i == len(terms) - 1:
                before = before + [t[-1] for t in terms[:2]]
            before = [hop_sum(held, rows, before)]
            held.append(swap(before[0], axis, orders[i][hop]))
    return terms


def softmax_kernel(counts, size, width, *refs):
    parts, (targets, *refs) = refs[: sum(counts)], refs[sum(counts) :]
    qs, stats = refs[:-1], refs[-1]
    target = targets[:, 0:1]
    pieces, hits, at = [], [], 0
    for i, count in enumerate(counts):
        total, squares = piece_sum(parts[at : at + count], slice(None), size)
        at += count
        if i == 0:
            inv = lax.rsqrt(squares / width + 1e-05)
        ids = lax.broadcasted_iota(jnp.int32, total.shape, 1) + i * size
        pieces.append(total * inv)
        hits.append(ids == target)
    top = functools.reduce(jnp.maximum, [jnp.max(p, axis=1, keepdims=True) for p in pieces])
    mass, moment, picked = 0.0, 0.0, 0.0
    for i, (piece, hit) in enumerate(zip(pieces, hits)):
        shifted = piece - top
        e = jnp.exp(shifted)
        mass = mass + jnp.sum(e, axis=1, keepdims=True)
        moment = moment + jnp.sum(e * shifted, axis=1, keepdims=True)
        picked = picked + jnp.sum(jnp.where(hit, piece, 0.0), axis=1, keepdims=True)
        first = i // len(qs) * size
        qs[i % len(qs)][:, first : first + size] = e.astype(BF16)
    stats[...] = lanes_of([top, mass, moment, picked, inv], stats.shape)


def softmax(pieces, targets, size, width):
    counts = [len(p) for p in pieces]
    flat = [part for p in pieces for part in p]
    rows = targets.shape[0]
    return pl.pallas_call(
        functools.partial(softmax_kernel, counts, size, width),
        out_shape=[jax.ShapeDtypeStruct((rows, len(pieces) // 2 * size), BF16)] * 2
        + [jax.ShapeDtypeStruct((rows, LANES), F32)],
        grid=(1,),
        in_specs=[whole((rows, part.shape[1])) for part in flat] + [whole(targets.shape)],
        out_specs=[whole((rows, len(pieces) // 2 * size))] * 2 + [whole((rows, LANES))],
        compiler_params=params(48),
    )(*flat, targets)


def tree(op, values):
    while len(values) > 1:
        half = len(values) // 2
        values = [op(a, b) for a, b in zip(values[:half], values[half:])]
    return values[0]


def lanes_of(values, shape):
    lane = lax.broadcasted_iota(jnp.int32, shape, 1)
    out = jnp.zeros(shape, F32)
    for i, value in enumerate(values):
        out = jnp.where(lane == i, value, out)
    return out


def merge_two(a, b):
    top = jnp.maximum(a[:, 0:1], b[:, 0:1])
    mass, moment = 0.0, 0.0
    for part in (a, b):
        shift = part[:, 0:1] - top
        weight = jnp.exp(shift)
        mass = mass + weight * part[:, 1:2]
        moment = moment + weight * (part[:, 2:3] + part[:, 1:2] * shift)
    return top, mass, moment, a[:, 3:4] + b[:, 3:4]


def merge_kernel(a, b, *refs):
    refs[-1][...] = lanes_of(merge_two(a[...], b[...]), refs[-1].shape)


def finish_kernel(tokens, width, a, b, own, targets, *refs):
    top, mass, moment, picked = merge_two(a[...], b[...])
    lse = top + jnp.log(mass)
    inv = own[:, 4:5]
    scale = jnp.exp(own[:, 0:1] - lse) / tokens
    at_target = (jnp.exp(picked - lse) - 1.0) / tokens
    pull = (moment / mass + (top - picked)) * (inv * inv) / (tokens * width)
    values = [scale, at_target, targets[:, 0:1].astype(F32), inv, pull, lse - picked]
    refs[-1][...] = lanes_of(values, refs[-1].shape)


def merge(body, values, deps):
    shape = values[0].shape
    return pl.pallas_call(
        body,
        out_shape=jax.ShapeDtypeStruct(shape, F32),
        grid=(1,),
        in_specs=[whole(shape)] * len(values) + after(deps),
        out_specs=whole(shape),
        compiler_params=params(48),
    )(*values, *deps)


def dlogits_kernel(places, quarter, *refs):
    qs, (packs, dlogits, loss) = refs[:-3], refs[-3:]
    n = 2 * len(places[0])
    rows = packs.shape[0] // n
    sums = [jnp.sum(packs[s * rows : (s + 1) * rows, 5:6], axis=0, keepdims=True) for s in range(n)]
    loss[...] = jnp.broadcast_to(tree(jnp.add, sums) / packs.shape[0], loss.shape)
    for i, (q, order) in enumerate(zip(qs, places)):
        for here, s in enumerate(order):
            at = slice(s * rows, (s + 1) * rows)
            scale, at_target, target = packs[at, 0:1], packs[at, 1:2], packs[at, 2:3].astype(jnp.int32)
            for j in range(q.shape[1] // quarter):
                first = (j * len(qs) // 2 + i // 2) * quarter
                values = q[here * rows : (here + 1) * rows, j * quarter : (j + 1) * quarter].astype(F32) * scale
                ids = lax.broadcasted_iota(jnp.int32, values.shape, 1) + first
                dlogits[at, first : first + quarter] = jnp.where(ids == target, at_target, values).astype(BF16)


def scale_rows(q, packs, quarter):
    values, places = zip(*[part for half in q for part in half])
    shape = (packs.shape[0], 2 * values[0].shape[1])
    return pl.pallas_call(
        functools.partial(dlogits_kernel, places, quarter),
        out_shape=[jax.ShapeDtypeStruct(shape, BF16), jax.ShapeDtypeStruct((8, LANES), F32)],
        compiler_params=params(48),
    )(*values, packs)


def dpre_kernel(n, *refs):
    parts, (packs, pre, h, gain, out) = refs[:n], refs[n:]
    dnormed = parts[0][0]
    for part in parts[1:]:
        dnormed = dnormed + part[0].astype(F32)
    inv, pull = packs[:, 3:4], packs[:, 4:5]
    v = pre[...]
    sigma = 1.0 / (1.0 + jnp.exp(-v))
    act = h[...].astype(F32) + v * sigma
    dact = inv * gain[...] * dnormed - act * pull
    out[...] = (dact * sigma * (1.0 + v * (1.0 - sigma))).astype(BF16)


def grad_pre(parts, packs, pre, h, gain):
    rows, block = pre.shape
    rest = [packs, pre, h, gain]
    return pl.pallas_call(
        functools.partial(dpre_kernel, len(parts)),
        out_shape=jax.ShapeDtypeStruct(pre.shape, BF16),
        grid=(1,),
        in_specs=[pick(t, rows, block) for t in parts] + [whole(r.shape) for r in rest],
        out_specs=whole(pre.shape),
        compiler_params=params(48),
    )(*[t[0] for t in parts], *rest)


def grad_kernel(order, step, me, h, *refs):
    n = len(order)
    ds, (out, placed, mixed, outputs, left) = refs[:n], refs[n:]
    slots = outputs.shape[0]
    lanes = range(0, out.shape[1], LANES)
    for s, d in zip(order, ds):
        placed[me[0] ^ s] = d[...]

    def leave(i):
        target = out.at[pl.ds(i * step * n, step * n), :]
        return pltpu.make_async_copy(outputs.at[i % slots], target, left.at[i % slots])

    steps = h.shape[0] // step
    for i in range(steps):
        if i >= slots:
            leave(i - slots).wait()
        for k in range(n):
            product = jnp.dot(h[i * step : (i + 1) * step, :], placed[k], preferred_element_type=F32)
            for j, lane in enumerate(lanes):
                mixed[j, pl.ds(k, step, stride=n + 1), :] = product[:, lane : lane + LANES]

        def collect(first, group):
            at = pl.multiple_of(first * n, 16)
            for j, lane in enumerate(lanes):
                parts = [
                    mixed[j, pl.ds((first + g) * (n + 1) + p, 8), :]
                    for g in range(group)
                    for p in range(0, n, 8)
                ]
                values = jnp.concatenate(parts, axis=0).astype(BF16)
                outputs[i % slots, pl.ds(at, group * n), lane : lane + LANES] = values

        each_tile(n, step, collect)
        leave(i).start()
    for i in range(max(0, steps - slots), steps):
        leave(i).wait()


def weight_grad(h, ds, me):
    width, rows = h.shape
    n = len(ds)
    block = ds[0].shape[1]
    order = sorted(ds)
    step = min(256, width)
    slots = 3
    return pl.pallas_call(
        functools.partial(grad_kernel, order, step),
        out_shape=jax.ShapeDtypeStruct((width * n, block), BF16),
        grid_spec=pltpu.PrefetchScalarGridSpec(
            num_scalar_prefetch=1,
            grid=(1,),
            in_specs=[whole(h.shape)] + [whole((rows, block))] * n,
            out_specs=pl.BlockSpec(memory_space=pl.ANY),
            scratch_shapes=[
                pltpu.VMEM((n, rows, block), BF16),
                pltpu.VMEM((block // LANES, step * (n + 1), LANES), F32),
                pltpu.VMEM((slots, step * n, block), BF16),
                pltpu.SemaphoreType.DMA((slots,)),
            ],
        ),
        compiler_params=params(48),
        cost_estimate=SHORT,
    )(me, h, *[ds[s] for s in order])


def column(values):
    return jnp.broadcast_to(values[:, None], (values.shape[0], LANES))


def on_device(hidden_rows, head_weight, norm_gain, vocab_embed, targets):
    n_dp, n_mp = lax.axis_size("dp"), lax.axis_size("mp")
    tok_dp, width_mp = hidden_rows.shape
    block = head_weight.shape[3]
    width = width_mp * n_mp
    tokens = tok_dp * n_dp
    vocab_mp = vocab_embed.shape[0]
    dp_bits, mp_bits = bits_of(n_dp), bits_of(n_mp)
    dp_index = lax.axis_index("dp")
    mp_index = lax.axis_index("mp")
    me = mp_index.astype(jnp.int32).reshape(1)
    pairs = list(range(n_mp - 2, -1, -2))

    embed_rows = vocab_embed.reshape(vocab_mp * n_mp, block)
    gain = norm_gain.reshape(1, block)
    quarter = vocab_mp // 4

    orders = [dp_bits, dp_bits[::-1]] * 2
    half = width_mp // 2
    weight_rows = head_weight.reshape(width_mp * n_mp, block)
    weight = relayout(weight_rows, n_mp, 0, half, None, [])
    gathered, hops = zip(
        *[gather_rows(hidden_rows[:, i * half : (i + 1) * half], "dp", orders[i], [weight]) for i in range(2)]
    )
    weight = relayout(weight_rows, n_mp, half, half, weight, hops)
    h = lay(gathered)
    own_h = lax.dynamic_slice_in_dim(h, dp_index * block, block, 1)

    def reduce_product(lhs, w, fillers):
        terms, totals, made = collections.defaultdict(list), {}, None

        def run(group, deps):
            outs = project(lhs, w, me, group, deps)
            for pair, odd, even in zip(group, outs[::2], outs[1::2]):
                terms[pair][:0] = [(even, 0), (swap(odd, "mp", 1), 0)]
            return [outs[1]]

        def leave(s, bit, deps=()):
            totals[s] = add_round(terms[s], deps)
            terms[s ^ bit].append((swap(totals[s], "mp", bit), 0))

        first = pairs[0]
        before = run(pairs[1:2], run([first], []))
        leave(first, mp_bits[1])
        run(pairs[2:], [*before, totals[first]])
        done = 1
        for bit, filler in itertools.zip_longest(mp_bits[1:], fillers):
            for s in sorted(terms, reverse=True):
                if s & bit and not s & done and s not in totals:
                    leave(s, bit, [] if made is None else [made])
            done |= bit
            if filler:
                made = filler(None, list(totals.values()))
        return terms[0], made

    def fill(first, count):
        def run(into, deps):
            return relayout(embed_rows, n_mp, first * quarter, count * quarter, into, deps)

        return run

    parts, embed = reduce_product(h, weight, [None, fill(0, 2)])
    pre, x = activate(parts, own_h, gain, [embed])

    embed = fill(2, 2)(embed, [x])
    xs = gather_xor(x, "mp", mp_bits[::-1], [embed])
    pieces, before = [], []
    for i, order in enumerate(orders):
        late = [pieces[0][1]] if i == 3 else []
        sent, kept = project_vocab(xs, embed, me, order, i * quarter, quarter, before + late)
        pieces.append([kept, swap(sent, "dp", order[0])])
        before = [kept]
    pieces = sum_hops(pieces, "dp", orders)

    local = lax.dynamic_slice_in_dim(targets, dp_index * tok_dp, tok_dp, 0) - mp_index * vocab_mp
    local = column(local)
    *own_q, stats = softmax(pieces, local, quarter, width)
    total = stats
    for bit in mp_bits[:-1]:
        total = merge(merge_kernel, [total, swap(total, "mp", bit)], [])
    q, hops = zip(*[gather_rows(own_q[i], "dp", orders[i], [total]) for i in range(2)])
    finish = functools.partial(finish_kernel, tokens, width)
    packed = merge(finish, [total, swap(total, "mp", mp_bits[-1]), stats, local], hops)
    packs = jnp.concatenate(gather_direct(packed, "dp"), axis=0)
    dlogits, loss = scale_rows(q, packs, quarter)
    parts, _ = reduce_product(dlogits, embed, [None, None])
    dpre = grad_pre(parts, packs, pre, own_h, gain)
    grad = weight_grad(h.T, gather_xor(dpre, "mp", mp_bits[::-1]), me)
    return (grad.reshape(head_weight.shape), loss[0, 0])


def solution(mesh):
    return jax.shard_map(
        on_device,
        mesh=mesh,
        in_specs=(
            P("dp", "mp"),
            P("mp", None, "dp", None),
            P("mp", "dp", None),
            P("mp", None, "dp", None),
            P(),
        ),
        out_specs=(P("mp", None, "dp", None), P()),
        check_vma=False,
    )
```

```python
import collections
import functools
import itertools
import math

import jax
import jax.numpy as jnp
from jax import lax
from jax.experimental import pallas as pl
from jax.experimental.pallas import tpu as pltpu
from jax.sharding import PartitionSpec as P

F32 = jnp.float32
BF16 = jnp.bfloat16
LANES = 128
SHORT = pl.CostEstimate(flops=1, bytes_accessed=1, transcendentals=0)


def params(mib):
    return pltpu.CompilerParams(vmem_limit_bytes=mib * 2**20)


def bits_of(n):
    bits = [1 << i for i in range(n.bit_length() - 1)]
    assert 1 << len(bits) == n
    return bits


def swap(value, axis, bit):
    n = lax.axis_size(axis)
    return lax.ppermute(value, axis, [(i, i ^ bit) for i in range(n)])


def gather_xor(value, axis, bits, deps=()):
    held = {0: value}
    if deps:
        first, second = bits[:2]
        held[second] = swap(value, axis, second)
        held[first] = hold(swap(value, axis, first), [*deps, held[second]])
    for bit in bits:
        for s in list(held):
            if s % (2 * bit) == 0 and s | bit not in held:
                held[s | bit] = swap(held[s], axis, bit)
    return held


def join_kernel(a, b, *refs):
    out = refs[-1]
    out[: a.shape[0]] = a[...]
    out[a.shape[0] :] = b[...]


def join(a, b, deps):
    shape = (2 * a.shape[0], a.shape[1])
    return pl.pallas_call(
        join_kernel,
        out_shape=jax.ShapeDtypeStruct(shape, a.dtype),
        grid=(1,),
        in_specs=[whole(a.shape)] * 2 + after(deps),
        out_specs=whole(shape),
        compiler_params=params(16),
    )(a, b, *deps)


def gather_rows(value, axis, bits, deps):
    places, hops = [0], []
    for bit in bits[:-1]:
        value = join(value, swap(value, axis, bit), [] if hops else deps)
        hops.append(value)
        places = places + [s ^ bit for s in places]
    arrived = swap(value, axis, bits[-1])
    return [(value, places), (arrived, [s ^ bits[-1] for s in places])], hops[0]


def lay_kernel(places, *refs):
    out = refs[-1]
    width = refs[0].shape[1]
    for i, order in enumerate(places):
        rows = refs[i].shape[0] // len(order)
        first = i // 2 * width
        for j, s in enumerate(order):
            out[s * rows : (s + 1) * rows, first : first + width] = refs[i][j * rows : (j + 1) * rows]


def lay(gathered):
    values, places = zip(*[part for half in gathered for part in half])
    shape = (2 * values[0].shape[0], 2 * values[0].shape[1])
    return pl.pallas_call(
        functools.partial(lay_kernel, places),
        out_shape=jax.ShapeDtypeStruct(shape, values[0].dtype),
        grid=(1,),
        in_specs=[whole(v.shape) for v in values],
        out_specs=whole(shape),
        compiler_params=params(16),
    )(*values)


def gather_direct(value, axis):
    return [value] + [swap(value, axis, s) for s in range(1, lax.axis_size(axis))]


def whole(shape):
    return pl.BlockSpec(shape, lambda *_: (0,) * len(shape))


def stream(sources, buffer, sems, use):
    slots = buffer.shape[0]

    def copy(i):
        return pltpu.make_async_copy(sources[i], buffer.at[i % slots], sems.at[i % slots])

    for i in range(min(slots, len(sources))):
        copy(i).start()
    for i in range(len(sources)):
        copy(i).wait()
        use(i, i % slots)
        if i + slots < len(sources):
            copy(i + slots).start()


def after(deps):
    return [pl.BlockSpec(memory_space=pl.ANY)] * len(deps)


def each_tile(n, rows, run):
    group = max(1, 16 // n)

    def body(i, carry):
        run(i * group, group)
        return carry

    lax.fori_loop(0, rows // group, body, 0, unroll=8)


def relayout_kernel(n, start, rows, step, x, *refs):
    out, token, order, inputs, outputs, arrived, left = refs[-7:]
    token[...] = jnp.zeros(token.shape, F32)
    size = order.shape[0]
    group = size // n

    to = lax.broadcasted_iota(jnp.int32, order.shape, 0)
    source = lax.broadcasted_iota(jnp.int32, order.shape, 1)
    order[...] = jnp.where(source == to % group * n + to // group, 1.0, 0.0).astype(BF16)
    slots = outputs.shape[0]

    def leave(i):
        target = out.at[:, pl.ds(start + i * step, step), :]
        return pltpu.make_async_copy(outputs.at[i % slots], target, left.at[i % slots])

    def use(i, slot):
        if i >= slots:
            leave(i - slots).wait()
        for part in range(step // group):
            taken = inputs[slot, part * size : (part + 1) * size, :]
            mixed = jnp.dot(order[...], taken, preferred_element_type=F32).astype(BF16)
            for k in range(n):
                at = slice(part * group, (part + 1) * group)
                outputs[i % slots, k, at, :] = mixed[k * group : (k + 1) * group]
        leave(i).start()

    steps = rows // step
    sources = [x.at[pl.ds((start + i * step) * n, step * n), :] for i in range(steps)]
    stream(sources, inputs, arrived, use)
    for i in range(max(0, steps - slots), steps):
        leave(i).wait()


def relayout(flat, n, start, rows, into, deps):
    total, block = flat.shape[0] // n, flat.shape[1]
    step = min(128, rows)
    slots = 4
    skipped = list(deps) if into is None else [into, *deps]
    return pl.pallas_call(
        functools.partial(relayout_kernel, n, start, rows, step),
        out_shape=[jax.ShapeDtypeStruct((n, total, block), BF16), jax.ShapeDtypeStruct((8, LANES), F32)],
        in_specs=after([flat, *skipped]),
        out_specs=[pl.BlockSpec(memory_space=pl.ANY), pl.BlockSpec(memory_space=pltpu.VMEM)],
        scratch_shapes=[
            pltpu.VMEM((256, 256), BF16),
            pltpu.VMEM((slots, step * n, block), BF16),
            pltpu.VMEM((slots, n, step, block), BF16),
            pltpu.SemaphoreType.DMA((slots,)),
            pltpu.SemaphoreType.DMA((slots,)),
        ],
        input_output_aliases={} if into is None else {1: 0},
        compiler_params=params(48),
        cost_estimate=SHORT,
    )(flat, *skipped)


def hold_kernel(value, *refs):
    refs[-1][...] = value[...]


def hold(value, deps):
    return pl.pallas_call(
        hold_kernel,
        out_shape=jax.ShapeDtypeStruct(value.shape, value.dtype),
        grid=(1,),
        in_specs=[whole(value.shape)] + after(deps),
        out_specs=whole(value.shape),
        compiler_params=params(16),
    )(value, *deps)


def project_kernel(pairs, step, me, lhs, w, *refs):
    total, buffer, sems = refs[-3:]
    outs = refs[-3 - 2 * len(pairs) : -3]
    steps = w.shape[1] // step
    blocks = [me[0] ^ s for pair in pairs for s in (pair + 1, pair)]
    sources = [w.at[k, pl.ds(c * step, step), :] for k in blocks for c in range(steps)]

    def use(i, slot):
        c = i % steps
        part = jnp.dot(lhs[:, c * step : (c + 1) * step], buffer[slot], preferred_element_type=F32)
        if c > 0:
            part = part + total[...]
        if c < steps - 1:
            total[...] = part
        else:
            out = outs[i // steps]
            out[0] = part.astype(out.dtype)

    stream(sources, buffer, sems, use)


def project(lhs, w, me, pairs, deps):
    _, depth, block = w.shape
    rows = lhs.shape[0]
    step = min(1024, depth)
    slots = 4
    out = whole((1, rows, block))
    return pl.pallas_call(
        functools.partial(project_kernel, pairs, step),
        out_shape=[jax.ShapeDtypeStruct((1, rows, block), kind) for _ in pairs for kind in (BF16, F32)],
        grid_spec=pltpu.PrefetchScalarGridSpec(
            num_scalar_prefetch=1,
            grid=(1,),
            in_specs=[whole(lhs.shape)] + after([w, *deps]),
            out_specs=[out] * (2 * len(pairs)),
            scratch_shapes=[
                pltpu.VMEM((rows, block), F32),
                pltpu.VMEM((slots, step, block), BF16),
                pltpu.SemaphoreType.DMA((slots,)),
            ],
        ),
        compiler_params=params(48),
        cost_estimate=SHORT,
    )(me, lhs, w, *deps)


def pick(term, rows, block):
    array, place = term
    return pl.BlockSpec((1, rows, block), lambda *_: (place, 0, 0))


def add_kernel(n, *refs):
    out = refs[-1]
    total = refs[0][0].astype(F32)
    for ref in refs[1:n]:
        total = total + ref[0].astype(F32)
    out[0] = total.astype(out.dtype)


def add_round(terms, deps=()):
    _, rows, block = terms[0][0].shape
    return pl.pallas_call(
        functools.partial(add_kernel, len(terms)),
        out_shape=jax.ShapeDtypeStruct((1, rows, block), BF16),
        grid=(1,),
        in_specs=[pick(t, rows, block) for t in terms] + after(deps),
        out_specs=whole((1, rows, block)),
        compiler_params=params(16),
    )(*[t[0] for t in terms], *deps)


def square_rows(tokens, block):
    return max(1, tokens // block)


def act_kernel(n, *refs):
    parts, (h, gain, pre, x) = refs[:n], refs[-4:]
    total = parts[0][0].astype(F32)
    for part in parts[1:]:
        total = total + part[0].astype(F32)
    pre[...] = total
    act = h[...].astype(F32) + total / (1.0 + jnp.exp(-total))
    tokens, block = act.shape
    x[:tokens] = (act * gain[...]).astype(BF16)

    sums = jnp.broadcast_to(jnp.sum(act * act, axis=1, keepdims=True), (tokens, LANES))
    rest = jnp.transpose(sums)[0:1]
    count = square_rows(tokens, block)
    span = tokens // count
    row = lax.broadcasted_iota(jnp.int32, (16, span), 0)
    extra = jnp.zeros((16, span), F32)
    for term in range(3):
        high = rest.astype(BF16).astype(F32)
        rest = rest - high
        for i in range(count):
            extra = jnp.where(row == term * count + i, high[:, i * span : (i + 1) * span], extra)
    x[tokens:] = jnp.zeros((16, block), BF16)
    x[tokens:, :span] = extra.astype(BF16)


def activate(parts, h, gain, deps=()):
    rows, block = h.shape
    return pl.pallas_call(
        functools.partial(act_kernel, len(parts)),
        out_shape=[
            jax.ShapeDtypeStruct((rows, block), F32),
            jax.ShapeDtypeStruct((rows + 16, block), BF16),
        ],
        grid=(1,),
        in_specs=[pick(t, rows, block) for t in parts] + after(deps) + [whole(h.shape), whole(gain.shape)],
        out_specs=[whole((rows, block)), whole((rows + 16, block))],
        compiler_params=params(16),
    )(*[t[0] for t in parts], *deps, h, gain)


def hop_order(bits):
    places = [0]
    for bit in bits[::-1]:
        places = places + [s | bit for s in places]
    return places


def power(exponent):
    return jnp.exp(exponent * math.log(2.0))


def exponent_of(values):
    return jnp.ceil(jnp.log(jnp.maximum(values, 1e-30)) * (1.0 / math.log(2.0)))


def integers(values):
    values = jnp.clip(jnp.floor(values), -32768.0, 32767.0)
    return values.astype(jnp.int32).astype(jnp.int16)


def encode(values, squares):
    exponent = exponent_of(jnp.max(jnp.abs(values), axis=1, keepdims=True))
    own = exponent_of(squares)
    scaled = squares * power(15.0 - own)
    high = jnp.minimum(jnp.floor(scaled), 32767.0)
    extra = [exponent, own, high, (scaled - high) * 32768.0]
    return integers(values * power(15.0 - exponent) + 0.5), integers(
        lanes_of(extra, (values.shape[0], LANES))
    )


def decode(ref, rows, size):
    values = ref[rows, :size].astype(jnp.int32).astype(F32)
    extra = ref[rows, size:].astype(jnp.int32).astype(F32)
    squares = (extra[:, 2:3] + extra[:, 3:4] / 32768.0) * power(extra[:, 1:2] - 15.0)
    return values * power(extra[:, 0:1] - 15.0), squares


def piece_sum(refs, rows, size):
    values, squares = refs[0][rows, :size], refs[0][rows, size : size + 1]
    for ref in refs[1:]:
        more = decode(ref, rows, size)
        values, squares = values + more[0], squares + more[1]
    return values, squares


def logits_kernel(order, places, start, me, *refs):
    n = len(order)
    xs, e, (sent, kept, total, buffer, sems) = refs[:n], refs[n], refs[-5:]
    tokens, block = xs[0].shape[0] - 16, xs[0].shape[1]
    rows = tokens // len(places)
    size = kept.shape[1] - LANES

    extra = functools.reduce(jnp.add, [x[tokens:].astype(F32) for x in xs])
    count = square_rows(tokens, block)
    span = tokens // count
    columns = []
    for i in range(count):
        terms = [extra[t * count + i : t * count + i + 1, :span] for t in range(3)]
        columns.append(jnp.transpose(jnp.broadcast_to(functools.reduce(jnp.add, terms), (LANES, span))))
    squares = jnp.concatenate(columns, axis=0) if count > 1 else columns[0]

    def use(i, slot):
        part = lax.dot_general(
            xs[i][:tokens], buffer[slot], (((1,), (1,)), ((), ())), preferred_element_type=F32
        )
        if i > 0:
            part = part + total[...]
        if i < n - 1:
            total[...] = part
            return
        for j, s in enumerate(places):
            here = slice(s * rows, (s + 1) * rows)
            first = j % (len(places) // 2) * rows
            to = slice(first, first + rows)
            if j < len(places) // 2:
                kept[to, :size], kept[to, size:] = part[here], squares[here]
            else:
                sent[to, :size], sent[to, size:] = encode(part[here], squares[here, 0:1])

    stream([e.at[me[0] ^ s, pl.ds(start, size), :] for s in order], buffer, sems, use)


def project_vocab(xs, embed, me, bits, start, size, deps):
    n, _, block = embed.shape
    order = sorted(xs)
    rows = xs[0].shape[0] - 16
    slots = 4
    shape = (rows // 2, size + LANES)
    return pl.pallas_call(
        functools.partial(logits_kernel, order, hop_order(bits), start),
        out_shape=[jax.ShapeDtypeStruct(shape, kind) for kind in (jnp.int16, F32)],
        grid_spec=pltpu.PrefetchScalarGridSpec(
            num_scalar_prefetch=1,
            grid=(1,),
            in_specs=[whole((rows + 16, block))] * n + after([embed, *deps]),
            out_specs=[whole(shape)] * 2,
            scratch_shapes=[
                pltpu.VMEM((rows, size), F32),
                pltpu.VMEM((slots, size, block), BF16),
                pltpu.SemaphoreType.DMA((slots,)),
            ],
        ),
        compiler_params=params(48),
        cost_estimate=SHORT,
    )(me, *[xs[s] for s in order], embed, *deps)


def hop_kernel(n, *refs):
    out = refs[-1]
    size = out.shape[1] - LANES
    out[:, :size], out[:, size:] = encode(*piece_sum(refs[:n], slice(None), size))


def hop_sum(terms, rows, deps):
    size = terms[0].shape[1]
    return pl.pallas_call(
        functools.partial(hop_kernel, len(terms)),
        out_shape=jax.ShapeDtypeStruct((rows, size), jnp.int16),
        grid=(1,),
        in_specs=[pl.BlockSpec((rows, size), lambda i: (1, 0))] * len(terms) + after(deps),
        out_specs=whole((rows, size)),
        compiler_params=params(16),
    )(*terms, *deps)


def sum_hops(terms, axis, orders):
    rows, before = terms[0][0].shape[0], []
    for hop in range(1, len(orders[0])):
        rows //= 2
        for i, held in enumerate(terms):
            if i >= len(terms) - 2:
                before = before + [terms[i - 2][-1]]
            before = [hop_sum(held, rows, before)]
            held.append(swap(before[0], axis, orders[i][hop]))
    return terms


def softmax_kernel(counts, size, width, *refs):
    parts, (targets, *refs) = refs[: sum(counts)], refs[sum(counts) :]
    qs, stats = refs[:-1], refs[-1]
    target = targets[:, 0:1]
    pieces, hits, at = [], [], 0
    for i, count in enumerate(counts):
        total, squares = piece_sum(parts[at : at + count], slice(None), size)
        at += count
        if i == 0:
            inv = lax.rsqrt(squares / width + 1e-05)
        ids = lax.broadcasted_iota(jnp.int32, total.shape, 1) + i * size
        pieces.append(total * inv)
        hits.append(ids == target)
    top = functools.reduce(jnp.maximum, [jnp.max(p, axis=1, keepdims=True) for p in pieces])
    mass, moment, picked = 0.0, 0.0, 0.0
    for i, (piece, hit) in enumerate(zip(pieces, hits)):
        shifted = piece - top
        e = jnp.exp(shifted)
        mass = mass + jnp.sum(e, axis=1, keepdims=True)
        moment = moment + jnp.sum(e * shifted, axis=1, keepdims=True)
        picked = picked + jnp.sum(jnp.where(hit, piece, 0.0), axis=1, keepdims=True)
        first = i // len(qs) * size
        qs[i % len(qs)][:, first : first + size] = e.astype(BF16)
    stats[...] = lanes_of([top, mass, moment, picked, inv], stats.shape)


def softmax(pieces, targets, size, width):
    counts = [len(p) for p in pieces]
    flat = [part for p in pieces for part in p]
    rows = targets.shape[0]
    return pl.pallas_call(
        functools.partial(softmax_kernel, counts, size, width),
        out_shape=[jax.ShapeDtypeStruct((rows, len(pieces) // 2 * size), BF16)] * 2
        + [jax.ShapeDtypeStruct((rows, LANES), F32)],
        grid=(1,),
        in_specs=[whole((rows, part.shape[1])) for part in flat] + [whole(targets.shape)],
        out_specs=[whole((rows, len(pieces) // 2 * size))] * 2 + [whole((rows, LANES))],
        compiler_params=params(16),
    )(*flat, targets)


def tree(op, values):
    while len(values) > 1:
        half = len(values) // 2
        values = [op(a, b) for a, b in zip(values[:half], values[half:])]
    return values[0]


def lanes_of(values, shape):
    lane = lax.broadcasted_iota(jnp.int32, shape, 1)
    out = jnp.zeros(shape, F32)
    for i, value in enumerate(values):
        out = jnp.where(lane == i, value, out)
    return out


def merge_two(a, b):
    top = jnp.maximum(a[:, 0:1], b[:, 0:1])
    mass, moment = 0.0, 0.0
    for part in (a, b):
        shift = part[:, 0:1] - top
        weight = jnp.exp(shift)
        mass = mass + weight * part[:, 1:2]
        moment = moment + weight * (part[:, 2:3] + part[:, 1:2] * shift)
    return top, mass, moment, a[:, 3:4] + b[:, 3:4]


def merge_kernel(a, b, *refs):
    refs[-1][...] = lanes_of(merge_two(a[...], b[...]), refs[-1].shape)


def finish_kernel(tokens, width, a, b, own, targets, *refs):
    top, mass, moment, picked = merge_two(a[...], b[...])
    lse = top + jnp.log(mass)
    inv = own[:, 4:5]
    scale = jnp.exp(own[:, 0:1] - lse) / tokens
    at_target = (jnp.exp(picked - lse) - 1.0) / tokens
    pull = (moment / mass + (top - picked)) * (inv * inv) / (tokens * width)
    values = [scale, at_target, targets[:, 0:1].astype(F32), inv, pull, lse - picked]
    refs[-1][...] = lanes_of(values, refs[-1].shape)


def merge(body, values, deps):
    shape = values[0].shape
    return pl.pallas_call(
        body,
        out_shape=jax.ShapeDtypeStruct(shape, F32),
        grid=(1,),
        in_specs=[whole(shape)] * len(values) + after(deps),
        out_specs=whole(shape),
        compiler_params=params(16),
    )(*values, *deps)


def dlogits_kernel(places, quarter, *refs):
    qs, (packs, dlogits, loss) = refs[:-3], refs[-3:]
    n = 2 * len(places[0])
    rows = packs.shape[0] // n
    sums = [jnp.sum(packs[s * rows : (s + 1) * rows, 5:6], axis=0, keepdims=True) for s in range(n)]
    loss[...] = jnp.broadcast_to(tree(jnp.add, sums) / packs.shape[0], loss.shape)
    for i, (q, order) in enumerate(zip(qs, places)):
        for here, s in enumerate(order):
            at = slice(s * rows, (s + 1) * rows)
            scale, at_target, target = packs[at, 0:1], packs[at, 1:2], packs[at, 2:3].astype(jnp.int32)
            for j in range(q.shape[1] // quarter):
                first = (j * len(qs) // 2 + i // 2) * quarter
                values = q[here * rows : (here + 1) * rows, j * quarter : (j + 1) * quarter].astype(F32) * scale
                ids = lax.broadcasted_iota(jnp.int32, values.shape, 1) + first
                dlogits[at, first : first + quarter] = jnp.where(ids == target, at_target, values).astype(BF16)


def scale_rows(q, packs, quarter):
    values, places = zip(*[part for half in q for part in half])
    shape = (packs.shape[0], 2 * values[0].shape[1])
    return pl.pallas_call(
        functools.partial(dlogits_kernel, places, quarter),
        out_shape=[jax.ShapeDtypeStruct(shape, BF16), jax.ShapeDtypeStruct((8, LANES), F32)],
        compiler_params=params(16),
    )(*values, packs)


def dpre_kernel(n, *refs):
    parts, (packs, pre, h, gain, out) = refs[:n], refs[n:]
    dnormed = parts[0][0]
    for part in parts[1:]:
        dnormed = dnormed + part[0].astype(F32)
    inv, pull = packs[:, 3:4], packs[:, 4:5]
    v = pre[...]
    sigma = 1.0 / (1.0 + jnp.exp(-v))
    act = h[...].astype(F32) + v * sigma
    dact = inv * gain[...] * dnormed - act * pull
    out[...] = (dact * sigma * (1.0 + v * (1.0 - sigma))).astype(BF16)


def grad_pre(parts, packs, pre, h, gain):
    rows, block = pre.shape
    rest = [packs, pre, h, gain]
    return pl.pallas_call(
        functools.partial(dpre_kernel, len(parts)),
        out_shape=jax.ShapeDtypeStruct(pre.shape, BF16),
        grid=(1,),
        in_specs=[pick(t, rows, block) for t in parts] + [whole(r.shape) for r in rest],
        out_specs=whole(pre.shape),
        compiler_params=params(16),
    )(*[t[0] for t in parts], *rest)


def grad_kernel(order, step, me, h, *refs):
    n = len(order)
    ds, (out, placed, mixed, outputs, left) = refs[:n], refs[n:]
    slots = outputs.shape[0]
    lanes = range(0, out.shape[1], LANES)
    for s, d in zip(order, ds):
        placed[me[0] ^ s] = d[...]

    def leave(i):
        target = out.at[pl.ds(i * step * n, step * n), :]
        return pltpu.make_async_copy(outputs.at[i % slots], target, left.at[i % slots])

    steps = h.shape[0] // step
    for i in range(steps):
        if i >= slots:
            leave(i - slots).wait()
        for k in range(n):
            product = jnp.dot(h[i * step : (i + 1) * step, :], placed[k], preferred_element_type=F32)
            for j, lane in enumerate(lanes):
                mixed[j, pl.ds(k, step, stride=n + 1), :] = product[:, lane : lane + LANES]

        def collect(first, group):
            at = pl.multiple_of(first * n, 16)
            for j, lane in enumerate(lanes):
                parts = [
                    mixed[j, pl.ds((first + g) * (n + 1) + p, 8), :]
                    for g in range(group)
                    for p in range(0, n, 8)
                ]
                values = jnp.concatenate(parts, axis=0).astype(BF16)
                outputs[i % slots, pl.ds(at, group * n), lane : lane + LANES] = values

        each_tile(n, step, collect)
        leave(i).start()
    for i in range(max(0, steps - slots), steps):
        leave(i).wait()


def weight_grad(h, ds, me):
    width, rows = h.shape
    n = len(ds)
    block = ds[0].shape[1]
    order = sorted(ds)
    step = min(256, width)
    slots = 3
    return pl.pallas_call(
        functools.partial(grad_kernel, order, step),
        out_shape=jax.ShapeDtypeStruct((width * n, block), BF16),
        grid_spec=pltpu.PrefetchScalarGridSpec(
            num_scalar_prefetch=1,
            grid=(1,),
            in_specs=[whole(h.shape)] + [whole((rows, block))] * n,
            out_specs=pl.BlockSpec(memory_space=pl.ANY),
            scratch_shapes=[
                pltpu.VMEM((n, rows, block), BF16),
                pltpu.VMEM((block // LANES, step * (n + 1), LANES), F32),
                pltpu.VMEM((slots, step * n, block), BF16),
                pltpu.SemaphoreType.DMA((slots,)),
            ],
        ),
        compiler_params=params(48),
        cost_estimate=SHORT,
    )(me, h, *[ds[s] for s in order])


def column(values):
    return jnp.broadcast_to(values[:, None], (values.shape[0], LANES))


def on_device(hidden_rows, head_weight, norm_gain, vocab_embed, targets):
    n_dp, n_mp = lax.axis_size("dp"), lax.axis_size("mp")
    tok_dp, width_mp = hidden_rows.shape
    block = head_weight.shape[3]
    width = width_mp * n_mp
    tokens = tok_dp * n_dp
    vocab_mp = vocab_embed.shape[0]
    dp_bits, mp_bits = bits_of(n_dp), bits_of(n_mp)
    dp_index = lax.axis_index("dp")
    mp_index = lax.axis_index("mp")
    me = mp_index.astype(jnp.int32).reshape(1)
    pairs = list(range(n_mp - 2, -1, -2))

    embed_rows = vocab_embed.reshape(vocab_mp * n_mp, block)
    gain = norm_gain.reshape(1, block)
    quarter, eighth = vocab_mp // 4, vocab_mp // 8

    orders = [dp_bits, dp_bits[::-1]] * 2
    half = width_mp // 2
    weight_rows = head_weight.reshape(width_mp * n_mp, block)
    weight, made = relayout(weight_rows, n_mp, 0, half, None, [])
    gathered, hops = zip(
        *[gather_rows(hidden_rows[:, i * half : (i + 1) * half], "dp", orders[i], [made]) for i in range(2)]
    )
    weight, _ = relayout(weight_rows, n_mp, half, half, weight, hops)
    h = lay(gathered)
    own_h = lax.dynamic_slice_in_dim(h, dp_index * block, block, 1)

    def reduce_product(lhs, w, fillers):
        terms, totals, made = collections.defaultdict(list), {}, None

        def run(group, deps):
            outs = project(lhs, w, me, group, deps)
            for pair, odd, even in zip(group, outs[::2], outs[1::2]):
                terms[pair][:0] = [(even, 0), (swap(odd, "mp", 1), 0)]
            return [outs[1]]

        def leave(s, bit, deps=()):
            totals[s] = add_round(terms[s], deps)
            terms[s ^ bit].append((swap(totals[s], "mp", bit), 0))

        first = pairs[0]
        before = run(pairs[1:2], run([first], []))
        leave(first, mp_bits[1])
        run(pairs[2:], [*before, totals[first]])
        done = 1
        for bit, filler in itertools.zip_longest(mp_bits[1:], fillers):
            for s in sorted(terms, reverse=True):
                if s & bit and not s & done and s not in totals:
                    leave(s, bit, [] if made is None else [made[1]])
            done |= bit
            if filler:
                made = filler(made and made[0], list(totals.values()))
        return terms[0], made

    def fill(first, count):
        def run(into, deps):
            return relayout(embed_rows, n_mp, first * eighth, count * eighth, into, deps)

        return run

    parts, (embed, made) = reduce_product(h, weight, [None, fill(0, 3)])
    pre, x = activate(parts, own_h, gain, [made])

    embed, made = fill(3, 4)(embed, [x])
    xs = gather_xor(x, "mp", mp_bits[::-1], [made])
    embed, _ = fill(7, 1)(embed, [xs[mp_bits[-1]]])
    pieces, before = [], []
    for i, order in enumerate(orders):
        late = [pieces[0][1]] if i == 3 else []
        sent, kept = project_vocab(xs, embed, me, order, i * quarter, quarter, before + late)
        pieces.append([kept, swap(sent, "dp", order[0])])
        before = [kept]
    pieces = sum_hops(pieces, "dp", orders)

    local = lax.dynamic_slice_in_dim(targets, dp_index * tok_dp, tok_dp, 0) - mp_index * vocab_mp
    local = column(local)
    *own_q, stats = softmax(pieces, local, quarter, width)
    total = stats
    for bit in mp_bits[:-1]:
        total = merge(merge_kernel, [total, swap(total, "mp", bit)], [])
    q, hops = zip(*[gather_rows(own_q[i], "dp", orders[i], [total]) for i in range(2)])
    finish = functools.partial(finish_kernel, tokens, width)
    packed = merge(finish, [total, swap(total, "mp", mp_bits[-1]), stats, local], hops)
    packs = jnp.concatenate(gather_direct(packed, "dp"), axis=0)
    dlogits, loss = scale_rows(q, packs, quarter)
    parts, _ = reduce_product(dlogits, embed, [None, None])
    dpre = grad_pre(parts, packs, pre, own_h, gain)
    grad = weight_grad(h.T, gather_xor(dpre, "mp", mp_bits[::-1]), me)
    return (grad.reshape(head_weight.shape), loss[0, 0])


def solution(mesh):
    return jax.shard_map(
        on_device,
        mesh=mesh,
        in_specs=(
            P("dp", "mp"),
            P("mp", None, "dp", None),
            P("mp", "dp", None),
            P("mp", None, "dp", None),
            P(),
        ),
        out_specs=(P("mp", None, "dp", None), P()),
        check_vma=False,
    )
```

```python
import collections
import functools
import itertools
import math

import jax
import jax.numpy as jnp
from jax import lax
from jax.experimental import pallas as pl
from jax.experimental.pallas import tpu as pltpu
from jax.sharding import PartitionSpec as P

F32 = jnp.float32
BF16 = jnp.bfloat16
LANES = 128
SHORT = pl.CostEstimate(flops=1, bytes_accessed=1, transcendentals=0)


def params(mib):
    return pltpu.CompilerParams(vmem_limit_bytes=mib * 2**20)


def bits_of(n):
    bits = [1 << i for i in range(n.bit_length() - 1)]
    assert 1 << len(bits) == n
    return bits


def swap(value, axis, bit):
    n = lax.axis_size(axis)
    return lax.ppermute(value, axis, [(i, i ^ bit) for i in range(n)])


def gather_xor(value, axis, bits, deps=()):
    held = {0: value}
    if deps:
        first, second = bits[:2]
        held[second] = swap(value, axis, second)
        held[first] = hold(swap(value, axis, first), [*deps, held[second]])
    for bit in bits:
        for s in list(held):
            if s % (2 * bit) == 0 and s | bit not in held:
                held[s | bit] = swap(held[s], axis, bit)
    return held


def join_kernel(a, b, *refs):
    out = refs[-1]
    out[: a.shape[0]] = a[...]
    out[a.shape[0] :] = b[...]


def join(a, b, deps):
    shape = (2 * a.shape[0], a.shape[1])
    return pl.pallas_call(
        join_kernel,
        out_shape=jax.ShapeDtypeStruct(shape, a.dtype),
        grid=(1,),
        in_specs=[whole(a.shape)] * 2 + after(deps),
        out_specs=whole(shape),
        compiler_params=params(48),
    )(a, b, *deps)


def gather_rows(value, axis, bits, deps):
    places, hops = [0], []
    for bit in bits[:-1]:
        value = join(value, swap(value, axis, bit), [] if hops else deps)
        hops.append(value)
        places = places + [s ^ bit for s in places]
    arrived = swap(value, axis, bits[-1])
    return [(value, places), (arrived, [s ^ bits[-1] for s in places])], hops[0]


def lay_kernel(places, *refs):
    out = refs[-1]
    width = refs[0].shape[1]
    for i, order in enumerate(places):
        rows = refs[i].shape[0] // len(order)
        first = i // 2 * width
        for j, s in enumerate(order):
            out[s * rows : (s + 1) * rows, first : first + width] = refs[i][j * rows : (j + 1) * rows]


def lay(gathered):
    values, places = zip(*[part for half in gathered for part in half])
    shape = (2 * values[0].shape[0], 2 * values[0].shape[1])
    return pl.pallas_call(
        functools.partial(lay_kernel, places),
        out_shape=jax.ShapeDtypeStruct(shape, values[0].dtype),
        grid=(1,),
        in_specs=[whole(v.shape) for v in values],
        out_specs=whole(shape),
        compiler_params=params(48),
    )(*values)


def gather_direct(value, axis):
    return [value] + [swap(value, axis, s) for s in range(1, lax.axis_size(axis))]


def whole(shape):
    return pl.BlockSpec(shape, lambda *_: (0,) * len(shape))


def stream(sources, buffer, sems, use):
    slots = buffer.shape[0]

    def copy(i):
        return pltpu.make_async_copy(sources[i], buffer.at[i % slots], sems.at[i % slots])

    for i in range(min(slots, len(sources))):
        copy(i).start()
    for i in range(len(sources)):
        copy(i).wait()
        use(i, i % slots)
        if i + slots < len(sources):
            copy(i + slots).start()


def after(deps):
    return [pl.BlockSpec(memory_space=pl.ANY)] * len(deps)


def each_tile(n, rows, run):
    group = max(1, 16 // n)

    def body(i, carry):
        run(i * group, group)
        return carry

    lax.fori_loop(0, rows // group, body, 0, unroll=8)


def relayout_kernel(n, start, rows, step, x, *refs):
    out, order, inputs, outputs, arrived, left = refs[-6:]
    size = order.shape[0]
    group = size // n

    to = lax.broadcasted_iota(jnp.int32, order.shape, 0)
    source = lax.broadcasted_iota(jnp.int32, order.shape, 1)
    order[...] = jnp.where(source == to % group * n + to // group, 1.0, 0.0).astype(BF16)
    slots = outputs.shape[0]

    def leave(i):
        target = out.at[:, pl.ds(start + i * step, step), :]
        return pltpu.make_async_copy(outputs.at[i % slots], target, left.at[i % slots])

    def use(i, slot):
        if i >= slots:
            leave(i - slots).wait()
        for part in range(step // group):
            taken = inputs[slot, part * size : (part + 1) * size, :]
            mixed = jnp.dot(order[...], taken, preferred_element_type=F32).astype(BF16)
            for k in range(n):
                at = slice(part * group, (part + 1) * group)
                outputs[i % slots, k, at, :] = mixed[k * group : (k + 1) * group]
        leave(i).start()

    steps = rows // step
    sources = [x.at[pl.ds((start + i * step) * n, step * n), :] for i in range(steps)]
    stream(sources, inputs, arrived, use)
    for i in range(max(0, steps - slots), steps):
        leave(i).wait()


def relayout(flat, n, start, rows, into, deps):
    total, block = flat.shape[0] // n, flat.shape[1]
    step = min(128, rows)
    slots = 4
    skipped = list(deps) if into is None else [into, *deps]
    return pl.pallas_call(
        functools.partial(relayout_kernel, n, start, rows, step),
        out_shape=jax.ShapeDtypeStruct((n, total, block), BF16),
        in_specs=after([flat, *skipped]),
        out_specs=pl.BlockSpec(memory_space=pl.ANY),
        scratch_shapes=[
            pltpu.VMEM((256, 256), BF16),
            pltpu.VMEM((slots, step * n, block), BF16),
            pltpu.VMEM((slots, n, step, block), BF16),
            pltpu.SemaphoreType.DMA((slots,)),
            pltpu.SemaphoreType.DMA((slots,)),
        ],
        input_output_aliases={} if into is None else {1: 0},
        compiler_params=params(48),
        cost_estimate=SHORT,
    )(flat, *skipped)


def hold_kernel(value, *refs):
    refs[-1][...] = value[...]


def hold(value, deps):
    return pl.pallas_call(
        hold_kernel,
        out_shape=jax.ShapeDtypeStruct(value.shape, value.dtype),
        grid=(1,),
        in_specs=[whole(value.shape)] + after(deps),
        out_specs=whole(value.shape),
        compiler_params=params(48),
    )(value, *deps)


def project_kernel(pairs, step, me, lhs, w, *refs):
    total, buffer, sems = refs[-3:]
    outs = refs[-3 - 2 * len(pairs) : -3]
    steps = w.shape[1] // step
    blocks = [me[0] ^ s for pair in pairs for s in (pair + 1, pair)]
    sources = [w.at[k, pl.ds(c * step, step), :] for k in blocks for c in range(steps)]

    def use(i, slot):
        c = i % steps
        part = jnp.dot(lhs[:, c * step : (c + 1) * step], buffer[slot], preferred_element_type=F32)
        if c > 0:
            part = part + total[...]
        if c < steps - 1:
            total[...] = part
        else:
            out = outs[i // steps]
            out[0] = part.astype(out.dtype)

    stream(sources, buffer, sems, use)


def project(lhs, w, me, pairs, deps):
    _, depth, block = w.shape
    rows = lhs.shape[0]
    step = min(1024, depth)
    slots = 4
    out = whole((1, rows, block))
    return pl.pallas_call(
        functools.partial(project_kernel, pairs, step),
        out_shape=[jax.ShapeDtypeStruct((1, rows, block), kind) for _ in pairs for kind in (BF16, F32)],
        grid_spec=pltpu.PrefetchScalarGridSpec(
            num_scalar_prefetch=1,
            grid=(1,),
            in_specs=[whole(lhs.shape)] + after([w, *deps]),
            out_specs=[out] * (2 * len(pairs)),
            scratch_shapes=[
                pltpu.VMEM((rows, block), F32),
                pltpu.VMEM((slots, step, block), BF16),
                pltpu.SemaphoreType.DMA((slots,)),
            ],
        ),
        compiler_params=params(48),
        cost_estimate=SHORT,
    )(me, lhs, w, *deps)


def pick(term, rows, block):
    array, place = term
    return pl.BlockSpec((1, rows, block), lambda *_: (place, 0, 0))


def add_kernel(n, *refs):
    out = refs[-1]
    total = refs[0][0].astype(F32)
    for ref in refs[1:n]:
        total = total + ref[0].astype(F32)
    out[0] = total.astype(out.dtype)


def add_round(terms, deps=()):
    _, rows, block = terms[0][0].shape
    return pl.pallas_call(
        functools.partial(add_kernel, len(terms)),
        out_shape=jax.ShapeDtypeStruct((1, rows, block), BF16),
        grid=(1,),
        in_specs=[pick(t, rows, block) for t in terms] + after(deps),
        out_specs=whole((1, rows, block)),
        compiler_params=params(48),
    )(*[t[0] for t in terms], *deps)


def square_rows(tokens, block):
    return max(1, tokens // block)


def act_kernel(n, *refs):
    parts, (h, gain, pre, x) = refs[:n], refs[-4:]
    total = parts[0][0].astype(F32)
    for part in parts[1:]:
        total = total + part[0].astype(F32)
    pre[...] = total
    act = h[...].astype(F32) + total / (1.0 + jnp.exp(-total))
    tokens, block = act.shape
    x[:tokens] = (act * gain[...]).astype(BF16)

    sums = jnp.broadcast_to(jnp.sum(act * act, axis=1, keepdims=True), (tokens, LANES))
    rest = jnp.transpose(sums)[0:1]
    count = square_rows(tokens, block)
    span = tokens // count
    row = lax.broadcasted_iota(jnp.int32, (16, span), 0)
    extra = jnp.zeros((16, span), F32)
    for term in range(3):
        high = rest.astype(BF16).astype(F32)
        rest = rest - high
        for i in range(count):
            extra = jnp.where(row == term * count + i, high[:, i * span : (i + 1) * span], extra)
    x[tokens:] = jnp.zeros((16, block), BF16)
    x[tokens:, :span] = extra.astype(BF16)


def activate(parts, h, gain, deps=()):
    rows, block = h.shape
    return pl.pallas_call(
        functools.partial(act_kernel, len(parts)),
        out_shape=[
            jax.ShapeDtypeStruct((rows, block), F32),
            jax.ShapeDtypeStruct((rows + 16, block), BF16),
        ],
        grid=(1,),
        in_specs=[pick(t, rows, block) for t in parts] + after(deps) + [whole(h.shape), whole(gain.shape)],
        out_specs=[whole((rows, block)), whole((rows + 16, block))],
        compiler_params=params(48),
    )(*[t[0] for t in parts], *deps, h, gain)


def hop_order(bits):
    places = [0]
    for bit in bits[::-1]:
        places = places + [s | bit for s in places]
    return places


def power(exponent):
    return jnp.exp(exponent * math.log(2.0))


def exponent_of(values):
    return jnp.ceil(jnp.log(jnp.maximum(values, 1e-30)) * (1.0 / math.log(2.0)))


def integers(values):
    values = jnp.clip(jnp.floor(values), -32768.0, 32767.0)
    return values.astype(jnp.int32).astype(jnp.int16)


def encode(values, squares):
    exponent = exponent_of(jnp.max(jnp.abs(values), axis=1, keepdims=True))
    own = exponent_of(squares)
    scaled = squares * power(15.0 - own)
    high = jnp.minimum(jnp.floor(scaled), 32767.0)
    extra = [exponent, own, high, (scaled - high) * 32768.0]
    return integers(values * power(15.0 - exponent) + 0.5), integers(
        lanes_of(extra, (values.shape[0], LANES))
    )


def decode(ref, rows, size):
    values = ref[rows, :size].astype(jnp.int32).astype(F32)
    extra = ref[rows, size:].astype(jnp.int32).astype(F32)
    squares = (extra[:, 2:3] + extra[:, 3:4] / 32768.0) * power(extra[:, 1:2] - 15.0)
    return values * power(extra[:, 0:1] - 15.0), squares


def piece_sum(refs, rows, size):
    values, squares = refs[0][rows, :size], refs[0][rows, size : size + 1]
    for ref in refs[1:]:
        more = decode(ref, rows, size)
        values, squares = values + more[0], squares + more[1]
    return values, squares


def logits_kernel(order, places, start, me, *refs):
    n = len(order)
    xs, e, (sent, kept, total, buffer, sems) = refs[:n], refs[n], refs[-5:]
    tokens, block = xs[0].shape[0] - 16, xs[0].shape[1]
    rows = tokens // len(places)
    size = kept.shape[1] - LANES

    extra = functools.reduce(jnp.add, [x[tokens:].astype(F32) for x in xs])
    count = square_rows(tokens, block)
    span = tokens // count
    columns = []
    for i in range(count):
        terms = [extra[t * count + i : t * count + i + 1, :span] for t in range(3)]
        columns.append(jnp.transpose(jnp.broadcast_to(functools.reduce(jnp.add, terms), (LANES, span))))
    squares = jnp.concatenate(columns, axis=0) if count > 1 else columns[0]

    def use(i, slot):
        part = lax.dot_general(
            xs[i][:tokens], buffer[slot], (((1,), (1,)), ((), ())), preferred_element_type=F32
        )
        if i > 0:
            part = part + total[...]
        if i < n - 1:
            total[...] = part
            return
        for j, s in enumerate(places):
            here = slice(s * rows, (s + 1) * rows)
            first = j % (len(places) // 2) * rows
            to = slice(first, first + rows)
            if j < len(places) // 2:
                kept[to, :size], kept[to, size:] = part[here], squares[here]
            else:
                sent[to, :size], sent[to, size:] = encode(part[here], squares[here, 0:1])

    stream([e.at[me[0] ^ s, pl.ds(start, size), :] for s in order], buffer, sems, use)


def project_vocab(xs, embed, me, bits, start, size, deps):
    n, _, block = embed.shape
    order = sorted(xs)
    rows = xs[0].shape[0] - 16
    slots = 4
    shape = (rows // 2, size + LANES)
    return pl.pallas_call(
        functools.partial(logits_kernel, order, hop_order(bits), start),
        out_shape=[jax.ShapeDtypeStruct(shape, kind) for kind in (jnp.int16, F32)],
        grid_spec=pltpu.PrefetchScalarGridSpec(
            num_scalar_prefetch=1,
            grid=(1,),
            in_specs=[whole((rows + 16, block))] * n + after([embed, *deps]),
            out_specs=[whole(shape)] * 2,
            scratch_shapes=[
                pltpu.VMEM((rows, size), F32),
                pltpu.VMEM((slots, size, block), BF16),
                pltpu.SemaphoreType.DMA((slots,)),
            ],
        ),
        compiler_params=params(48),
        cost_estimate=SHORT,
    )(me, *[xs[s] for s in order], embed, *deps)


def hop_kernel(kept, arrived, *refs):
    out, rest = refs[-2:]
    rows, size = out.shape[0], out.shape[1] - LANES
    out[:, :size], out[:, size:] = encode(*piece_sum([kept, arrived], slice(rows, 2 * rows), size))
    values, squares = piece_sum([kept, arrived], slice(0, rows), size)
    rest[:, :size], rest[:, size:] = values, jnp.broadcast_to(squares, (rows, LANES))


def hop_sum(kept, arrived, deps):
    rows, size = kept.shape[0] // 2, kept.shape[1]
    return pl.pallas_call(
        hop_kernel,
        out_shape=[jax.ShapeDtypeStruct((rows, size), kind) for kind in (jnp.int16, F32)],
        grid=(1,),
        in_specs=[whole(kept.shape)] * 2 + after(deps),
        out_specs=[whole((rows, size))] * 2,
        compiler_params=params(48),
    )(kept, arrived, *deps)


def sum_hops(terms, axis, orders):
    before = []
    for hop in range(1, len(orders[0])):
        for i, held in enumerate(terms):
            if i == len(terms) - 1:
                before = before + [t[1] for t in terms[:2]]
            sent, kept = hop_sum(*held, before)
            before = [sent]
            terms[i] = [kept, swap(sent, axis, orders[i][hop])]
    return terms


def softmax_kernel(counts, size, width, *refs):
    parts, (targets, *refs) = refs[: sum(counts)], refs[sum(counts) :]
    qs, stats = refs[:-1], refs[-1]
    target = targets[:, 0:1]
    pieces, hits, at = [], [], 0
    for i, count in enumerate(counts):
        total, squares = piece_sum(parts[at : at + count], slice(None), size)
        at += count
        if i == 0:
            inv = lax.rsqrt(squares / width + 1e-05)
        ids = lax.broadcasted_iota(jnp.int32, total.shape, 1) + i * size
        pieces.append(total * inv)
        hits.append(ids == target)
    top = functools.reduce(jnp.maximum, [jnp.max(p, axis=1, keepdims=True) for p in pieces])
    mass, moment, picked = 0.0, 0.0, 0.0
    for i, (piece, hit) in enumerate(zip(pieces, hits)):
        shifted = piece - top
        e = jnp.exp(shifted)
        mass = mass + jnp.sum(e, axis=1, keepdims=True)
        moment = moment + jnp.sum(e * shifted, axis=1, keepdims=True)
        picked = picked + jnp.sum(jnp.where(hit, piece, 0.0), axis=1, keepdims=True)
        first = i // len(qs) * size
        qs[i % len(qs)][:, first : first + size] = e.astype(BF16)
    stats[...] = lanes_of([top, mass, moment, picked, inv], stats.shape)


def softmax(pieces, targets, size, width):
    counts = [len(p) for p in pieces]
    flat = [part for p in pieces for part in p]
    rows = targets.shape[0]
    return pl.pallas_call(
        functools.partial(softmax_kernel, counts, size, width),
        out_shape=[jax.ShapeDtypeStruct((rows, len(pieces) // 2 * size), BF16)] * 2
        + [jax.ShapeDtypeStruct((rows, LANES), F32)],
        grid=(1,),
        in_specs=[whole((rows, part.shape[1])) for part in flat] + [whole(targets.shape)],
        out_specs=[whole((rows, len(pieces) // 2 * size))] * 2 + [whole((rows, LANES))],
        compiler_params=params(48),
    )(*flat, targets)


def tree(op, values):
    while len(values) > 1:
        half = len(values) // 2
        values = [op(a, b) for a, b in zip(values[:half], values[half:])]
    return values[0]


def lanes_of(values, shape):
    lane = lax.broadcasted_iota(jnp.int32, shape, 1)
    out = jnp.zeros(shape, F32)
    for i, value in enumerate(values):
        out = jnp.where(lane == i, value, out)
    return out


def merge_two(a, b):
    top = jnp.maximum(a[:, 0:1], b[:, 0:1])
    mass, moment = 0.0, 0.0
    for part in (a, b):
        shift = part[:, 0:1] - top
        weight = jnp.exp(shift)
        mass = mass + weight * part[:, 1:2]
        moment = moment + weight * (part[:, 2:3] + part[:, 1:2] * shift)
    return top, mass, moment, a[:, 3:4] + b[:, 3:4]


def merge_kernel(a, b, *refs):
    refs[-1][...] = lanes_of(merge_two(a[...], b[...]), refs[-1].shape)


def finish_kernel(tokens, width, a, b, own, targets, *refs):
    top, mass, moment, picked = merge_two(a[...], b[...])
    lse = top + jnp.log(mass)
    inv = own[:, 4:5]
    scale = jnp.exp(own[:, 0:1] - lse) / tokens
    at_target = (jnp.exp(picked - lse) - 1.0) / tokens
    pull = (moment / mass + (top - picked)) * (inv * inv) / (tokens * width)
    values = [scale, at_target, targets[:, 0:1].astype(F32), inv, pull, lse - picked]
    refs[-1][...] = lanes_of(values, refs[-1].shape)


def merge(body, values, deps):
    shape = values[0].shape
    return pl.pallas_call(
        body,
        out_shape=jax.ShapeDtypeStruct(shape, F32),
        grid=(1,),
        in_specs=[whole(shape)] * len(values) + after(deps),
        out_specs=whole(shape),
        compiler_params=params(48),
    )(*values, *deps)


def dlogits_kernel(places, quarter, *refs):
    qs, (packs, dlogits, loss) = refs[:-3], refs[-3:]
    n = 2 * len(places[0])
    rows = packs.shape[0] // n
    sums = [jnp.sum(packs[s * rows : (s + 1) * rows, 5:6], axis=0, keepdims=True) for s in range(n)]
    loss[...] = jnp.broadcast_to(tree(jnp.add, sums) / packs.shape[0], loss.shape)
    for i, (q, order) in enumerate(zip(qs, places)):
        for here, s in enumerate(order):
            at = slice(s * rows, (s + 1) * rows)
            scale, at_target, target = packs[at, 0:1], packs[at, 1:2], packs[at, 2:3].astype(jnp.int32)
            for j in range(q.shape[1] // quarter):
                first = (j * len(qs) // 2 + i // 2) * quarter
                values = q[here * rows : (here + 1) * rows, j * quarter : (j + 1) * quarter].astype(F32) * scale
                ids = lax.broadcasted_iota(jnp.int32, values.shape, 1) + first
                dlogits[at, first : first + quarter] = jnp.where(ids == target, at_target, values).astype(BF16)


def scale_rows(q, packs, quarter):
    values, places = zip(*[part for half in q for part in half])
    shape = (packs.shape[0], 2 * values[0].shape[1])
    return pl.pallas_call(
        functools.partial(dlogits_kernel, places, quarter),
        out_shape=[jax.ShapeDtypeStruct(shape, BF16), jax.ShapeDtypeStruct((8, LANES), F32)],
        compiler_params=params(48),
    )(*values, packs)


def dpre_kernel(n, *refs):
    parts, (packs, pre, h, gain, out) = refs[:n], refs[n:]
    dnormed = parts[0][0]
    for part in parts[1:]:
        dnormed = dnormed + part[0].astype(F32)
    inv, pull = packs[:, 3:4], packs[:, 4:5]
    v = pre[...]
    sigma = 1.0 / (1.0 + jnp.exp(-v))
    act = h[...].astype(F32) + v * sigma
    dact = inv * gain[...] * dnormed - act * pull
    out[...] = (dact * sigma * (1.0 + v * (1.0 - sigma))).astype(BF16)


def grad_pre(parts, packs, pre, h, gain):
    rows, block = pre.shape
    rest = [packs, pre, h, gain]
    return pl.pallas_call(
        functools.partial(dpre_kernel, len(parts)),
        out_shape=jax.ShapeDtypeStruct(pre.shape, BF16),
        grid=(1,),
        in_specs=[pick(t, rows, block) for t in parts] + [whole(r.shape) for r in rest],
        out_specs=whole(pre.shape),
        compiler_params=params(48),
    )(*[t[0] for t in parts], *rest)


def grad_kernel(order, step, me, h, *refs):
    n = len(order)
    ds, (out, placed, mixed, outputs, left) = refs[:n], refs[n:]
    slots = outputs.shape[0]
    lanes = range(0, out.shape[1], LANES)
    for s, d in zip(order, ds):
        placed[me[0] ^ s] = d[...]

    def leave(i):
        target = out.at[pl.ds(i * step * n, step * n), :]
        return pltpu.make_async_copy(outputs.at[i % slots], target, left.at[i % slots])

    steps = h.shape[0] // step
    for i in range(steps):
        if i >= slots:
            leave(i - slots).wait()
        for k in range(n):
            product = jnp.dot(h[i * step : (i + 1) * step, :], placed[k], preferred_element_type=F32)
            for j, lane in enumerate(lanes):
                mixed[j, pl.ds(k, step, stride=n + 1), :] = product[:, lane : lane + LANES]

        def collect(first, group):
            at = pl.multiple_of(first * n, 16)
            for j, lane in enumerate(lanes):
                parts = [
                    mixed[j, pl.ds((first + g) * (n + 1) + p, 8), :]
                    for g in range(group)
                    for p in range(0, n, 8)
                ]
                values = jnp.concatenate(parts, axis=0).astype(BF16)
                outputs[i % slots, pl.ds(at, group * n), lane : lane + LANES] = values

        each_tile(n, step, collect)
        leave(i).start()
    for i in range(max(0, steps - slots), steps):
        leave(i).wait()


def weight_grad(h, ds, me):
    width, rows = h.shape
    n = len(ds)
    block = ds[0].shape[1]
    order = sorted(ds)
    step = min(256, width)
    slots = 3
    return pl.pallas_call(
        functools.partial(grad_kernel, order, step),
        out_shape=jax.ShapeDtypeStruct((width * n, block), BF16),
        grid_spec=pltpu.PrefetchScalarGridSpec(
            num_scalar_prefetch=1,
            grid=(1,),
            in_specs=[whole(h.shape)] + [whole((rows, block))] * n,
            out_specs=pl.BlockSpec(memory_space=pl.ANY),
            scratch_shapes=[
                pltpu.VMEM((n, rows, block), BF16),
                pltpu.VMEM((block // LANES, step * (n + 1), LANES), F32),
                pltpu.VMEM((slots, step * n, block), BF16),
                pltpu.SemaphoreType.DMA((slots,)),
            ],
        ),
        compiler_params=params(48),
        cost_estimate=SHORT,
    )(me, h, *[ds[s] for s in order])


def column(values):
    return jnp.broadcast_to(values[:, None], (values.shape[0], LANES))


def on_device(hidden_rows, head_weight, norm_gain, vocab_embed, targets):
    n_dp, n_mp = lax.axis_size("dp"), lax.axis_size("mp")
    tok_dp, width_mp = hidden_rows.shape
    block = head_weight.shape[3]
    width = width_mp * n_mp
    tokens = tok_dp * n_dp
    vocab_mp = vocab_embed.shape[0]
    dp_bits, mp_bits = bits_of(n_dp), bits_of(n_mp)
    dp_index = lax.axis_index("dp")
    mp_index = lax.axis_index("mp")
    me = mp_index.astype(jnp.int32).reshape(1)
    pairs = list(range(n_mp - 2, -1, -2))

    embed_rows = vocab_embed.reshape(vocab_mp * n_mp, block)
    gain = norm_gain.reshape(1, block)
    quarter = vocab_mp // 4

    orders = [dp_bits, dp_bits[::-1]] * 2
    half = width_mp // 2
    weight_rows = head_weight.reshape(width_mp * n_mp, block)
    weight = relayout(weight_rows, n_mp, 0, half, None, [])
    gathered, hops = zip(
        *[gather_rows(hidden_rows[:, i * half : (i + 1) * half], "dp", orders[i], [weight]) for i in range(2)]
    )
    weight = relayout(weight_rows, n_mp, half, half, weight, hops)
    h = lay(gathered)
    own_h = lax.dynamic_slice_in_dim(h, dp_index * block, block, 1)

    def reduce_product(lhs, w, fillers):
        terms, totals, made = collections.defaultdict(list), {}, None

        def run(group, deps):
            outs = project(lhs, w, me, group, deps)
            for pair, odd, even in zip(group, outs[::2], outs[1::2]):
                terms[pair][:0] = [(even, 0), (swap(odd, "mp", 1), 0)]
            return [outs[1]]

        def leave(s, bit, deps=()):
            totals[s] = add_round(terms[s], deps)
            terms[s ^ bit].append((swap(totals[s], "mp", bit), 0))

        first = pairs[0]
        before = run(pairs[1:2], run([first], []))
        leave(first, mp_bits[1])
        run(pairs[2:], [*before, totals[first]])
        done = 1
        for bit, filler in itertools.zip_longest(mp_bits[1:], fillers):
            for s in sorted(terms, reverse=True):
                if s & bit and not s & done and s not in totals:
                    leave(s, bit, [] if made is None else [made])
            done |= bit
            if filler:
                made = filler(None, list(totals.values()))
        return terms[0], made

    def fill(first, count):
        def run(into, deps):
            return relayout(embed_rows, n_mp, first * quarter, count * quarter, into, deps)

        return run

    parts, embed = reduce_product(h, weight, [None, fill(0, 2)])
    pre, x = activate(parts, own_h, gain, [embed])

    embed = fill(2, 2)(embed, [x])
    xs = gather_xor(x, "mp", mp_bits[::-1], [embed])
    pieces, before = [], []
    for i, order in enumerate(orders):
        late = [pieces[0][1]] if i == 3 else []
        sent, kept = project_vocab(xs, embed, me, order, i * quarter, quarter, before + late)
        pieces.append([kept, swap(sent, "dp", order[0])])
        before = [kept]
    pieces = sum_hops(pieces, "dp", orders)

    local = lax.dynamic_slice_in_dim(targets, dp_index * tok_dp, tok_dp, 0) - mp_index * vocab_mp
    local = column(local)
    *own_q, stats = softmax(pieces, local, quarter, width)
    total = stats
    for bit in mp_bits[:-1]:
        total = merge(merge_kernel, [total, swap(total, "mp", bit)], [])
    q, hops = zip(*[gather_rows(own_q[i], "dp", orders[i], [total]) for i in range(2)])
    finish = functools.partial(finish_kernel, tokens, width)
    packed = merge(finish, [total, swap(total, "mp", mp_bits[-1]), stats, local], hops)
    packs = jnp.concatenate(gather_direct(packed, "dp"), axis=0)
    dlogits, loss = scale_rows(q, packs, quarter)
    parts, _ = reduce_product(dlogits, embed, [None, None])
    dpre = grad_pre(parts, packs, pre, own_h, gain)
    grad = weight_grad(h.T, gather_xor(dpre, "mp", mp_bits[::-1]), me)
    return (grad.reshape(head_weight.shape), loss[0, 0])


def solution(mesh):
    return jax.shard_map(
        on_device,
        mesh=mesh,
        in_specs=(
            P("dp", "mp"),
            P("mp", None, "dp", None),
            P("mp", "dp", None),
            P("mp", None, "dp", None),
            P(),
        ),
        out_specs=(P("mp", None, "dp", None), P()),
        check_vma=False,
    )
```

```python
import collections
import functools
import itertools
import math

import jax
import jax.numpy as jnp
from jax import lax
from jax.experimental import pallas as pl
from jax.experimental.pallas import tpu as pltpu
from jax.sharding import PartitionSpec as P

F32 = jnp.float32
BF16 = jnp.bfloat16
LANES = 128
SHORT = pl.CostEstimate(flops=1, bytes_accessed=1, transcendentals=0)


def params(mib):
    return pltpu.CompilerParams(vmem_limit_bytes=mib * 2**20)


def bits_of(n):
    bits = [1 << i for i in range(n.bit_length() - 1)]
    assert 1 << len(bits) == n
    return bits


def swap(value, axis, bit):
    n = lax.axis_size(axis)
    return lax.ppermute(value, axis, [(i, i ^ bit) for i in range(n)])


def gather_xor(value, axis, bits, deps=()):
    held = {0: value}
    if deps:
        first, second = bits[:2]
        held[second] = swap(value, axis, second)
        held[first] = hold(swap(value, axis, first), [*deps, held[second]])
    for bit in bits:
        for s in list(held):
            if s % (2 * bit) == 0 and s | bit not in held:
                held[s | bit] = swap(held[s], axis, bit)
    return held


def join_kernel(a, b, *refs):
    out = refs[-1]
    out[: a.shape[0]] = a[...]
    out[a.shape[0] :] = b[...]


def join(a, b, deps):
    shape = (2 * a.shape[0], a.shape[1])
    return pl.pallas_call(
        join_kernel,
        out_shape=jax.ShapeDtypeStruct(shape, a.dtype),
        grid=(1,),
        in_specs=[whole(a.shape)] * 2 + after(deps),
        out_specs=whole(shape),
        compiler_params=params(48),
    )(a, b, *deps)


def gather_rows(value, axis, bits, deps):
    places, hops = [0], []
    for bit in bits[:-1]:
        value = join(value, swap(value, axis, bit), [] if hops else deps)
        hops.append(value)
        places = places + [s ^ bit for s in places]
    arrived = swap(value, axis, bits[-1])
    return [(value, places), (arrived, [s ^ bits[-1] for s in places])], hops[0]


def lay_kernel(places, *refs):
    out = refs[-1]
    width = refs[0].shape[1]
    for i, order in enumerate(places):
        rows = refs[i].shape[0] // len(order)
        first = i // 2 * width
        for j, s in enumerate(order):
            out[s * rows : (s + 1) * rows, first : first + width] = refs[i][j * rows : (j + 1) * rows]


def lay(gathered):
    values, places = zip(*[part for half in gathered for part in half])
    shape = (2 * values[0].shape[0], 2 * values[0].shape[1])
    return pl.pallas_call(
        functools.partial(lay_kernel, places),
        out_shape=jax.ShapeDtypeStruct(shape, values[0].dtype),
        grid=(1,),
        in_specs=[whole(v.shape) for v in values],
        out_specs=whole(shape),
        compiler_params=params(48),
    )(*values)


def gather_direct(value, axis):
    return [value] + [swap(value, axis, s) for s in range(1, lax.axis_size(axis))]


def whole(shape):
    return pl.BlockSpec(shape, lambda *_: (0,) * len(shape))


def stream(sources, buffer, sems, use):
    slots = buffer.shape[0]

    def copy(i):
        return pltpu.make_async_copy(sources[i], buffer.at[i % slots], sems.at[i % slots])

    for i in range(min(slots, len(sources))):
        copy(i).start()
    for i in range(len(sources)):
        copy(i).wait()
        use(i, i % slots)
        if i + slots < len(sources):
            copy(i + slots).start()


def after(deps):
    return [pl.BlockSpec(memory_space=pl.ANY)] * len(deps)


def each_tile(n, rows, run):
    group = max(1, 16 // n)

    def body(i, carry):
        run(i * group, group)
        return carry

    lax.fori_loop(0, rows // group, body, 0, unroll=8)


def relayout_kernel(n, start, rows, step, x, *refs):
    out, order, inputs, outputs, arrived, left = refs[-6:]
    size = order.shape[0]
    group = size // n

    to = lax.broadcasted_iota(jnp.int32, order.shape, 0)
    source = lax.broadcasted_iota(jnp.int32, order.shape, 1)
    order[...] = jnp.where(source == to % group * n + to // group, 1.0, 0.0).astype(BF16)
    slots = outputs.shape[0]

    def leave(i):
        target = out.at[:, pl.ds(start + i * step, step), :]
        return pltpu.make_async_copy(outputs.at[i % slots], target, left.at[i % slots])

    def use(i, slot):
        if i >= slots:
            leave(i - slots).wait()
        for part in range(step // group):
            taken = inputs[slot, part * size : (part + 1) * size, :]
            mixed = jnp.dot(order[...], taken, preferred_element_type=F32).astype(BF16)
            for k in range(n):
                at = slice(part * group, (part + 1) * group)
                outputs[i % slots, k, at, :] = mixed[k * group : (k + 1) * group]
        leave(i).start()

    steps = rows // step
    sources = [x.at[pl.ds((start + i * step) * n, step * n), :] for i in range(steps)]
    stream(sources, inputs, arrived, use)
    for i in range(max(0, steps - slots), steps):
        leave(i).wait()


def relayout(flat, n, start, rows, into, deps):
    total, block = flat.shape[0] // n, flat.shape[1]
    step = min(128, rows)
    slots = 4
    skipped = list(deps) if into is None else [into, *deps]
    return pl.pallas_call(
        functools.partial(relayout_kernel, n, start, rows, step),
        out_shape=jax.ShapeDtypeStruct((n, total, block), BF16),
        in_specs=after([flat, *skipped]),
        out_specs=pl.BlockSpec(memory_space=pl.ANY),
        scratch_shapes=[
            pltpu.VMEM((256, 256), BF16),
            pltpu.VMEM((slots, step * n, block), BF16),
            pltpu.VMEM((slots, n, step, block), BF16),
            pltpu.SemaphoreType.DMA((slots,)),
            pltpu.SemaphoreType.DMA((slots,)),
        ],
        input_output_aliases={} if into is None else {1: 0},
        compiler_params=params(48),
        cost_estimate=SHORT,
    )(flat, *skipped)


def hold_kernel(value, *refs):
    refs[-1][...] = value[...]


def hold(value, deps):
    return pl.pallas_call(
        hold_kernel,
        out_shape=jax.ShapeDtypeStruct(value.shape, value.dtype),
        grid=(1,),
        in_specs=[whole(value.shape)] + after(deps),
        out_specs=whole(value.shape),
        compiler_params=params(48),
    )(value, *deps)


def project_kernel(pairs, step, me, lhs, w, *refs):
    total, buffer, sems = refs[-3:]
    outs = refs[-3 - 2 * len(pairs) : -3]
    steps = w.shape[1] // step
    blocks = [me[0] ^ s for pair in pairs for s in (pair + 1, pair)]
    sources = [w.at[k, pl.ds(c * step, step), :] for k in blocks for c in range(steps)]

    def use(i, slot):
        c = i % steps
        part = jnp.dot(lhs[:, c * step : (c + 1) * step], buffer[slot], preferred_element_type=F32)
        if c > 0:
            part = part + total[...]
        if c < steps - 1:
            total[...] = part
        else:
            out = outs[i // steps]
            out[0] = part.astype(out.dtype)

    stream(sources, buffer, sems, use)


def project(lhs, w, me, pairs, deps):
    _, depth, block = w.shape
    rows = lhs.shape[0]
    step = min(1024, depth)
    slots = 4
    out = whole((1, rows, block))
    return pl.pallas_call(
        functools.partial(project_kernel, pairs, step),
        out_shape=[jax.ShapeDtypeStruct((1, rows, block), kind) for _ in pairs for kind in (BF16, F32)],
        grid_spec=pltpu.PrefetchScalarGridSpec(
            num_scalar_prefetch=1,
            grid=(1,),
            in_specs=[whole(lhs.shape)] + after([w, *deps]),
            out_specs=[out] * (2 * len(pairs)),
            scratch_shapes=[
                pltpu.VMEM((rows, block), F32),
                pltpu.VMEM((slots, step, block), BF16),
                pltpu.SemaphoreType.DMA((slots,)),
            ],
        ),
        compiler_params=params(48),
        cost_estimate=SHORT,
    )(me, lhs, w, *deps)


def pick(term, rows, block):
    array, place = term
    return pl.BlockSpec((1, rows, block), lambda *_: (place, 0, 0))


def add_kernel(n, *refs):
    out = refs[-1]
    total = refs[0][0].astype(F32)
    for ref in refs[1:n]:
        total = total + ref[0].astype(F32)
    out[0] = total.astype(out.dtype)


def add_round(terms, deps=()):
    _, rows, block = terms[0][0].shape
    return pl.pallas_call(
        functools.partial(add_kernel, len(terms)),
        out_shape=jax.ShapeDtypeStruct((1, rows, block), BF16),
        grid=(1,),
        in_specs=[pick(t, rows, block) for t in terms] + after(deps),
        out_specs=whole((1, rows, block)),
        compiler_params=params(48),
    )(*[t[0] for t in terms], *deps)


def square_rows(tokens, block):
    return max(1, tokens // block)


def act_kernel(n, *refs):
    parts, (h, gain, pre, x) = refs[:n], refs[-4:]
    total = parts[0][0].astype(F32)
    for part in parts[1:]:
        total = total + part[0].astype(F32)
    pre[...] = total
    act = h[...].astype(F32) + total / (1.0 + jnp.exp(-total))
    tokens, block = act.shape
    x[:tokens] = (act * gain[...]).astype(BF16)

    sums = jnp.broadcast_to(jnp.sum(act * act, axis=1, keepdims=True), (tokens, LANES))
    rest = jnp.transpose(sums)[0:1]
    count = square_rows(tokens, block)
    span = tokens // count
    row = lax.broadcasted_iota(jnp.int32, (16, span), 0)
    extra = jnp.zeros((16, span), F32)
    for term in range(3):
        high = rest.astype(BF16).astype(F32)
        rest = rest - high
        for i in range(count):
            extra = jnp.where(row == term * count + i, high[:, i * span : (i + 1) * span], extra)
    x[tokens:] = jnp.zeros((16, block), BF16)
    x[tokens:, :span] = extra.astype(BF16)


def activate(parts, h, gain, deps=()):
    rows, block = h.shape
    return pl.pallas_call(
        functools.partial(act_kernel, len(parts)),
        out_shape=[
            jax.ShapeDtypeStruct((rows, block), F32),
            jax.ShapeDtypeStruct((rows + 16, block), BF16),
        ],
        grid=(1,),
        in_specs=[pick(t, rows, block) for t in parts] + after(deps) + [whole(h.shape), whole(gain.shape)],
        out_specs=[whole((rows, block)), whole((rows + 16, block))],
        compiler_params=params(48),
    )(*[t[0] for t in parts], *deps, h, gain)


def hop_order(bits):
    places = [0]
    for bit in bits[::-1]:
        places = places + [s | bit for s in places]
    return places


def power(exponent):
    return jnp.exp(exponent * math.log(2.0))


def exponent_of(values):
    return jnp.ceil(jnp.log(jnp.maximum(values, 1e-30)) * (1.0 / math.log(2.0)))


def integers(values):
    values = jnp.clip(jnp.floor(values), -32768.0, 32767.0)
    return values.astype(jnp.int32).astype(jnp.int16)


def encode(values, squares):
    exponent = exponent_of(jnp.max(jnp.abs(values), axis=1, keepdims=True))
    own = exponent_of(squares)
    scaled = squares * power(15.0 - own)
    high = jnp.minimum(jnp.floor(scaled), 32767.0)
    extra = [exponent, own, high, (scaled - high) * 32768.0]
    return integers(values * power(15.0 - exponent) + 0.5), integers(
        lanes_of(extra, (values.shape[0], LANES))
    )


def decode(ref, rows, size):
    values = ref[rows, :size].astype(jnp.int32).astype(F32)
    extra = ref[rows, size:].astype(jnp.int32).astype(F32)
    squares = (extra[:, 2:3] + extra[:, 3:4] / 32768.0) * power(extra[:, 1:2] - 15.0)
    return values * power(extra[:, 0:1] - 15.0), squares


def piece_sum(refs, rows, size):
    values, squares = refs[0][rows, :size], refs[0][rows, size : size + 1]
    for ref in refs[1:]:
        more = decode(ref, rows, size)
        values, squares = values + more[0], squares + more[1]
    return values, squares


def logits_kernel(order, places, start, me, *refs):
    n = len(order)
    xs, e, (sent, kept, total, buffer, sems) = refs[:n], refs[n], refs[-5:]
    tokens, block = xs[0].shape[0] - 16, xs[0].shape[1]
    rows = tokens // len(places)
    size = kept.shape[1] - LANES

    extra = functools.reduce(jnp.add, [x[tokens:].astype(F32) for x in xs])
    count = square_rows(tokens, block)
    span = tokens // count
    columns = []
    for i in range(count):
        terms = [extra[t * count + i : t * count + i + 1, :span] for t in range(3)]
        columns.append(jnp.transpose(jnp.broadcast_to(functools.reduce(jnp.add, terms), (LANES, span))))
    squares = jnp.concatenate(columns, axis=0) if count > 1 else columns[0]

    def use(i, slot):
        part = lax.dot_general(
            xs[i][:tokens], buffer[slot], (((1,), (1,)), ((), ())), preferred_element_type=F32
        )
        if i > 0:
            part = part + total[...]
        if i < n - 1:
            total[...] = part
            return
        for j, s in enumerate(places):
            here = slice(s * rows, (s + 1) * rows)
            first = j % (len(places) // 2) * rows
            to = slice(first, first + rows)
            if j < len(places) // 2:
                kept[to, :size], kept[to, size:] = part[here], squares[here]
            else:
                sent[to, :size], sent[to, size:] = encode(part[here], squares[here, 0:1])

    stream([e.at[me[0] ^ s, pl.ds(start, size), :] for s in order], buffer, sems, use)


def project_vocab(xs, embed, me, bits, start, size, deps):
    n, _, block = embed.shape
    order = sorted(xs)
    rows = xs[0].shape[0] - 16
    slots = 4
    shape = (rows // 2, size + LANES)
    return pl.pallas_call(
        functools.partial(logits_kernel, order, hop_order(bits), start),
        out_shape=[jax.ShapeDtypeStruct(shape, kind) for kind in (jnp.int16, F32)],
        grid_spec=pltpu.PrefetchScalarGridSpec(
            num_scalar_prefetch=1,
            grid=(1,),
            in_specs=[whole((rows + 16, block))] * n + after([embed, *deps]),
            out_specs=[whole(shape)] * 2,
            scratch_shapes=[
                pltpu.VMEM((rows, size), F32),
                pltpu.VMEM((slots, size, block), BF16),
                pltpu.SemaphoreType.DMA((slots,)),
            ],
        ),
        compiler_params=params(48),
        cost_estimate=SHORT,
    )(me, *[xs[s] for s in order], embed, *deps)


def hop_kernel(kept, arrived, *refs):
    out, rest = refs[-2:]
    rows, size = out.shape[0], out.shape[1] - LANES
    out[:, :size], out[:, size:] = encode(*piece_sum([kept, arrived], slice(rows, 2 * rows), size))
    values, squares = piece_sum([kept, arrived], slice(0, rows), size)
    rest[:, :size], rest[:, size:] = values, jnp.broadcast_to(squares, (rows, LANES))


def hop_sum(kept, arrived, deps):
    rows, size = kept.shape[0] // 2, kept.shape[1]
    return pl.pallas_call(
        hop_kernel,
        out_shape=[jax.ShapeDtypeStruct((rows, size), kind) for kind in (jnp.int16, F32)],
        grid=(1,),
        in_specs=[whole(kept.shape)] * 2 + after(deps),
        out_specs=[whole((rows, size))] * 2,
        compiler_params=params(48),
    )(kept, arrived, *deps)


def sum_hops(terms, axis, orders):
    before = []
    for hop in range(1, len(orders[0])):
        for i, held in enumerate(terms):
            if i == len(terms) - 1:
                before = before + [terms[1][1]]
            sent, kept = hop_sum(*held, before)
            before = [sent]
            terms[i] = [kept, swap(sent, axis, orders[i][hop])]
    return terms


def softmax_kernel(counts, size, width, *refs):
    parts, (targets, *refs) = refs[: sum(counts)], refs[sum(counts) :]
    qs, stats = refs[:-1], refs[-1]
    target = targets[:, 0:1]
    pieces, hits, at = [], [], 0
    for i, count in enumerate(counts):
        total, squares = piece_sum(parts[at : at + count], slice(None), size)
        at += count
        if i == 0:
            inv = lax.rsqrt(squares / width + 1e-05)
        ids = lax.broadcasted_iota(jnp.int32, total.shape, 1) + i * size
        pieces.append(total * inv)
        hits.append(ids == target)
    top = functools.reduce(jnp.maximum, [jnp.max(p, axis=1, keepdims=True) for p in pieces])
    mass, moment, picked = 0.0, 0.0, 0.0
    for i, (piece, hit) in enumerate(zip(pieces, hits)):
        shifted = piece - top
        e = jnp.exp(shifted)
        mass = mass + jnp.sum(e, axis=1, keepdims=True)
        moment = moment + jnp.sum(e * shifted, axis=1, keepdims=True)
        picked = picked + jnp.sum(jnp.where(hit, piece, 0.0), axis=1, keepdims=True)
        first = i // len(qs) * size
        qs[i % len(qs)][:, first : first + size] = e.astype(BF16)
    stats[...] = lanes_of([top, mass, moment, picked, inv], stats.shape)


def softmax(pieces, targets, size, width):
    counts = [len(p) for p in pieces]
    flat = [part for p in pieces for part in p]
    rows = targets.shape[0]
    return pl.pallas_call(
        functools.partial(softmax_kernel, counts, size, width),
        out_shape=[jax.ShapeDtypeStruct((rows, len(pieces) // 2 * size), BF16)] * 2
        + [jax.ShapeDtypeStruct((rows, LANES), F32)],
        grid=(1,),
        in_specs=[whole((rows, part.shape[1])) for part in flat] + [whole(targets.shape)],
        out_specs=[whole((rows, len(pieces) // 2 * size))] * 2 + [whole((rows, LANES))],
        compiler_params=params(48),
    )(*flat, targets)


def tree(op, values):
    while len(values) > 1:
        half = len(values) // 2
        values = [op(a, b) for a, b in zip(values[:half], values[half:])]
    return values[0]


def lanes_of(values, shape):
    lane = lax.broadcasted_iota(jnp.int32, shape, 1)
    out = jnp.zeros(shape, F32)
    for i, value in enumerate(values):
        out = jnp.where(lane == i, value, out)
    return out


def merge_two(a, b):
    top = jnp.maximum(a[:, 0:1], b[:, 0:1])
    mass, moment = 0.0, 0.0
    for part in (a, b):
        shift = part[:, 0:1] - top
        weight = jnp.exp(shift)
        mass = mass + weight * part[:, 1:2]
        moment = moment + weight * (part[:, 2:3] + part[:, 1:2] * shift)
    return top, mass, moment, a[:, 3:4] + b[:, 3:4]


def merge_kernel(a, b, *refs):
    refs[-1][...] = lanes_of(merge_two(a[...], b[...]), refs[-1].shape)


def finish_kernel(tokens, width, a, b, own, targets, *refs):
    top, mass, moment, picked = merge_two(a[...], b[...])
    lse = top + jnp.log(mass)
    inv = own[:, 4:5]
    scale = jnp.exp(own[:, 0:1] - lse) / tokens
    at_target = (jnp.exp(picked - lse) - 1.0) / tokens
    pull = (moment / mass + (top - picked)) * (inv * inv) / (tokens * width)
    values = [scale, at_target, targets[:, 0:1].astype(F32), inv, pull, lse - picked]
    refs[-1][...] = lanes_of(values, refs[-1].shape)


def merge(body, values, deps):
    shape = values[0].shape
    return pl.pallas_call(
        body,
        out_shape=jax.ShapeDtypeStruct(shape, F32),
        grid=(1,),
        in_specs=[whole(shape)] * len(values) + after(deps),
        out_specs=whole(shape),
        compiler_params=params(48),
    )(*values, *deps)


def dlogits_kernel(places, quarter, *refs):
    qs, (packs, dlogits, loss) = refs[:-3], refs[-3:]
    n = 2 * len(places[0])
    rows = packs.shape[0] // n
    sums = [jnp.sum(packs[s * rows : (s + 1) * rows, 5:6], axis=0, keepdims=True) for s in range(n)]
    loss[...] = jnp.broadcast_to(tree(jnp.add, sums) / packs.shape[0], loss.shape)
    for i, (q, order) in enumerate(zip(qs, places)):
        for here, s in enumerate(order):
            at = slice(s * rows, (s + 1) * rows)
            scale, at_target, target = packs[at, 0:1], packs[at, 1:2], packs[at, 2:3].astype(jnp.int32)
            for j in range(q.shape[1] // quarter):
                first = (j * len(qs) // 2 + i // 2) * quarter
                values = q[here * rows : (here + 1) * rows, j * quarter : (j + 1) * quarter].astype(F32) * scale
                ids = lax.broadcasted_iota(jnp.int32, values.shape, 1) + first
                dlogits[at, first : first + quarter] = jnp.where(ids == target, at_target, values).astype(BF16)


def scale_rows(q, packs, quarter):
    values, places = zip(*[part for half in q for part in half])
    shape = (packs.shape[0], 2 * values[0].shape[1])
    return pl.pallas_call(
        functools.partial(dlogits_kernel, places, quarter),
        out_shape=[jax.ShapeDtypeStruct(shape, BF16), jax.ShapeDtypeStruct((8, LANES), F32)],
        compiler_params=params(48),
    )(*values, packs)


def dpre_kernel(n, *refs):
    parts, (packs, pre, h, gain, out) = refs[:n], refs[n:]
    dnormed = parts[0][0]
    for part in parts[1:]:
        dnormed = dnormed + part[0].astype(F32)
    inv, pull = packs[:, 3:4], packs[:, 4:5]
    v = pre[...]
    sigma = 1.0 / (1.0 + jnp.exp(-v))
    act = h[...].astype(F32) + v * sigma
    dact = inv * gain[...] * dnormed - act * pull
    out[...] = (dact * sigma * (1.0 + v * (1.0 - sigma))).astype(BF16)


def grad_pre(parts, packs, pre, h, gain):
    rows, block = pre.shape
    rest = [packs, pre, h, gain]
    return pl.pallas_call(
        functools.partial(dpre_kernel, len(parts)),
        out_shape=jax.ShapeDtypeStruct(pre.shape, BF16),
        grid=(1,),
        in_specs=[pick(t, rows, block) for t in parts] + [whole(r.shape) for r in rest],
        out_specs=whole(pre.shape),
        compiler_params=params(48),
    )(*[t[0] for t in parts], *rest)


def grad_kernel(order, step, me, h, *refs):
    n = len(order)
    ds, (out, placed, mixed, outputs, left) = refs[:n], refs[n:]
    slots = outputs.shape[0]
    lanes = range(0, out.shape[1], LANES)
    for s, d in zip(order, ds):
        placed[me[0] ^ s] = d[...]

    def leave(i):
        target = out.at[pl.ds(i * step * n, step * n), :]
        return pltpu.make_async_copy(outputs.at[i % slots], target, left.at[i % slots])

    steps = h.shape[0] // step
    for i in range(steps):
        if i >= slots:
            leave(i - slots).wait()
        for k in range(n):
            product = jnp.dot(h[i * step : (i + 1) * step, :], placed[k], preferred_element_type=F32)
            for j, lane in enumerate(lanes):
                mixed[j, pl.ds(k, step, stride=n + 1), :] = product[:, lane : lane + LANES]

        def collect(first, group):
            at = pl.multiple_of(first * n, 16)
            for j, lane in enumerate(lanes):
                parts = [
                    mixed[j, pl.ds((first + g) * (n + 1) + p, 8), :]
                    for g in range(group)
                    for p in range(0, n, 8)
                ]
                values = jnp.concatenate(parts, axis=0).astype(BF16)
                outputs[i % slots, pl.ds(at, group * n), lane : lane + LANES] = values

        each_tile(n, step, collect)
        leave(i).start()
    for i in range(max(0, steps - slots), steps):
        leave(i).wait()


def weight_grad(h, ds, me):
    width, rows = h.shape
    n = len(ds)
    block = ds[0].shape[1]
    order = sorted(ds)
    step = min(256, width)
    slots = 3
    return pl.pallas_call(
        functools.partial(grad_kernel, order, step),
        out_shape=jax.ShapeDtypeStruct((width * n, block), BF16),
        grid_spec=pltpu.PrefetchScalarGridSpec(
            num_scalar_prefetch=1,
            grid=(1,),
            in_specs=[whole(h.shape)] + [whole((rows, block))] * n,
            out_specs=pl.BlockSpec(memory_space=pl.ANY),
            scratch_shapes=[
                pltpu.VMEM((n, rows, block), BF16),
                pltpu.VMEM((block // LANES, step * (n + 1), LANES), F32),
                pltpu.VMEM((slots, step * n, block), BF16),
                pltpu.SemaphoreType.DMA((slots,)),
            ],
        ),
        compiler_params=params(48),
        cost_estimate=SHORT,
    )(me, h, *[ds[s] for s in order])


def column(values):
    return jnp.broadcast_to(values[:, None], (values.shape[0], LANES))


def on_device(hidden_rows, head_weight, norm_gain, vocab_embed, targets):
    n_dp, n_mp = lax.axis_size("dp"), lax.axis_size("mp")
    tok_dp, width_mp = hidden_rows.shape
    block = head_weight.shape[3]
    width = width_mp * n_mp
    tokens = tok_dp * n_dp
    vocab_mp = vocab_embed.shape[0]
    dp_bits, mp_bits = bits_of(n_dp), bits_of(n_mp)
    dp_index = lax.axis_index("dp")
    mp_index = lax.axis_index("mp")
    me = mp_index.astype(jnp.int32).reshape(1)
    pairs = list(range(n_mp - 2, -1, -2))

    embed_rows = vocab_embed.reshape(vocab_mp * n_mp, block)
    gain = norm_gain.reshape(1, block)
    quarter = vocab_mp // 4

    orders = [dp_bits, dp_bits[::-1]] * 2
    half = width_mp // 2
    weight_rows = head_weight.reshape(width_mp * n_mp, block)
    weight = relayout(weight_rows, n_mp, 0, half, None, [])
    gathered, hops = zip(
        *[gather_rows(hidden_rows[:, i * half : (i + 1) * half], "dp", orders[i], [weight]) for i in range(2)]
    )
    weight = relayout(weight_rows, n_mp, half, half, weight, hops)
    h = lay(gathered)
    own_h = lax.dynamic_slice_in_dim(h, dp_index * block, block, 1)

    def reduce_product(lhs, w, fillers):
        terms, totals, made = collections.defaultdict(list), {}, None

        def run(group, deps):
            outs = project(lhs, w, me, group, deps)
            for pair, odd, even in zip(group, outs[::2], outs[1::2]):
                terms[pair][:0] = [(even, 0), (swap(odd, "mp", 1), 0)]
            return [outs[1]]

        def leave(s, bit, deps=()):
            totals[s] = add_round(terms[s], deps)
            terms[s ^ bit].append((swap(totals[s], "mp", bit), 0))

        first = pairs[0]
        before = run(pairs[1:2], run([first], []))
        leave(first, mp_bits[1])
        run(pairs[2:], [*before, totals[first]])
        done = 1
        for bit, filler in itertools.zip_longest(mp_bits[1:], fillers):
            for s in sorted(terms, reverse=True):
                if s & bit and not s & done and s not in totals:
                    leave(s, bit, [] if made is None else [made])
            done |= bit
            if filler:
                made = filler(None, list(totals.values()))
        return terms[0], made

    def fill(first, count):
        def run(into, deps):
            return relayout(embed_rows, n_mp, first * quarter, count * quarter, into, deps)

        return run

    parts, embed = reduce_product(h, weight, [None, fill(0, 2)])
    pre, x = activate(parts, own_h, gain, [embed])

    embed = fill(2, 2)(embed, [x])
    xs = gather_xor(x, "mp", mp_bits[::-1], [embed])
    pieces, before = [], []
    for i, order in enumerate(orders):
        late = [pieces[0][1]] if i == 3 else []
        sent, kept = project_vocab(xs, embed, me, order, i * quarter, quarter, before + late)
        pieces.append([kept, swap(sent, "dp", order[0])])
        before = [kept]
    pieces = sum_hops(pieces, "dp", orders)

    local = lax.dynamic_slice_in_dim(targets, dp_index * tok_dp, tok_dp, 0) - mp_index * vocab_mp
    local = column(local)
    *own_q, stats = softmax(pieces, local, quarter, width)
    total = stats
    for bit in mp_bits[:-1]:
        total = merge(merge_kernel, [total, swap(total, "mp", bit)], [])
    q, hops = zip(*[gather_rows(own_q[i], "dp", orders[i], [total]) for i in range(2)])
    finish = functools.partial(finish_kernel, tokens, width)
    packed = merge(finish, [total, swap(total, "mp", mp_bits[-1]), stats, local], hops)
    packs = jnp.concatenate(gather_direct(packed, "dp"), axis=0)
    dlogits, loss = scale_rows(q, packs, quarter)
    parts, _ = reduce_product(dlogits, embed, [None, None])
    dpre = grad_pre(parts, packs, pre, own_h, gain)
    grad = weight_grad(h.T, gather_xor(dpre, "mp", mp_bits[::-1]), me)
    return (grad.reshape(head_weight.shape), loss[0, 0])


def solution(mesh):
    return jax.shard_map(
        on_device,
        mesh=mesh,
        in_specs=(
            P("dp", "mp"),
            P("mp", None, "dp", None),
            P("mp", "dp", None),
            P("mp", None, "dp", None),
            P(),
        ),
        out_specs=(P("mp", None, "dp", None), P()),
        check_vma=False,
    )
```
